32 devices in a mesh: dp: 4 (over y, x), ctx: 8 (over z, core).
Axes of the slice: x: 2, y: 2, z: 4, core: 2. Of those that a mesh axis runs over, the one named last changes fastest.
Arguments:
- tokens: bfloat16 [4, 1024, 4096], P('dp', 'ctx'), may hold values from -6 to 6
- grad_attn: bfloat16 [4, 1024, 1024], P('dp', 'ctx'), may hold values from -6 to 6
- w_packed: bfloat16 [10240, 128], P('ctx'), may hold values from -0.1875 to 0.1875
- block_rows: int32 [10, 8], replicated, may hold values from 0 to 31, as said below
- span_pairs: int32 [8, 2], replicated, may hold values from 0 to 15, as said below
Outputs:
- grad_tokens: bfloat16 [4, 1024, 4096], P('dp', 'ctx')
- grad_weights: float32 [10240, 128], P('ctx')
The draws below stay inside these ranges and needn't reach their ends.
Inputs may be any that keep to these rules, and one draw needn't show every extreme that they name: `block_rows`: row c lists the 8 row blocks in which column block c is nonzero, all different; rows 0 to 3 together list each of the 32 row blocks exactly once. Index k of ctx holds spans span_pairs[k, 0] and span_pairs[k, 1] = 15 - span_pairs[k, 0]; the first column takes each of 0 to 7 once.
All inputs are finite; a program needn't handle non-finite values.
Results may differ from the reference program's by a relative error of at most 0.0087.
Values may be sent and summed in bfloat16 or wider, within the bound.
No kernel may reach another device: no remote copies, remote signals or barrier semaphores. Data moves between devices by JAX's collectives and lax.ppermute only.
A program may use at most 64 MiB of HBM per device.

```python
import math
import jax
import jax.numpy as jnp
from jax import lax

D = 4096
HD = 128
BLK = 128
QPG = 8
GROUPS = 1
SPAN = 64
NRB = 32
NBR = 8
NCB = 10
NNZ = 80
TOK_DEV = 128
SEQ = 1024
SEQS = 4
N_CTX = 8


def draw_block_rows(key, part):
    first_cover = jax.random.permutation(jax.random.fold_in(key, 11), NRB)
    cover = NRB // NBR
    columns = []
    for column in range(NCB):
        if column < cover:
            columns.append(first_cover[column * NBR:(column + 1) * NBR])
        else:
            columns.append(jax.random.permutation(jax.random.fold_in(key, 100 + column), NRB)[:NBR])
    return jnp.stack(columns).astype(jnp.int32)


def draw_span_pairs(key, part):
    span_order = jax.random.permutation(jax.random.fold_in(key, 7), N_CTX).astype(jnp.int32)
    return jnp.stack([span_order, 2 * N_CTX - 1 - span_order], axis=1).astype(jnp.int32)


def level_of(key, extent, cuts, smallest, top_value):
    level = 1.0
    for axis_at, shards_of in cuts:
        draws = jax.random.uniform(jax.random.fold_in(jax.random.fold_in(key, 6), axis_at), (shards_of,), jnp.float32, smallest / len(cuts), top_value / len(cuts))
        level = level * jnp.repeat(jnp.exp(draws), extent[axis_at] // shards_of).reshape((-1,) + (1,) * (len(extent) - 1 - axis_at))
    return level


def normal_values(key, extent, scale, limit, split=(), kind=jnp.bfloat16):
    drawn = scale * jax.random.normal(key, extent, jnp.float32)
    if split:
        drawn = drawn * level_of(key, extent, split, -0.22, 0.18)
    return jnp.clip(drawn, -limit, limit).astype(kind)


def setup_inputs(seed: int = 0) -> dict:
    key_of = jax.random.split(jax.random.key(seed), 6)
    tokens = normal_values(key_of[0], (SEQS, SEQ, D), 1.0, 6.0, ((0, 4), (1, 8)))
    grad_attn = normal_values(key_of[1], (SEQS, SEQ, GROUPS * QPG * HD), 1.0, 6.0, ((0, 4), (1, 8)))
    w_packed = normal_values(key_of[2], (NNZ * BLK, BLK), (NBR * BLK) ** -0.5, 0.1875, ((0, 8),))
    block_rows = draw_block_rows(jax.random.fold_in(key_of[5], 71), 0)
    span_pairs = draw_span_pairs(jax.random.fold_in(key_of[5], 71), 0)
    return {"tokens": tokens, "grad_attn": grad_attn, "w_packed": w_packed, "block_rows": block_rows, "span_pairs": span_pairs}


EPSILON = 1e-06
HIGH = lax.Precision.HIGHEST

def norm_forward(values):
    factor = lax.rsqrt(lax.optimization_barrier(jnp.mean(values * values, axis=-1, keepdims=True)) + EPSILON)
    return (values * factor, factor)

def norm_backward(values, factor, upstream):
    return factor * upstream - values * (factor * factor * factor) * lax.optimization_barrier(jnp.mean(upstream * values, axis=-1, keepdims=True))

def reference(tokens, grad_attn, w_packed, block_rows, span_pairs):
    nquery = GROUPS * QPG
    score_scale = 1.0 / math.sqrt(HD)
    weights = w_packed.reshape(NCB, NBR, BLK, BLK).astype(jnp.float32)
    flat_ids = block_rows.reshape(-1)
    onehot = (flat_ids[:, None] == jnp.arange(NRB, dtype=jnp.int32)[None, :]).astype(jnp.float32)
    positions = (span_pairs[:, :, None] * SPAN + jnp.arange(SPAN, dtype=jnp.int32)[None, None, :]).reshape(-1).astype(jnp.int32)
    length = positions.shape[0]
    nblocks = length // TOK_DEV

    def one_sequence(running, inputs):
        token_rows, upstream_rows = inputs
        selected = jnp.take(token_rows.reshape(length, NRB, BLK), flat_ids, axis=1).reshape(length, NCB, NBR, BLK)
        projected = jnp.einsum('tcri,crio->tco', selected.astype(jnp.float32), weights, precision=HIGH).astype(jnp.bfloat16)
        query_raw = projected[:, :nquery].astype(jnp.float32).reshape(length, GROUPS, QPG, HD)
        key_raw = projected[:, nquery:nquery + GROUPS].astype(jnp.float32)
        values = projected[:, nquery + GROUPS:].astype(jnp.float32)
        query_norm, query_factor = norm_forward(query_raw)
        key_norm, key_factor = norm_forward(key_raw)
        query_hat = query_norm.astype(jnp.bfloat16).astype(jnp.float32)
        key_hat = key_norm.astype(jnp.bfloat16).astype(jnp.float32)
        upstream = upstream_rows.reshape(length, GROUPS, QPG, HD).astype(jnp.float32)

        def scores_of(first_row):
            query_block = lax.dynamic_slice_in_dim(query_hat, first_row, TOK_DEV, 0)
            query_pos = lax.dynamic_slice_in_dim(positions, first_row, TOK_DEV, 0)
            raw_scores = jnp.einsum('tgqd,ugd->tgqu', query_block, key_hat, precision=HIGH) * score_scale
            keep = positions[None, None, None, :] <= query_pos[:, None, None, None]
            return (query_block, jnp.where(keep, jnp.exp(raw_scores), 0.0))

        def forward_block(block_index):
            first_row = block_index * TOK_DEV
            query_block, exp_scores = scores_of(first_row)
            totals = lax.optimization_barrier(jnp.sum(exp_scores, axis=-1))
            expo_low = lax.optimization_barrier(exp_scores.astype(jnp.bfloat16)).astype(jnp.float32)
            attn = jnp.einsum('tgqu,ugd->tgqd', expo_low, values, precision=HIGH) / totals[..., None]
            grad_rows = lax.dynamic_slice_in_dim(upstream, first_row, TOK_DEV, 0)
            return (totals, lax.optimization_barrier(jnp.sum(grad_rows * attn, axis=-1)))
        totals_all, deltas_all = lax.map(forward_block, jnp.arange(nblocks, dtype=jnp.int32))

        def backward_block(sums, block_index):
            key_sum, value_sum = sums
            first_row = block_index * TOK_DEV
            query_block, exp_scores = scores_of(first_row)
            prob = exp_scores / totals_all[block_index][..., None]
            prob_low = lax.optimization_barrier(prob.astype(jnp.bfloat16)).astype(jnp.float32)
            grad_rows = lax.dynamic_slice_in_dim(upstream, first_row, TOK_DEV, 0)
            dprob = jnp.einsum('tgqd,ugd->tgqu', grad_rows, values, precision=HIGH)
            dscore = (prob * (dprob - deltas_all[block_index][..., None]) * score_scale).astype(jnp.bfloat16)
            dscore = lax.optimization_barrier(dscore).astype(jnp.float32)
            grad_query_block = jnp.einsum('tgqu,ugd->tgqd', dscore, key_hat, precision=HIGH)
            key_sum = key_sum + jnp.einsum('tgqu,tgqd->ugd', dscore, query_block, precision=HIGH)
            value_sum = value_sum + jnp.einsum('tgqu,tgqd->ugd', prob_low, grad_rows, precision=HIGH)
            return ((key_sum, value_sum), grad_query_block)
        empty_kv = jnp.zeros((length, GROUPS, HD), jnp.float32)
        (grad_key_hat, grad_value), grad_query_blocks = lax.scan(backward_block, (empty_kv, empty_kv), jnp.arange(nblocks, dtype=jnp.int32))
        grad_query_hat = grad_query_blocks.reshape(length, GROUPS, QPG, HD)
        grad_query = norm_backward(query_raw, query_factor, grad_query_hat).astype(jnp.bfloat16)
        grad_key = norm_backward(key_raw, key_factor, grad_key_hat).astype(jnp.bfloat16)
        grad_proj = jnp.concatenate([grad_query.reshape(length, nquery, HD), grad_key, grad_value.astype(jnp.bfloat16)], axis=1)
        grad_proj_wide = grad_proj.astype(jnp.float32)
        spread = jnp.einsum('tco,crio->tcri', grad_proj_wide, weights, precision=HIGH).reshape(length, NNZ, BLK)
        grad_rows_out = jnp.einsum('tki,kb->tbi', spread, onehot, precision=HIGH).reshape(length, D).astype(jnp.bfloat16)
        device_sel = selected.reshape(nblocks, TOK_DEV, NCB, NBR, BLK)
        device_grad = grad_proj.reshape(nblocks, TOK_DEV, NCB, HD)

        def add_partial(total, pieces):
            token_part, grad_part = pieces
            partial_w = jnp.einsum('tcri,tco->crio', token_part.astype(jnp.float32), grad_part.astype(jnp.float32), precision=HIGH).astype(jnp.bfloat16)
            partial_w = lax.optimization_barrier(partial_w)
            return (total + partial_w.astype(jnp.float32), None)
        running, unused = lax.scan(add_partial, running, (device_sel, device_grad))
        return (running, grad_rows_out)
    start_sum = jnp.zeros((NCB, NBR, BLK, BLK), jnp.float32)
    grad_w, grad_x = lax.scan(one_sequence, start_sum, (tokens, grad_attn))
    return (grad_x, grad_w.reshape(NNZ * BLK, BLK))
```

```python
import functools
import math

import jax
import jax.numpy as jnp
from jax import lax
from jax.experimental import pallas as pl
from jax.experimental.pallas import tpu as pltpu
from jax.sharding import PartitionSpec as P

HD = 128
BLK = 128
QPG = 8
GROUPS = 1
SPAN = 64
NBR = 8
NCB = 10
NNZ = 80
NQ = GROUPS * QPG
KEYS = 128
EPSILON = 1e-06
SCALE = 1.0 / math.sqrt(HD)
LOG2E = math.log2(math.e)

F32 = jnp.float32
BF16 = jnp.bfloat16
VMEM = pl.BlockSpec(memory_space=pltpu.VMEM)
SMEM = pl.BlockSpec(memory_space=pltpu.SMEM)


def call(kernel, scalars, arrays, outs, scratch=(), flops=0, moved=0, exps=0):
    return pl.pallas_call(
        kernel,
        in_specs=[SMEM] * len(scalars) + [VMEM] * len(arrays),
        out_specs=[VMEM] * len(outs),
        out_shape=[jax.ShapeDtypeStruct(s, t) for s, t in outs],
        scratch_shapes=list(scratch),
        compiler_params=pltpu.CompilerParams(vmem_limit_bytes=56 * 2**20),
        cost_estimate=pl.CostEstimate(flops=flops, bytes_accessed=moved, transcendentals=exps),
    )(*scalars, *arrays)


def dot(a, b, contract=((1,), (0,))):
    return lax.dot_general(a, b, (contract, ((), ())), preferred_element_type=F32)


def rows_at(start, size, step):
    return pl.ds(pl.multiple_of(start, step), size)


def inverse_rms(values):
    return lax.rsqrt(jnp.mean(values * values, axis=-1, keepdims=True) + EPSILON)


def norm_backward(values, factor, upstream):
    return factor * upstream - values * (factor * factor * factor) * jnp.mean(
        upstream * values, axis=-1, keepdims=True
    )


def transpose_kernel(x_ref, out_ref):
    for b in range(x_ref.shape[1] // BLK):
        out_ref[b * BLK : (b + 1) * BLK, :] = x_ref[:, b * BLK : (b + 1) * BLK].T


def project_kernel(layout, ids, offsets, x_ref, *refs):
    pieces, (w_ref, q_ref, kv_ref, key_ref) = refs[: len(layout)], refs[len(layout) :]
    at = 0
    for piece, (parts, rows) in zip(pieces, layout):
        for part in range(parts):
            w_ref[rows_at(offsets[at], rows, 16), :] = piece[part * rows : (part + 1) * rows, :]
            at += 1
    wide = NBR * BLK
    for c in range(NCB):
        picked = jnp.concatenate(
            [x_ref[:, rows_at(ids[c * NBR + r] * BLK, BLK, BLK)] for r in range(NBR)], axis=1
        )
        out = dot(picked, w_ref[c * wide : (c + 1) * wide, :]).astype(BF16)
        if c < NQ:
            for p in range(2):
                at_row = (p * NQ + c) * SPAN
                q_ref[at_row : at_row + SPAN, :] = out[p * SPAN : (p + 1) * SPAN, :]
        elif c == NQ:
            key = out.astype(F32)
            key_ref[...] = out
            kv_ref[:, :HD] = (key * inverse_rms(key)).astype(BF16)
        else:
            kv_ref[:, HD:] = out


def attend_kernel(nz, meta, spans, q_ref, up_ref, *refs):
    pieces = refs[: 2 * nz]
    dq_ref = refs[2 * nz]
    keep = refs[2 * nz + 1 : 3 * nz + 1]
    send = refs[3 * nz + 1 : 4 * nz + 1]
    kv, qhat, up, expo, dprob, acc, dq_t = refs[4 * nz + 1 :]
    half = NQ * SPAN
    me, zi, core = meta[0], meta[1], meta[2]
    for k in range(nz):
        z_from = lax.rem(zi + nz - k, nz)
        for other in range(2):
            source = z_from * 2 + (core if other == 0 else 1 - core)
            for p in range(2):
                kv[rows_at(spans[2 * source + p] * SPAN, SPAN, SPAN), :] = pieces[2 * k + other][
                    p * SPAN : (p + 1) * SPAN, :
                ]
    query = q_ref[...].astype(F32)
    qhat[...] = (query * inverse_rms(query)).astype(BF16)
    for p in range(2):
        for h in range(NQ):
            at = (p * NQ + h) * SPAN
            up[at : at + SPAN, :] = up_ref[p * SPAN : (p + 1) * SPAN, h * HD : (h + 1) * HD]
    acc[...] = jnp.zeros_like(acc)
    key_row = lax.broadcasted_iota(jnp.int32, (KEYS, half), 0)
    query_at = lax.broadcasted_iota(jnp.int32, (KEYS, half), 1) % SPAN
    for p in range(2):
        span = spans[2 * me + p]
        blocks = ((span + 1) * SPAN + KEYS - 1) // KEYS
        q_part = qhat[p * half : (p + 1) * half, :]
        up_part = up[p * half : (p + 1) * half, :]
        limit = query_at + span * SPAN

        def forward(b, sums):
            rows = rows_at(b * KEYS, KEYS, KEYS)
            raw = dot(kv[rows, :HD], q_part, ((1,), (1,)))
            e = jnp.where(key_row + b * KEYS <= limit, jnp.exp2(raw * (SCALE * LOG2E)), 0.0)
            dp = dot(kv[rows, HD:], up_part, ((1,), (1,)))
            expo[rows, :] = e
            dprob[rows, :] = dp
            weighted = e.astype(BF16).astype(F32) * dp
            return (
                sums[0] + jnp.sum(e.reshape(KEYS // 8, 8, half), axis=0),
                sums[1] + jnp.sum(weighted.reshape(KEYS // 8, 8, half), axis=0),
            )

        zero = jnp.zeros((8, half), F32)
        total, weighted = lax.fori_loop(0, blocks, forward, (zero, zero))
        inverse = 1.0 / jnp.sum(total, axis=0, keepdims=True)
        delta = jnp.sum(weighted, axis=0, keepdims=True) * inverse
        dq_t[...] = jnp.zeros_like(dq_t)

        def backward(b, carry):
            rows = rows_at(b * KEYS, KEYS, KEYS)
            prob = expo[rows, :] * inverse
            dscore = (prob * (dprob[rows, :] - delta) * SCALE).astype(BF16)
            acc[rows, :HD] += dot(dscore, q_part)
            acc[rows, HD:] += dot(prob.astype(BF16), up_part)
            dq_t[...] += dot(kv[rows, :HD].T, dscore)
            return carry

        lax.fori_loop(0, blocks, backward, 0)
        q_rows = q_ref[p * half : (p + 1) * half, :].astype(F32)
        dq = norm_backward(q_rows, inverse_rms(q_rows), dq_t[...].T).astype(BF16)
        for h in range(NQ):
            dq_ref[h, p * SPAN : (p + 1) * SPAN, :] = dq[h * SPAN : (h + 1) * SPAN, :]
    for k in range(nz):
        z_to = lax.rem(zi + k, nz)
        for p in range(2):
            part = slice(p * SPAN, (p + 1) * SPAN)
            for out, owner in ((keep[k], z_to * 2 + core), (send[k], z_to * 2 + 1 - core)):
                rows = rows_at(spans[2 * owner + p] * SPAN, SPAN, SPAN)
                out[part, :] = acc[rows, :].astype(BF16)


def kv_grad(key_ref, terms, dkv_ref):
    total = terms[0][...].astype(F32)
    for term in terms[1:]:
        total = total + term[...].astype(F32)
    key = key_ref[...].astype(F32)
    dkv_ref[0, :, :] = norm_backward(key, inverse_rms(key), total[:, :HD]).astype(BF16)
    dkv_ref[1, :, :] = total[:, HD:].astype(BF16)


def block_products(first, last, ids, xt_ref, grad_of, work):
    for c in range(first // NBR, (last - 1) // NBR + 1):
        lo, hi = max(first, c * NBR), min(last, (c + 1) * NBR)
        picked = jnp.concatenate(
            [xt_ref[rows_at(ids[b] * BLK, BLK, BLK), :] for b in range(lo, hi)], axis=0
        )
        work[(lo - first) * BLK : (hi - first) * BLK, :] = dot(picked, grad_of(c)).astype(BF16)


def emit_terms(meta, work, keep, send, z_count, shard, piece):
    core, dp = meta[2], meta[3]
    for k in range(len(keep)):
        for z in range(z_count):
            rows = slice(z * piece, (z + 1) * piece)
            at = lax.bitwise_xor(dp, k) * piece + z * 2 * shard
            keep[k][rows, :] = work[rows_at(at + core * shard, piece, 16), :]
            send[k][rows, :] = work[rows_at(at + (1 - core) * shard, piece, 16), :]


def query_terms_kernel(ndp, z_count, shard, piece, meta, ids, xt_ref, dq_ref, *refs):
    keep, send, work = refs[:ndp], refs[ndp : 2 * ndp], refs[2 * ndp]
    block_products(0, z_count * 2 * shard // BLK, ids, xt_ref, lambda c: dq_ref[c], work)
    emit_terms(meta, work, keep, send, z_count, shard, piece)


def last_terms_kernel(ndp, nz, z_first, shard, piece, meta, ids, xt_ref, dq_ref, key_ref, *refs):
    terms, dkv_ref = refs[:nz], refs[nz]
    keep, send = refs[nz + 1 : nz + 1 + ndp], refs[nz + 1 + ndp : nz + 1 + 2 * ndp]
    work = refs[nz + 1 + 2 * ndp]
    kv_grad(key_ref, terms, dkv_ref)
    block_products(
        z_first * 2 * shard // BLK,
        NNZ,
        ids,
        xt_ref,
        lambda c: dq_ref[c] if c < NQ else dkv_ref[c - NQ],
        work,
    )
    emit_terms(meta, work, keep, send, nz - z_first, shard, piece)


def all_terms_kernel(nz, ids, xt_ref, dq_ref, key_ref, *refs):
    terms, (dkv_ref, out_ref) = refs[:nz], refs[nz:]
    kv_grad(key_ref, terms, dkv_ref)
    block_products(
        0, NNZ, ids, xt_ref, lambda c: dq_ref[c] if c < NQ else dkv_ref[c - NQ], out_ref
    )


def sum_kernel(ndp, nz, z_first, piece, meta, *refs):
    head, tail = refs[:ndp], refs[ndp : 2 * ndp]
    outs, work = refs[2 * ndp : 2 * ndp + nz], refs[2 * ndp + nz]
    for group, first, count in ((head, 0, z_first), (tail, z_first, nz - z_first)):
        total = group[0][...].astype(F32)
        for term in group[1:]:
            total = total + term[...].astype(F32)
        work[first * piece : (first + count) * piece, :] = total.astype(BF16)
    for k in range(nz):
        outs[k][...] = work[rows_at(lax.rem(meta[1] + k, nz) * piece, piece, 16), :]


def place_kernel(piece, meta, *refs):
    for k, ref in enumerate(refs[:-1]):
        at = lax.bitwise_xor(meta[3], k) * piece
        refs[-1][rows_at(at, piece, 16), :] = ref[...].astype(F32)


def token_grad_kernel(ids, dq_ref, dkv_ref, w_ref, out_ref, work):
    wide = NBR * BLK
    cover = out_ref.shape[1] // wide
    for c in range(NCB):
        grad = dq_ref[c] if c < NQ else dkv_ref[c - NQ]
        spread = dot(grad, w_ref[c * wide : (c + 1) * wide, :], ((1,), (1,)))
        for r in range(NBR):
            columns = rows_at(ids[c * NBR + r] * BLK, BLK, BLK)
            term = spread[:, r * BLK : (r + 1) * BLK]
            if c < cover:
                work[:, columns] = term
            else:
                work[:, columns] += term
    out_ref[...] = work[...].astype(BF16)


def per_device(ndp, tokens, grad_attn, w_packed, block_rows, span_pairs):
    nctx = lax.axis_size("ctx")
    nz = nctx // 2
    me = lax.axis_index("ctx")
    dp = lax.axis_index("dp")
    zi, core = me // 2, me % 2
    meta = jnp.stack([me, zi, core, dp]).astype(jnp.int32)
    ids, spans = block_rows.reshape(-1), span_pairs.reshape(-1)
    x, up = tokens[0], grad_attn[0]
    tok, width = x.shape
    length = span_pairs.shape[0] * 2 * SPAN
    shard = w_packed.shape[0]
    piece = shard // ndp
    z_first = NQ * NBR * BLK // (2 * shard)
    fast = shard % BLK == 0 and shard % (16 * ndp) == 0 and ndp & (ndp - 1) == 0

    def swap_core(v):
        return lax.ppermute(v, "ctx", [(i, i ^ 1) for i in range(nctx)])

    def shift_z(v, k):
        return lax.ppermute(
            v, "ctx", [(i, ((i // 2 + k) % nz) * 2 + i % 2) for i in range(nctx)]
        )

    def swap_dp(v, k):
        return lax.ppermute(v, "dp", [(i, i ^ k) for i in range(ndp)])

    (xt,) = call(transpose_kernel, (), (x,), [((width, tok), BF16)], moved=4 * x.size)

    if fast:
        mine = lax.dynamic_slice_in_dim(w_packed, dp * piece, piece, 0)
        from_z = [shift_z(mine, k) for k in range(1, nz)]
        gathered = [jnp.concatenate(from_z, axis=0)]
        gathered += [swap_dp(gathered[0], k) for k in range(1, ndp)]
        pieces, layout, offsets = [], [], []
        for other in range(2):
            parity = core if other == 0 else 1 - core
            pieces.append(w_packed if other == 0 else swap_core(w_packed))
            layout.append((1, shard))
            offsets.append(me * shard if other == 0 else (zi * 2 + parity) * shard)
            for k, part in enumerate(gathered):
                pieces.append(part if other == 0 else swap_core(part))
                layout.append((nz - 1, piece))
                for j in range(1, nz):
                    source = ((zi + nz - j) % nz) * 2 + parity
                    offsets.append(source * shard + (dp ^ k) * piece)
        offsets = jnp.stack(offsets).astype(jnp.int32)
    else:
        pieces = [lax.all_gather(w_packed, "ctx", axis=0, tiled=True)]
        layout = [(1, NNZ * BLK)]
        offsets = jnp.zeros((1,), jnp.int32)
    weights, query, kv, key = call(
        functools.partial(project_kernel, tuple(layout)),
        (ids, offsets),
        (x, *pieces),
        [
            ((NNZ * BLK, BLK), BF16),
            ((tok * NQ, HD), BF16),
            ((tok, 2 * HD), BF16),
            ((tok, HD), BF16),
        ],
        flops=2 * tok * NNZ * BLK * BLK,
        moved=8 * 2**20,
    )

    kv_pieces = []
    for k in range(nz):
        part = kv if k == 0 else shift_z(kv, k)
        kv_pieces += [part, swap_core(part)]
    half = NQ * SPAN
    outs = call(
        functools.partial(attend_kernel, nz),
        (meta, spans),
        (query, up, *kv_pieces),
        [((NQ, tok, HD), BF16)] + [((tok, 2 * HD), BF16)] * (2 * nz),
        scratch=[
            pltpu.VMEM((length, 2 * HD), BF16),
            pltpu.VMEM((tok * NQ, HD), BF16),
            pltpu.VMEM((tok * NQ, HD), BF16),
            pltpu.VMEM((length, half), F32),
            pltpu.VMEM((length, half), F32),
            pltpu.VMEM((length, 2 * HD), F32),
            pltpu.VMEM((HD, half), F32),
        ],
        flops=10 * tok * NQ * length * HD // 2,
        moved=4 * 2**20,
        exps=tok * NQ * length // 2,
    )
    dq, keep, send = outs[0], outs[1 : nz + 1], outs[nz + 1 :]

    def add(a, b):
        return (a.astype(F32) + b.astype(F32)).astype(BF16)

    sums = [add(keep[k], swap_core(send[k])) for k in range(nz)]
    terms = [sums[0]] + [shift_z(sums[k], k) for k in range(1, nz)]

    if fast:
        head = call(
            functools.partial(query_terms_kernel, ndp, z_first, shard, piece),
            (meta, ids),
            (xt, dq),
            [((z_first * piece, BLK), BF16)] * (2 * ndp),
            scratch=[pltpu.VMEM((z_first * 2 * shard, BLK), BF16)],
            flops=2 * tok * z_first * 2 * shard * BLK,
            moved=4 * 2**20,
        )
        head = [add(head[k], swap_core(head[ndp + k])) for k in range(ndp)]
        head = [head[0]] + [swap_dp(head[k], k) for k in range(1, ndp)]
        tail = call(
            functools.partial(last_terms_kernel, ndp, nz, z_first, shard, piece),
            (meta, ids),
            (xt, dq, key, *terms),
            [((2, tok, HD), BF16)] + [(((nz - z_first) * piece, BLK), BF16)] * (2 * ndp),
            scratch=[pltpu.VMEM(((nz - z_first) * 2 * shard, BLK), BF16)],
            flops=2 * tok * (nz - z_first) * 2 * shard * BLK,
            moved=3 * 2**20,
        )
        dkv, tail = tail[0], tail[1:]
        tail = [add(tail[k], swap_core(tail[ndp + k])) for k in range(ndp)]
        tail = [tail[0]] + [swap_dp(tail[k], k) for k in range(1, ndp)]
        by_z = call(
            functools.partial(sum_kernel, ndp, nz, z_first, piece),
            (meta,),
            (*head, *tail),
            [((piece, BLK), BF16)] * nz,
            scratch=[pltpu.VMEM((nz * piece, BLK), BF16)],
            moved=2 * 2**20,
        )
        owned = by_z[0].astype(F32)
        for k in range(1, nz):
            owned = owned + shift_z(by_z[k], k).astype(F32)
        owned = owned.astype(BF16)
        (grad_weights,) = call(
            functools.partial(place_kernel, piece),
            (meta,),
            [owned] + [swap_dp(owned, k) for k in range(1, ndp)],
            [((shard, BLK), F32)],
            moved=2**20,
        )
    else:
        dkv, partial_w = call(
            functools.partial(all_terms_kernel, nz),
            (ids,),
            (xt, dq, key, *terms),
            [((2, tok, HD), BF16), ((NNZ * BLK, BLK), BF16)],
            flops=2 * tok * NNZ * BLK * BLK,
            moved=4 * 2**20,
        )
        received = lax.all_to_all(
            partial_w.reshape(nctx, shard, BLK), "ctx", split_axis=0, concat_axis=0, tiled=True
        )
        grad_weights = lax.psum(jnp.sum(received.astype(F32), axis=0), "dp")

    (grad_tokens,) = call(
        token_grad_kernel,
        (ids,),
        (dq, dkv, weights),
        [((tok, width), BF16)],
        scratch=[pltpu.VMEM((tok, width), F32)],
        flops=2 * tok * NNZ * BLK * BLK,
        moved=4 * 2**20,
    )
    return (grad_tokens[None], grad_weights)


def solution(mesh):
    in_specs = (P("dp", "ctx", None), P("dp", "ctx", None), P("ctx", None), P(), P())
    out_specs = (P("dp", "ctx", None), P("ctx", None))
    return jax.shard_map(
        functools.partial(per_device, mesh.shape["dp"]),
        mesh=mesh,
        in_specs=in_specs,
        out_specs=out_specs,
        check_vma=False,
    )
```

```python
import functools
import math

import jax
import jax.numpy as jnp
from jax import lax
from jax.experimental import pallas as pl
from jax.experimental.pallas import tpu as pltpu
from jax.sharding import PartitionSpec as P

HD = 128
BLK = 128
QPG = 8
GROUPS = 1
SPAN = 64
NBR = 8
NCB = 10
NNZ = 80
NQ = GROUPS * QPG
KEYS = 128
EPSILON = 1e-06
SCALE = 1.0 / math.sqrt(HD)
LOG2E = math.log2(math.e)

F32 = jnp.float32
BF16 = jnp.bfloat16
VMEM = pl.BlockSpec(memory_space=pltpu.VMEM)
SMEM = pl.BlockSpec(memory_space=pltpu.SMEM)
ANY = pl.BlockSpec(memory_space=pl.ANY)


def nbytes(shape, dtype):
    return math.prod(shape) * jnp.dtype(dtype).itemsize


def call(kernel, scalars, arrays, outs, scratch=(), wait=(), flops=0, moved=0, exps=0):
    def body(*refs):
        at = len(scalars) + len(arrays)
        kernel(*refs[:at], *refs[at + len(wait) :])

    held = [(v.shape, v.dtype) for v in arrays] + [(s, t) for s, t in outs]
    held += [(v.shape, v.dtype) for v in scratch]
    need = sum(nbytes(s, t) for s, t in held)
    return pl.pallas_call(
        body,
        in_specs=[SMEM] * len(scalars) + [VMEM] * len(arrays) + [ANY] * len(wait),
        out_specs=[SMEM if t == jnp.int32 else VMEM for _, t in outs],
        out_shape=[jax.ShapeDtypeStruct(s, t) for s, t in outs],
        scratch_shapes=list(scratch),
        compiler_params=pltpu.CompilerParams(vmem_limit_bytes=need + need // 4 + 4 * 2**20),
        cost_estimate=pl.CostEstimate(flops=flops, bytes_accessed=moved, transcendentals=exps),
    )(*scalars, *arrays, *wait)


def dot(a, b, contract=((1,), (0,))):
    return lax.dot_general(a, b, (contract, ((), ())), preferred_element_type=F32)


def rows_at(start, size, step):
    return pl.ds(pl.multiple_of(start, step), size)


def inverse_rms(values):
    return lax.rsqrt(jnp.mean(values * values, axis=-1, keepdims=True) + EPSILON)


def norm_backward(values, factor, upstream):
    return factor * upstream - values * (factor * factor * factor) * jnp.mean(
        upstream * values, axis=-1, keepdims=True
    )


def prepare_kernel(ids, spans, x_ref, xt_ref, ids_out, spans_out):
    for b in range(x_ref.shape[1] // BLK):
        xt_ref[b * BLK : (b + 1) * BLK, :] = x_ref[:, b * BLK : (b + 1) * BLK].T
    for source, out in ((ids, ids_out), (spans, spans_out)):

        @pl.loop(0, source.shape[0])
        def _(i):
            for j in range(source.shape[1]):
                out[i, j] = source[i, j]


def arrange_kernel(z_lo, z_hi, *refs):
    pieces, out = refs[:-1], refs[-1]
    nz, rows = len(pieces), pieces[0].shape[0]
    me = lax.axis_index("ctx") // 2
    for z in range(z_lo, z_hi):
        at = (z - z_lo) * rows
        for k in range(nz):

            @pl.when(lax.rem(me + nz - k, nz) == z)
            def _():
                out[at : at + rows, :] = pieces[k][...]


def join_pieces(pieces, z_count, shard, piece, w_ref):
    core, dp = lax.axis_index("ctx") % 2, lax.axis_index("dp")
    for n, ref in enumerate(pieces):
        k, parity = n // 2, core if n % 2 == 0 else 1 - core
        for z in range(z_count):
            at = z * 2 * shard + parity * shard + lax.bitwise_xor(dp, k) * piece
            w_ref[rows_at(at, piece, 16), :] = ref[z * piece : (z + 1) * piece, :]


def column_of(c, ids, x_ref):
    return jnp.concatenate(
        [x_ref[:, rows_at(ids[c, r] * BLK, BLK, BLK)] for r in range(NBR)], axis=1
    )


def project_keys(ids, x_ref, w_ref, first, kv_ref, key_ref):
    wide = NBR * BLK
    for c in range(NQ, NCB):
        at = c * wide - first
        out = dot(column_of(c, ids, x_ref), w_ref[at : at + wide, :]).astype(BF16)
        if c == NQ:
            key = out.astype(F32)
            key_ref[...] = out
            kv_ref[:, :HD] = (key * inverse_rms(key)).astype(BF16)
        else:
            kv_ref[:, HD:] = out


def project_queries(ids, x_ref, rows_of, q_ref):
    wide = NBR * BLK
    for c in range(NQ):
        out = dot(column_of(c, ids, x_ref), rows_of(c * wide, (c + 1) * wide)).astype(BF16)
        for p in range(2):
            at = (p * NQ + c) * SPAN
            q_ref[at : at + SPAN, :] = out[p * SPAN : (p + 1) * SPAN, :]


def keys_kernel(z_count, shard, piece, ids, x_ref, *refs):
    pieces, (w_ref, kv_ref, key_ref) = refs[:-3], refs[-3:]
    join_pieces(pieces, z_count, shard, piece, w_ref)
    project_keys(ids, x_ref, w_ref, NNZ * BLK - z_count * 2 * shard, kv_ref, key_ref)


def queries_kernel(z_count, shard, piece, ids, x_ref, tail_ref, *refs):
    pieces, (w_ref, q_ref) = refs[:-2], refs[-2:]
    join_pieces(pieces, z_count, shard, piece, w_ref)
    cut = z_count * 2 * shard

    def rows_of(lo, hi):
        if hi <= cut:
            return w_ref[lo:hi, :]
        if lo >= cut:
            return tail_ref[lo - cut : hi - cut, :]
        return jnp.concatenate([w_ref[lo:cut, :], tail_ref[0 : hi - cut, :]], axis=0)

    project_queries(ids, x_ref, rows_of, q_ref)


def project_kernel(ids, x_ref, w_ref, q_ref, kv_ref, key_ref):
    project_keys(ids, x_ref, w_ref, 0, kv_ref, key_ref)
    project_queries(ids, x_ref, lambda lo, hi: w_ref[lo:hi, :], q_ref)


def attend_kernel(nz, spans, q_ref, up_ref, *refs):
    pieces = refs[: 2 * nz]
    dq_ref = refs[2 * nz]
    keep = refs[2 * nz + 1 : 3 * nz + 1]
    send = refs[3 * nz + 1 : 4 * nz + 1]
    kv, qhat, up, expo, dprob, acc, dq_t = refs[4 * nz + 1 :]
    half = NQ * SPAN
    me = lax.axis_index("ctx")
    zi, core = me // 2, me % 2
    for k in range(nz):
        z_from = lax.rem(zi + nz - k, nz)
        for other in range(2):
            source = z_from * 2 + (core if other == 0 else 1 - core)
            for p in range(2):
                kv[rows_at(spans[source, p] * SPAN, SPAN, SPAN), :] = pieces[2 * k + other][
                    p * SPAN : (p + 1) * SPAN, :
                ]
    query = q_ref[...].astype(F32)
    qhat[...] = (query * inverse_rms(query)).astype(BF16)
    for p in range(2):
        for h in range(NQ):
            at = (p * NQ + h) * SPAN
            up[at : at + SPAN, :] = up_ref[p * SPAN : (p + 1) * SPAN, h * HD : (h + 1) * HD]
    acc[...] = jnp.zeros_like(acc)
    key_row = lax.broadcasted_iota(jnp.int32, (KEYS, half), 0)
    query_at = lax.broadcasted_iota(jnp.int32, (KEYS, half), 1) % SPAN
    for p in range(2):
        span = spans[me, p]
        blocks = ((span + 1) * SPAN + KEYS - 1) // KEYS
        q_part = qhat[p * half : (p + 1) * half, :]
        up_part = up[p * half : (p + 1) * half, :]
        limit = query_at + span * SPAN

        def forward(b, sums):
            rows = rows_at(b * KEYS, KEYS, KEYS)
            raw = dot(kv[rows, :HD], q_part, ((1,), (1,)))
            e = jnp.where(key_row + b * KEYS <= limit, jnp.exp2(raw * (SCALE * LOG2E)), 0.0)
            dp = dot(kv[rows, HD:], up_part, ((1,), (1,)))
            expo[rows, :] = e
            dprob[rows, :] = dp
            weighted = e.astype(BF16).astype(F32) * dp
            return (
                sums[0] + jnp.sum(e.reshape(KEYS // 8, 8, half), axis=0),
                sums[1] + jnp.sum(weighted.reshape(KEYS // 8, 8, half), axis=0),
            )

        zero = jnp.zeros((8, half), F32)
        total, weighted = lax.fori_loop(0, blocks, forward, (zero, zero))
        inverse = 1.0 / jnp.sum(total, axis=0, keepdims=True)
        delta = jnp.sum(weighted, axis=0, keepdims=True) * inverse
        dq_t[...] = jnp.zeros_like(dq_t)

        def backward(b, carry):
            rows = rows_at(b * KEYS, KEYS, KEYS)
            prob = expo[rows, :] * inverse
            dscore = (prob * (dprob[rows, :] - delta) * SCALE).astype(BF16)
            acc[rows, :HD] += dot(dscore, q_part)
            acc[rows, HD:] += dot(prob.astype(BF16), up_part)
            dq_t[...] += dot(kv[rows, :HD].T, dscore)
            return carry

        lax.fori_loop(0, blocks, backward, 0)
        q_rows = q_ref[p * half : (p + 1) * half, :].astype(F32)
        dq = norm_backward(q_rows, inverse_rms(q_rows), dq_t[...].T).astype(BF16)
        for h in range(NQ):
            dq_ref[h, p * SPAN : (p + 1) * SPAN, :] = dq[h * SPAN : (h + 1) * SPAN, :]
    for k in range(nz):
        z_to = lax.rem(zi + k, nz)
        for p in range(2):
            part = slice(p * SPAN, (p + 1) * SPAN)
            for out, owner in ((keep[k], z_to * 2 + core), (send[k], z_to * 2 + 1 - core)):
                rows = rows_at(spans[owner, p] * SPAN, SPAN, SPAN)
                out[part, :] = acc[rows, :].astype(BF16)


def kv_grad_kernel(nz, key_ref, *refs):
    terms, dkv_ref = refs[:nz], refs[nz]
    total = terms[0][...].astype(F32)
    for term in terms[1:]:
        total = total + term[...].astype(F32)
    key = key_ref[...].astype(F32)
    dkv_ref[0, :, :] = norm_backward(key, inverse_rms(key), total[:, :HD]).astype(BF16)
    dkv_ref[1, :, :] = total[:, HD:].astype(BF16)


def terms_kernel(z_first, z_count, shard, piece, ids, xt, xt_other, *refs):
    tok = xt.shape[1]
    grads, work = refs[-2:]
    columns = grads.shape[0]
    first = z_first * 2 * shard // (NBR * BLK)
    ndp = shard // piece
    sources, outs = refs[: -2 - ndp], refs[-2 - ndp : -2]
    for n, ref in enumerate(sources):
        other = n % 2
        for i in range(ref.shape[0]):
            c = i - first if n < 2 else NQ + i - first
            if 0 <= c < columns:
                grads[c, other * tok : (other + 1) * tok, :] = ref[i]
    core, dp = lax.axis_index("ctx") % 2, lax.axis_index("dp")
    count = shard // BLK
    for z in range(z_count):
        for i in range(count):
            b = (2 * (z_first + z) + core) * count + i
            c = b // NBR
            rows = rows_at(ids[c, b % NBR] * BLK, BLK, BLK)
            picked = jnp.concatenate([xt[rows, :], xt_other[rows, :]], axis=1)
            at = (z * count + i) * BLK
            work[at : at + BLK, :] = dot(picked, grads[c - first]).astype(BF16)
    for k in range(ndp):
        for z in range(z_count):
            at = z * shard + lax.bitwise_xor(dp, k) * piece
            outs[k][z * piece : (z + 1) * piece, :] = work[rows_at(at, piece, 16), :]


def all_terms_kernel(ids, xt, dq_ref, dkv_ref, out_ref):
    for c in range(NCB):
        picked = jnp.concatenate(
            [xt[rows_at(ids[c, r] * BLK, BLK, BLK), :] for r in range(NBR)], axis=0
        )
        grad = dq_ref[c] if c < NQ else dkv_ref[c - NQ]
        out_ref[c * NBR * BLK : (c + 1) * NBR * BLK, :] = dot(picked, grad).astype(BF16)


def sum_kernel(ndp, nz, z_first, piece, *refs):
    head, tail = refs[:ndp], refs[ndp : 2 * ndp]
    outs, work = refs[2 * ndp : 2 * ndp + nz], refs[2 * ndp + nz]
    for group, first, count in ((head, 0, z_first), (tail, z_first, nz - z_first)):
        total = group[0][...].astype(F32)
        for term in group[1:]:
            total = total + term[...].astype(F32)
        work[first * piece : (first + count) * piece, :] = total.astype(BF16)
    for k in range(nz):
        at = lax.rem(lax.axis_index("ctx") // 2 + k, nz) * piece
        outs[k][...] = work[rows_at(at, piece, 16), :]


def place_kernel(piece, *refs):
    for k, ref in enumerate(refs[:-1]):
        at = lax.bitwise_xor(lax.axis_index("dp"), k) * piece
        refs[-1][rows_at(at, piece, 16), :] = ref[...].astype(F32)


def token_grad_kernel(ids, dq_ref, dkv_ref, *refs):
    parts, (out_ref, work) = refs[:-2], refs[-2:]
    wide = NBR * BLK
    cover = out_ref.shape[1] // wide
    first = 0
    done = 0
    for w_ref in parts:
        last = first + w_ref.shape[0] // BLK
        while done < last:
            c = done // NBR
            stop = min(last, (c + 1) * NBR)
            grad = dq_ref[c] if c < NQ else dkv_ref[c - NQ]
            spread = dot(grad, w_ref[(done - first) * BLK : (stop - first) * BLK, :], ((1,), (1,)))
            for b in range(done, stop):
                columns = rows_at(ids[c, b % NBR] * BLK, BLK, BLK)
                term = spread[:, (b - done) * BLK : (b - done + 1) * BLK]
                if c < cover:
                    work[:, columns] = term
                else:
                    work[:, columns] += term
            done = stop
        first = last
    out_ref[...] = work[...].astype(BF16)


def per_device(ndp, tokens, grad_attn, w_packed, ids, spans):
    nctx = lax.axis_size("ctx")
    nz = nctx // 2
    dp = lax.axis_index("dp")
    x, up = tokens[0], grad_attn[0]
    tok, width = x.shape
    length = spans.shape[0] * 2 * SPAN
    shard = w_packed.shape[0]
    piece = shard // ndp
    z_first = NQ * NBR * BLK // (2 * shard)
    z_last = nz - z_first
    cut = z_first * 2 * shard
    half = NQ * SPAN
    fast = shard % BLK == 0 and shard % (16 * ndp) == 0 and ndp & (ndp - 1) == 0

    def swap_core(v):
        return lax.ppermute(v, "ctx", [(i, i ^ 1) for i in range(nctx)])

    def shift_z(v, k):
        return lax.ppermute(
            v, "ctx", [(i, ((i // 2 + k) % nz) * 2 + i % 2) for i in range(nctx)]
        )

    def swap_dp(v, k):
        return lax.ppermute(v, "dp", [(i, i ^ k) for i in range(ndp)])

    def add(a, b):
        return (a.astype(F32) + b.astype(F32)).astype(BF16)

    xt, ids, spans = call(
        prepare_kernel,
        (ids, spans),
        (x,),
        [((width, tok), BF16), (ids.shape, jnp.int32), (spans.shape, jnp.int32)],
        moved=4 * x.size,
    )

    if fast:
        mine = lax.dynamic_slice_in_dim(w_packed, dp * piece, piece, 0)
        from_z = [mine] + [shift_z(mine, k) for k in range(1, nz)]

        def arrange(z_lo, z_hi, wait):
            return call(
                functools.partial(arrange_kernel, z_lo, z_hi),
                (),
                from_z,
                [(((z_hi - z_lo) * piece, BLK), BF16)],
                wait=wait,
                moved=4 * nz * piece * BLK,
            )[0]

        tail = arrange(z_first, nz, (ids,))
        tail = [tail] + [swap_dp(tail, k) for k in range(1, ndp)]
        head = arrange(0, z_first, tail[1:2])
        head = [head] + [swap_dp(head, k) for k in range(1, ndp)]
        w_tail, kv, key = call(
            functools.partial(keys_kernel, z_last, shard, piece),
            (ids,),
            [x] + [v for part in tail for v in (part, swap_core(part))],
            [((NNZ * BLK - cut, BLK), BF16), ((tok, 2 * HD), BF16), ((tok, HD), BF16)],
            flops=2 * tok * (NCB - NQ) * NBR * BLK * BLK,
            moved=3 * 2**20,
        )
        w_head, query = call(
            functools.partial(queries_kernel, z_first, shard, piece),
            (ids,),
            [x, w_tail] + [v for part in head for v in (part, swap_core(part))],
            [((cut, BLK), BF16), ((tok * NQ, HD), BF16)],
            flops=2 * tok * NQ * NBR * BLK * BLK,
            moved=6 * 2**20,
        )
        weights = [w_head, w_tail]
    else:
        weights = [lax.all_gather(w_packed, "ctx", axis=0, tiled=True)]
        query, kv, key = call(
            project_kernel,
            (ids,),
            (x, *weights),
            [((tok * NQ, HD), BF16), ((tok, 2 * HD), BF16), ((tok, HD), BF16)],
            flops=2 * tok * NNZ * BLK * BLK,
            moved=4 * 2**20,
        )

    kv_pieces = []
    for k in range(nz):
        part = kv if k == 0 else shift_z(kv, k)
        kv_pieces += [part, swap_core(part)]
    outs = call(
        functools.partial(attend_kernel, nz),
        (spans,),
        (query, up, *kv_pieces),
        [((NQ, tok, HD), BF16)] + [((tok, 2 * HD), BF16)] * (2 * nz),
        scratch=[
            pltpu.VMEM((length, 2 * HD), BF16),
            pltpu.VMEM((tok * NQ, HD), BF16),
            pltpu.VMEM((tok * NQ, HD), BF16),
            pltpu.VMEM((length, half), F32),
            pltpu.VMEM((length, half), F32),
            pltpu.VMEM((length, 2 * HD), F32),
            pltpu.VMEM((HD, half), F32),
        ],
        flops=10 * tok * NQ * length * HD // 2,
        moved=4 * 2**20,
        exps=tok * NQ * length // 2,
    )
    dq, keep, send = outs[0], outs[1 : nz + 1], outs[nz + 1 :]
    sums = [add(keep[k], swap_core(send[k])) for k in range(nz)]
    kv_terms = [sums[0]] + [shift_z(sums[k], k) for k in range(1, nz)]

    def weight_terms(z_lo, z_count, grads):
        first = z_lo * 2 * shard // (NBR * BLK)
        last = ((z_lo + z_count) * 2 * shard - 1) // (NBR * BLK)
        return call(
            functools.partial(terms_kernel, z_lo, z_count, shard, piece),
            (ids,),
            (xt, xt_other, *grads),
            [((z_count * piece, BLK), BF16)] * ndp,
            scratch=[
                pltpu.VMEM((last - first + 1, 2 * tok, HD), BF16),
                pltpu.VMEM((z_count * shard, BLK), BF16),
            ],
            flops=4 * tok * z_count * shard * BLK,
            moved=4 * 2**20,
        )

    if fast:
        xt_other = swap_core(xt)
        dq_pair = (dq, swap_core(dq))
        head = weight_terms(0, z_first, dq_pair)
        head = [head[0]] + [swap_dp(head[k], k) for k in range(1, ndp)]
    (dkv,) = call(
        functools.partial(kv_grad_kernel, nz),
        (),
        (key, *kv_terms),
        [((2, tok, HD), BF16)],
        moved=2**19,
    )
    if fast:
        tail = weight_terms(z_first, z_last, (*dq_pair, dkv, swap_core(dkv)))
        tail = [tail[0]] + [swap_dp(tail[k], k) for k in range(1, ndp)]
        by_z = call(
            functools.partial(sum_kernel, ndp, nz, z_first, piece),
            (),
            (*head, *tail),
            [((piece, BLK), BF16)] * nz,
            scratch=[pltpu.VMEM((nz * piece, BLK), BF16)],
            moved=2 * 2**20,
        )
        owned = by_z[0].astype(F32)
        for k in range(1, nz):
            owned = owned + shift_z(by_z[k], k).astype(F32)
        owned = owned.astype(BF16)
        (grad_weights,) = call(
            functools.partial(place_kernel, piece),
            (),
            [owned] + [swap_dp(owned, k) for k in range(1, ndp)],
            [((shard, BLK), F32)],
            moved=2**20,
        )
    else:
        (partial_w,) = call(
            all_terms_kernel,
            (ids,),
            (xt, dq, dkv),
            [((NNZ * BLK, BLK), BF16)],
            flops=2 * tok * NNZ * BLK * BLK,
            moved=4 * 2**20,
        )
        received = lax.all_to_all(
            partial_w.reshape(nctx, shard, BLK), "ctx", split_axis=0, concat_axis=0, tiled=True
        )
        grad_weights = lax.psum(jnp.sum(received.astype(F32), axis=0), "dp")

    (grad_tokens,) = call(
        token_grad_kernel,
        (ids,),
        (dq, dkv, *weights),
        [((tok, width), BF16)],
        scratch=[pltpu.VMEM((tok, width), F32)],
        flops=2 * tok * NNZ * BLK * BLK,
        moved=4 * 2**20,
    )
    return (grad_tokens[None], grad_weights)


def solution(mesh):
    in_specs = (P("dp", "ctx", None), P("dp", "ctx", None), P("ctx", None), P(), P())
    out_specs = (P("dp", "ctx", None), P("ctx", None))
    return jax.shard_map(
        functools.partial(per_device, mesh.shape["dp"]),
        mesh=mesh,
        in_specs=in_specs,
        out_specs=out_specs,
        check_vma=False,
    )
```

```python
import functools
import math

import jax
import jax.numpy as jnp
from jax import lax
from jax.experimental import pallas as pl
from jax.experimental.pallas import tpu as pltpu
from jax.sharding import PartitionSpec as P

HD = 128
BLK = 128
QPG = 8
GROUPS = 1
SPAN = 64
NBR = 8
NCB = 10
NNZ = 80
NQ = GROUPS * QPG
KEYS = 128
EPSILON = 1e-06
SCALE = 1.0 / math.sqrt(HD)
LOG2E = math.log2(math.e)

F32 = jnp.float32
BF16 = jnp.bfloat16
VMEM = pl.BlockSpec(memory_space=pltpu.VMEM)
SMEM = pl.BlockSpec(memory_space=pltpu.SMEM)
ANY = pl.BlockSpec(memory_space=pl.ANY)


def nbytes(shape, dtype):
    return math.prod(shape) * jnp.dtype(dtype).itemsize


def call(kernel, scalars, arrays, outs, scratch=(), wait=(), flops=0, moved=0, exps=0):
    def body(*refs):
        at = len(scalars) + len(arrays)
        kernel(*refs[:at], *refs[at + len(wait) :])

    held = [(v.shape, v.dtype) for v in arrays] + [(s, t) for s, t in outs]
    held += [(v.shape, v.dtype) for v in scratch]
    need = sum(nbytes(s, t) for s, t in held)
    return pl.pallas_call(
        body,
        in_specs=[SMEM] * len(scalars) + [VMEM] * len(arrays) + [ANY] * len(wait),
        out_specs=[SMEM if t == jnp.int32 else VMEM for _, t in outs],
        out_shape=[jax.ShapeDtypeStruct(s, t) for s, t in outs],
        scratch_shapes=list(scratch),
        compiler_params=pltpu.CompilerParams(vmem_limit_bytes=need + need // 4 + 4 * 2**20),
        cost_estimate=pl.CostEstimate(flops=flops, bytes_accessed=moved, transcendentals=exps),
    )(*scalars, *arrays, *wait)


def after(value, *wait):
    return pl.pallas_call(
        lambda *refs: None,
        in_specs=[ANY] * (1 + len(wait)),
        out_specs=ANY,
        out_shape=jax.ShapeDtypeStruct(value.shape, value.dtype),
        input_output_aliases={0: 0},
        compiler_params=pltpu.CompilerParams(vmem_limit_bytes=2**20),
    )(value, *wait)


def dot(a, b, contract=((1,), (0,))):
    return lax.dot_general(a, b, (contract, ((), ())), preferred_element_type=F32)


def rows_at(start, size, step):
    return pl.ds(pl.multiple_of(start, step), size)


def inverse_rms(values):
    return lax.rsqrt(jnp.mean(values * values, axis=-1, keepdims=True) + EPSILON)


def norm_backward(values, factor, upstream):
    return factor * upstream - values * (factor * factor * factor) * jnp.mean(
        upstream * values, axis=-1, keepdims=True
    )


def prepare_kernel(ids, spans, x_ref, xt_ref, ids_out, spans_out):
    for b in range(x_ref.shape[1] // BLK):
        xt_ref[b * BLK : (b + 1) * BLK, :] = x_ref[:, b * BLK : (b + 1) * BLK].T
    for source, out in ((ids, ids_out), (spans, spans_out)):

        @pl.loop(0, source.shape[0])
        def _(i):
            for j in range(source.shape[1]):
                out[i, j] = source[i, j]


def stack_kernel(*refs):
    rows = refs[0].shape[0]
    for k, ref in enumerate(refs[:-1]):
        refs[-1][k * rows : (k + 1) * rows, :] = ref[...]


def join_shards(shards, base, w_ref):
    core = lax.axis_index("ctx") % 2
    shard = shards[0].shape[0]
    for n, ref in enumerate(shards):
        at = base + (core if n == 0 else 1 - core) * shard
        w_ref[rows_at(at, shard, 128), :] = ref[...]


def join_pieces(pieces, slot, shard, piece, base, w_ref):
    core, dp = lax.axis_index("ctx") % 2, lax.axis_index("dp")
    for n, ref in enumerate(pieces):
        at = base + (core if n % 2 == 0 else 1 - core) * shard + (dp ^ (n // 2)) * piece
        w_ref[rows_at(at, piece, 16), :] = ref[slot * piece : (slot + 1) * piece, :]


def column_of(c, ids, x_ref):
    return jnp.concatenate(
        [x_ref[:, rows_at(ids[c, r] * BLK, BLK, BLK)] for r in range(NBR)], axis=1
    )


def project_keys(ids, x_ref, w_ref, kv_ref, key_ref):
    wide = NBR * BLK
    for c in range(NQ, NCB):
        out = dot(column_of(c, ids, x_ref), w_ref[c * wide : (c + 1) * wide, :]).astype(BF16)
        if c == NQ:
            key = out.astype(F32)
            key_ref[...] = out
            kv_ref[:, :HD] = (key * inverse_rms(key)).astype(BF16)
        else:
            kv_ref[:, HD:] = out


def keys_kernel(nz, ids, x_ref, *refs):
    shards, pieces, (w_ref, kv_ref, key_ref) = refs[:2], refs[2:-3], refs[-3:]
    shard, piece = shards[0].shape[0], pieces[0].shape[0] // (nz - 1)
    zi = lax.axis_index("ctx") // 2
    join_shards(shards, zi * 2 * shard, w_ref)
    for k in range(1, nz):
        base = lax.rem(zi + nz - k, nz) * 2 * shard
        join_pieces(pieces, k - 1, shard, piece, base, w_ref)
    project_keys(ids, x_ref, w_ref, kv_ref, key_ref)


def queries_kernel(ids, x_ref, w_ref, q_ref):
    wide = NBR * BLK
    for c in range(NQ):
        out = dot(column_of(c, ids, x_ref), w_ref[c * wide : (c + 1) * wide, :]).astype(BF16)
        for p in range(2):
            at = (p * NQ + c) * SPAN
            q_ref[at : at + SPAN, :] = out[p * SPAN : (p + 1) * SPAN, :]


def project_kernel(ids, x_ref, w_ref, q_ref, kv_ref, key_ref):
    project_keys(ids, x_ref, w_ref, kv_ref, key_ref)
    queries_kernel(ids, x_ref, w_ref, q_ref)


def attend_kernel(nz, spans, q_ref, up_ref, *refs):
    pieces = refs[: 2 * nz]
    dq_ref = refs[2 * nz]
    keep = refs[2 * nz + 1 : 3 * nz + 1]
    send = refs[3 * nz + 1 : 4 * nz + 1]
    kv, qhat, up, expo, dprob, acc, dq_t = refs[4 * nz + 1 :]
    half = NQ * SPAN
    me = lax.axis_index("ctx")
    zi, core = me // 2, me % 2
    for k in range(nz):
        z_from = lax.rem(zi + nz - k, nz)
        for other in range(2):
            source = z_from * 2 + (core if other == 0 else 1 - core)
            for p in range(2):
                kv[rows_at(spans[source, p] * SPAN, SPAN, SPAN), :] = pieces[2 * k + other][
                    p * SPAN : (p + 1) * SPAN, :
                ]
    query = q_ref[...].astype(F32)
    qhat[...] = (query * inverse_rms(query)).astype(BF16)
    for p in range(2):
        for h in range(NQ):
            at = (p * NQ + h) * SPAN
            up[at : at + SPAN, :] = up_ref[p * SPAN : (p + 1) * SPAN, h * HD : (h + 1) * HD]
    acc[...] = jnp.zeros_like(acc)
    key_row = lax.broadcasted_iota(jnp.int32, (KEYS, half), 0)
    query_at = lax.broadcasted_iota(jnp.int32, (KEYS, half), 1) % SPAN
    for p in range(2):
        span = spans[me, p]
        blocks = ((span + 1) * SPAN + KEYS - 1) // KEYS
        q_part = qhat[p * half : (p + 1) * half, :]
        up_part = up[p * half : (p + 1) * half, :]
        limit = query_at + span * SPAN

        def forward(b, sums):
            rows = rows_at(b * KEYS, KEYS, KEYS)
            raw = dot(kv[rows, :HD], q_part, ((1,), (1,)))
            e = jnp.where(key_row + b * KEYS <= limit, jnp.exp2(raw * (SCALE * LOG2E)), 0.0)
            dp = dot(kv[rows, HD:], up_part, ((1,), (1,)))
            expo[rows, :] = e
            dprob[rows, :] = dp
            weighted = e.astype(BF16).astype(F32) * dp
            return (
                sums[0] + jnp.sum(e.reshape(KEYS // 8, 8, half), axis=0),
                sums[1] + jnp.sum(weighted.reshape(KEYS // 8, 8, half), axis=0),
            )

        zero = jnp.zeros((8, half), F32)
        total, weighted = lax.fori_loop(0, blocks, forward, (zero, zero))
        inverse = 1.0 / jnp.sum(total, axis=0, keepdims=True)
        delta = jnp.sum(weighted, axis=0, keepdims=True) * inverse
        dq_t[...] = jnp.zeros_like(dq_t)

        def backward(b, carry):
            rows = rows_at(b * KEYS, KEYS, KEYS)
            prob = expo[rows, :] * inverse
            dscore = (prob * (dprob[rows, :] - delta) * SCALE).astype(BF16)
            acc[rows, :HD] += dot(dscore, q_part)
            acc[rows, HD:] += dot(prob.astype(BF16), up_part)
            dq_t[...] += dot(kv[rows, :HD].T, dscore)
            return carry

        lax.fori_loop(0, blocks, backward, 0)
        q_rows = q_ref[p * half : (p + 1) * half, :].astype(F32)
        dq = norm_backward(q_rows, inverse_rms(q_rows), dq_t[...].T).astype(BF16)
        for h in range(NQ):
            dq_ref[h, p * SPAN : (p + 1) * SPAN, :] = dq[h * SPAN : (h + 1) * SPAN, :]
    for k in range(nz):
        z_to = lax.rem(zi + k, nz)
        for p in range(2):
            part = slice(p * SPAN, (p + 1) * SPAN)
            for out, owner in ((keep[k], z_to * 2 + core), (send[k], z_to * 2 + 1 - core)):
                rows = rows_at(spans[owner, p] * SPAN, SPAN, SPAN)
                out[part, :] = acc[rows, :].astype(BF16)


def kv_grad_kernel(nz, key_ref, *refs):
    terms, dkv_ref = refs[:nz], refs[nz]
    total = terms[0][...].astype(F32)
    for term in terms[1:]:
        total = total + term[...].astype(F32)
    key = key_ref[...].astype(F32)
    dkv_ref[0, :, :] = norm_backward(key, inverse_rms(key), total[:, :HD]).astype(BF16)
    dkv_ref[1, :, :] = total[:, HD:].astype(BF16)


def terms_kernel(z_first, z_count, shard, piece, ids, xt, xt_other, *refs):
    tok = xt.shape[1]
    grads, work = refs[-2:]
    columns = grads.shape[0]
    first = z_first * 2 * shard // (NBR * BLK)
    ndp = shard // piece
    sources, outs = refs[: -2 - ndp], refs[-2 - ndp : -2]
    for n, ref in enumerate(sources):
        other = n % 2
        for i in range(ref.shape[0]):
            c = i - first if n < 2 else NQ + i - first
            if 0 <= c < columns:
                grads[c, other * tok : (other + 1) * tok, :] = ref[i]
    core, dp = lax.axis_index("ctx") % 2, lax.axis_index("dp")
    count = shard // BLK
    for z in range(z_count):
        for i in range(count):
            b = (2 * (z_first + z) + core) * count + i
            c = b // NBR
            rows = rows_at(ids[c, b % NBR] * BLK, BLK, BLK)
            picked = jnp.concatenate([xt[rows, :], xt_other[rows, :]], axis=1)
            at = (z * count + i) * BLK
            work[at : at + BLK, :] = dot(picked, grads[c - first]).astype(BF16)
    for k in range(ndp):
        for z in range(z_count):
            at = z * shard + lax.bitwise_xor(dp, k) * piece
            outs[k][z * piece : (z + 1) * piece, :] = work[rows_at(at, piece, 16), :]


def all_terms_kernel(ids, xt, dq_ref, dkv_ref, out_ref):
    for c in range(NCB):
        picked = jnp.concatenate(
            [xt[rows_at(ids[c, r] * BLK, BLK, BLK), :] for r in range(NBR)], axis=0
        )
        grad = dq_ref[c] if c < NQ else dkv_ref[c - NQ]
        out_ref[c * NBR * BLK : (c + 1) * NBR * BLK, :] = dot(picked, grad).astype(BF16)


def sum_kernel(ndp, nz, piece, *refs):
    head, tail = refs[:ndp], refs[ndp : 2 * ndp]
    outs, work = refs[2 * ndp : 2 * ndp + nz], refs[2 * ndp + nz]
    for group, first, count in ((head, 0, nz - 1), (tail, nz - 1, 1)):
        total = group[0][...].astype(F32)
        for term in group[1:]:
            total = total + term[...].astype(F32)
        work[first * piece : (first + count) * piece, :] = total.astype(BF16)
    for k in range(nz):
        at = lax.rem(lax.axis_index("ctx") // 2 + k, nz) * piece
        outs[k][...] = work[rows_at(at, piece, 16), :]


def place_kernel(piece, *refs):
    for k, ref in enumerate(refs[:-1]):
        at = lax.bitwise_xor(lax.axis_index("dp"), k) * piece
        refs[-1][rows_at(at, piece, 16), :] = ref[...].astype(F32)


def token_grad_kernel(ids, dq_ref, dkv_ref, w_ref, out_ref, work):
    wide = NBR * BLK
    cover = out_ref.shape[1] // wide
    for c in range(NCB):
        grad = dq_ref[c] if c < NQ else dkv_ref[c - NQ]
        spread = dot(grad, w_ref[c * wide : (c + 1) * wide, :], ((1,), (1,)))
        for r in range(NBR):
            columns = rows_at(ids[c, r] * BLK, BLK, BLK)
            term = spread[:, r * BLK : (r + 1) * BLK]
            if c < cover:
                work[:, columns] = term
            else:
                work[:, columns] += term
    out_ref[...] = work[...].astype(BF16)


def per_device(ndp, tokens, grad_attn, w_packed, ids, spans):
    nctx = lax.axis_size("ctx")
    nz = nctx // 2
    dp = lax.axis_index("dp")
    x, up = tokens[0], grad_attn[0]
    tok, width = x.shape
    length = spans.shape[0] * 2 * SPAN
    shard = w_packed.shape[0]
    piece = shard // ndp
    cut = (nz - 1) * 2 * shard
    half = NQ * SPAN
    fast = 2 < nz and cut <= NQ * NBR * BLK and shard % BLK == 0
    fast = fast and shard % (16 * ndp) == 0 and 1 < ndp and ndp & (ndp - 1) == 0

    def swap_core(v):
        return lax.ppermute(v, "ctx", [(i, i ^ 1) for i in range(nctx)])

    def shift_z(v, k):
        return lax.ppermute(
            v, "ctx", [(i, ((i // 2 + k) % nz) * 2 + i % 2) for i in range(nctx)]
        )

    def swap_dp(v, k):
        return lax.ppermute(v, "dp", [(i, i ^ k) for i in range(ndp)])

    def add(a, b):
        return (a.astype(F32) + b.astype(F32)).astype(BF16)

    xt, ids, spans = call(
        prepare_kernel,
        (ids, spans),
        (x,),
        [((width, tok), BF16), (ids.shape, jnp.int32), (spans.shape, jnp.int32)],
        moved=4 * x.size,
    )

    if fast:
        mine = lax.dynamic_slice_in_dim(w_packed, dp * piece, piece, 0)
        from_z = [shift_z(mine, k) for k in range(1, nz)]

        def both_cores(parts):
            return [v for part in parts for v in (part, swap_core(part))]

        shards = both_cores([w_packed])
        (stacked,) = call(
            stack_kernel,
            (),
            from_z,
            [(((nz - 1) * piece, BLK), BF16)],
            wait=(ids, shards[1]),
            moved=4 * nz * piece * BLK,
        )
        xt_other = swap_core(after(xt, stacked))
        pieces = [stacked] + [swap_dp(stacked, k) for k in range(1, ndp)]
        weights, kv, key = call(
            functools.partial(keys_kernel, nz),
            (ids,),
            (x, *shards, *both_cores(pieces)),
            [((NNZ * BLK, BLK), BF16), ((tok, 2 * HD), BF16), ((tok, HD), BF16)],
            wait=(xt_other,),
            flops=2 * tok * (NCB - NQ) * NBR * BLK * BLK,
            moved=6 * 2**20,
        )
        (query,) = call(
            queries_kernel,
            (ids,),
            (x, weights),
            [((tok * NQ, HD), BF16)],
            flops=2 * tok * NQ * NBR * BLK * BLK,
            moved=3 * 2**20,
        )
    else:
        weights = lax.all_gather(w_packed, "ctx", axis=0, tiled=True)
        query, kv, key = call(
            project_kernel,
            (ids,),
            (x, weights),
            [((tok * NQ, HD), BF16), ((tok, 2 * HD), BF16), ((tok, HD), BF16)],
            flops=2 * tok * NNZ * BLK * BLK,
            moved=4 * 2**20,
        )

    kv_pieces = []
    for k in range(nz):
        part = kv if k == 0 else shift_z(kv, k)
        kv_pieces += [part, swap_core(part)]
    outs = call(
        functools.partial(attend_kernel, nz),
        (spans,),
        (query, up, *kv_pieces),
        [((NQ, tok, HD), BF16)] + [((tok, 2 * HD), BF16)] * (2 * nz),
        scratch=[
            pltpu.VMEM((length, 2 * HD), BF16),
            pltpu.VMEM((tok * NQ, HD), BF16),
            pltpu.VMEM((tok * NQ, HD), BF16),
            pltpu.VMEM((length, half), F32),
            pltpu.VMEM((length, half), F32),
            pltpu.VMEM((length, 2 * HD), F32),
            pltpu.VMEM((HD, half), F32),
        ],
        flops=10 * tok * NQ * length * HD // 2,
        moved=4 * 2**20,
        exps=tok * NQ * length // 2,
    )
    dq, keep, send = outs[0], outs[1 : nz + 1], outs[nz + 1 :]
    sums = [add(keep[k], swap_core(send[k])) for k in range(nz)]
    kv_terms = [sums[0]] + [shift_z(sums[k], k) for k in range(1, nz)]

    def weight_terms(z_lo, z_count, grads):
        first = z_lo * 2 * shard // (NBR * BLK)
        last = ((z_lo + z_count) * 2 * shard - 1) // (NBR * BLK)
        return call(
            functools.partial(terms_kernel, z_lo, z_count, shard, piece),
            (ids,),
            (xt, xt_other, *grads),
            [((z_count * piece, BLK), BF16)] * ndp,
            scratch=[
                pltpu.VMEM((last - first + 1, 2 * tok, HD), BF16),
                pltpu.VMEM((z_count * shard, BLK), BF16),
            ],
            flops=4 * tok * z_count * shard * BLK,
            moved=4 * 2**20,
        )

    if fast:
        dq_pair = (dq, swap_core(dq))
        head = weight_terms(0, nz - 1, dq_pair)
        head = [head[0]] + [swap_dp(head[k], k) for k in range(1, ndp)]
    (dkv,) = call(
        functools.partial(kv_grad_kernel, nz),
        (),
        (key, *kv_terms),
        [((2, tok, HD), BF16)],
        moved=2**19,
    )
    if fast:
        tail = weight_terms(nz - 1, 1, (*dq_pair, dkv, swap_core(dkv)))
        tail = [tail[0]] + [swap_dp(tail[k], k) for k in range(1, ndp)]
        by_z = call(
            functools.partial(sum_kernel, ndp, nz, piece),
            (),
            (*head, *tail),
            [((piece, BLK), BF16)] * nz,
            scratch=[pltpu.VMEM((nz * piece, BLK), BF16)],
            moved=2 * 2**20,
        )
        owned = by_z[0].astype(F32)
        for k in range(1, nz):
            owned = owned + shift_z(by_z[k], k).astype(F32)
        owned = owned.astype(BF16)
        (grad_weights,) = call(
            functools.partial(place_kernel, piece),
            (),
            [owned] + [swap_dp(owned, k) for k in range(1, ndp)],
            [((shard, BLK), F32)],
            moved=2**20,
        )
    else:
        (partial_w,) = call(
            all_terms_kernel,
            (ids,),
            (xt, dq, dkv),
            [((NNZ * BLK, BLK), BF16)],
            flops=2 * tok * NNZ * BLK * BLK,
            moved=4 * 2**20,
        )
        received = lax.all_to_all(
            partial_w.reshape(nctx, shard, BLK), "ctx", split_axis=0, concat_axis=0, tiled=True
        )
        grad_weights = lax.psum(jnp.sum(received.astype(F32), axis=0), "dp")

    (grad_tokens,) = call(
        token_grad_kernel,
        (ids,),
        (dq, dkv, weights),
        [((tok, width), BF16)],
        scratch=[pltpu.VMEM((tok, width), F32)],
        flops=2 * tok * NNZ * BLK * BLK,
        moved=4 * 2**20,
    )
    return (grad_tokens[None], grad_weights)


def solution(mesh):
    in_specs = (P("dp", "ctx", None), P("dp", "ctx", None), P("ctx", None), P(), P())
    out_specs = (P("dp", "ctx", None), P("ctx", None))
    return jax.shard_map(
        functools.partial(per_device, mesh.shape["dp"]),
        mesh=mesh,
        in_specs=in_specs,
        out_specs=out_specs,
        check_vma=False,
    )
```

```python
import functools
import math

import jax
import jax.numpy as jnp
from jax import lax
from jax.experimental import pallas as pl
from jax.experimental.pallas import tpu as pltpu
from jax.sharding import PartitionSpec as P

HD = 128
BLK = 128
QPG = 8
GROUPS = 1
SPAN = 64
NBR = 8
NCB = 10
NNZ = 80
NQ = GROUPS * QPG
EPSILON = 1e-06
SCALE = 1.0 / math.sqrt(HD)
LOG2E = math.log2(math.e)

F32 = jnp.float32
BF16 = jnp.bfloat16
VMEM = pl.BlockSpec(memory_space=pltpu.VMEM)
SMEM = pl.BlockSpec(memory_space=pltpu.SMEM)
ANY = pl.BlockSpec(memory_space=pl.ANY)


def nbytes(shape, dtype):
    return math.prod(shape) * jnp.dtype(dtype).itemsize


def call(kernel, scalars, arrays, outs, scratch=(), wait=(), flops=0, moved=0, exps=0):
    def body(*refs):
        at = len(scalars) + len(arrays)
        kernel(*refs[:at], *refs[at + len(wait) :])

    held = [(v.shape, v.dtype) for v in arrays] + [(s, t) for s, t in outs]
    held += [(v.shape, v.dtype) for v in scratch]
    need = sum(nbytes(s, t) for s, t in held)
    return pl.pallas_call(
        body,
        in_specs=[SMEM] * len(scalars) + [VMEM] * len(arrays) + [ANY] * len(wait),
        out_specs=[SMEM if t == jnp.int32 else VMEM for _, t in outs],
        out_shape=[jax.ShapeDtypeStruct(s, t) for s, t in outs],
        scratch_shapes=list(scratch),
        compiler_params=pltpu.CompilerParams(vmem_limit_bytes=need + need // 4 + 4 * 2**20),
        cost_estimate=pl.CostEstimate(flops=flops, bytes_accessed=moved, transcendentals=exps),
    )(*scalars, *arrays, *wait)


def after(value, *wait):
    return pl.pallas_call(
        lambda *refs: None,
        in_specs=[ANY] * (1 + len(wait)),
        out_specs=ANY,
        out_shape=jax.ShapeDtypeStruct(value.shape, value.dtype),
        input_output_aliases={0: 0},
        compiler_params=pltpu.CompilerParams(vmem_limit_bytes=2**20),
    )(value, *wait)


def dot(a, b, contract=((1,), (0,))):
    return lax.dot_general(a, b, (contract, ((), ())), preferred_element_type=F32)


def rows_at(start, size, step):
    return pl.ds(pl.multiple_of(start, step), size)


def inverse_rms(values):
    return lax.rsqrt(jnp.mean(values * values, axis=-1, keepdims=True) + EPSILON)


def norm_backward(values, factor, upstream):
    return factor * upstream - values * (factor * factor * factor) * jnp.mean(
        upstream * values, axis=-1, keepdims=True
    )


def head_rows(p, c):
    return slice((p * NQ + c) * SPAN, (p * NQ + c + 1) * SPAN)


def prepare_kernel(ids, spans, x_ref, up_ref, xt_ref, up_out, ids_out, spans_out):
    for p in range(2):
        for h in range(NQ):
            up_out[head_rows(p, h), :] = up_ref[p * SPAN : (p + 1) * SPAN, h * HD : (h + 1) * HD]
    for b in range(x_ref.shape[1] // BLK):
        xt_ref[b * BLK : (b + 1) * BLK, :] = x_ref[:, b * BLK : (b + 1) * BLK].T
    for source, out in ((ids, ids_out), (spans, spans_out)):

        @pl.loop(0, source.shape[0])
        def _(i):
            for j in range(source.shape[1]):
                out[i, j] = source[i, j]


def stack_kernel(*refs):
    rows = refs[0].shape[0]
    for k, ref in enumerate(refs[:-1]):
        refs[-1][k * rows : (k + 1) * rows, :] = ref[...]


def join_shards(shards, base, w_ref):
    core = lax.axis_index("ctx") % 2
    shard = shards[0].shape[0]
    for n, ref in enumerate(shards):
        at = base + (core if n == 0 else 1 - core) * shard
        w_ref[rows_at(at, shard, 128), :] = ref[...]


def join_pieces(pieces, slot, shard, piece, base, w_ref):
    core, dp = lax.axis_index("ctx") % 2, lax.axis_index("dp")
    for n, ref in enumerate(pieces):
        at = base + (core if n % 2 == 0 else 1 - core) * shard + (dp ^ (n // 2)) * piece
        w_ref[rows_at(at, piece, 16), :] = ref[slot * piece : (slot + 1) * piece, :]


def column_of(c, ids, x_ref):
    return jnp.concatenate(
        [x_ref[:, rows_at(ids[c, r] * BLK, BLK, BLK)] for r in range(NBR)], axis=1
    )


def project_keys(ids, x_ref, w_ref, kv_ref, key_ref):
    wide = NBR * BLK
    for c in range(NQ, NCB):
        out = dot(column_of(c, ids, x_ref), w_ref[c * wide : (c + 1) * wide, :]).astype(BF16)
        if c == NQ:
            key = out.astype(F32)
            key_ref[...] = out
            kv_ref[:, :HD] = (key * inverse_rms(key)).astype(BF16)
        else:
            kv_ref[:, HD:] = out


def keys_kernel(nz, ids, x_ref, *refs):
    shards, pieces, (w_ref, kv_ref, key_ref) = refs[:2], refs[2:-3], refs[-3:]
    shard, piece = shards[0].shape[0], pieces[0].shape[0] // (nz - 1)
    zi = lax.axis_index("ctx") // 2
    join_shards(shards, zi * 2 * shard, w_ref)
    for k in range(1, nz):
        base = lax.rem(zi + nz - k, nz) * 2 * shard
        join_pieces(pieces, k - 1, shard, piece, base, w_ref)
    project_keys(ids, x_ref, w_ref, kv_ref, key_ref)


def queries_kernel(ids, x_ref, w_ref, q_ref, qhat_ref):
    wide = NBR * BLK
    for c in range(NQ):
        out = dot(column_of(c, ids, x_ref), w_ref[c * wide : (c + 1) * wide, :]).astype(BF16)
        query = out.astype(F32)
        normed = (query * inverse_rms(query)).astype(BF16)
        for p in range(2):
            q_ref[head_rows(p, c), :] = out[p * SPAN : (p + 1) * SPAN, :]
            qhat_ref[head_rows(p, c), :] = normed[p * SPAN : (p + 1) * SPAN, :]


def project_kernel(ids, x_ref, w_ref, q_ref, qhat_ref, kv_ref, key_ref):
    project_keys(ids, x_ref, w_ref, kv_ref, key_ref)
    queries_kernel(ids, x_ref, w_ref, q_ref, qhat_ref)


def attend_kernel(nz, keys, spans, q_ref, qhat, up, *refs):
    pieces = refs[: 2 * nz]
    dq_ref = refs[2 * nz]
    keep = refs[2 * nz + 1 : 3 * nz + 1]
    send = refs[3 * nz + 1 : 4 * nz + 1]
    kv, expo, dprob, acc, dq_t = refs[4 * nz + 1 :]
    half = NQ * SPAN
    me = lax.axis_index("ctx")
    zi, core = me // 2, me % 2
    for k in range(nz):
        z_from = lax.rem(zi + nz - k, nz)
        for other in range(2):
            source = z_from * 2 + (core if other == 0 else 1 - core)
            for p in range(2):
                kv[rows_at(spans[source, p] * SPAN, SPAN, SPAN), :] = pieces[2 * k + other][
                    p * SPAN : (p + 1) * SPAN, :
                ]
    acc[...] = jnp.zeros_like(acc)
    key_row = lax.broadcasted_iota(jnp.int32, (keys, half), 0)
    query_at = lax.broadcasted_iota(jnp.int32, (keys, half), 1) % SPAN
    for p in range(2):
        span = spans[me, p]
        blocks = ((span + 1) * SPAN + keys - 1) // keys
        q_part = qhat[p * half : (p + 1) * half, :]
        up_part = up[p * half : (p + 1) * half, :]
        limit = query_at + span * SPAN

        def forward(b, sums):
            rows = rows_at(b * keys, keys, keys)
            raw = dot(kv[rows, :HD], q_part, ((1,), (1,)))
            e = jnp.where(key_row + b * keys <= limit, jnp.exp2(raw * (SCALE * LOG2E)), 0.0)
            dp = dot(kv[rows, HD:], up_part, ((1,), (1,)))
            expo[rows, :] = e
            dprob[rows, :] = dp
            weighted = e.astype(BF16).astype(F32) * dp
            return (
                sums[0] + jnp.sum(e.reshape(keys // 8, 8, half), axis=0),
                sums[1] + jnp.sum(weighted.reshape(keys // 8, 8, half), axis=0),
            )

        zero = jnp.zeros((8, half), F32)
        total, weighted = lax.fori_loop(0, blocks, forward, (zero, zero))
        inverse = 1.0 / jnp.sum(total, axis=0, keepdims=True)
        delta = jnp.sum(weighted, axis=0, keepdims=True) * inverse
        dq_t[...] = jnp.zeros_like(dq_t)

        def backward(b, carry):
            rows = rows_at(b * keys, keys, keys)
            prob = expo[rows, :] * inverse
            dscore = (prob * (dprob[rows, :] - delta) * SCALE).astype(BF16)
            acc[rows, :HD] += dot(dscore, q_part)
            acc[rows, HD:] += dot(prob.astype(BF16), up_part)
            dq_t[...] += dot(kv[rows, :HD].T, dscore)
            return carry

        lax.fori_loop(0, blocks, backward, 0)
        q_rows = q_ref[p * half : (p + 1) * half, :].astype(F32)
        dq = norm_backward(q_rows, inverse_rms(q_rows), dq_t[...].T).astype(BF16)
        for h in range(NQ):
            dq_ref[h, p * SPAN : (p + 1) * SPAN, :] = dq[h * SPAN : (h + 1) * SPAN, :]
    for k in range(nz):
        z_to = lax.rem(zi + k, nz)
        for p in range(2):
            part = slice(p * SPAN, (p + 1) * SPAN)
            for out, owner in ((keep[k], z_to * 2 + core), (send[k], z_to * 2 + 1 - core)):
                rows = rows_at(spans[owner, p] * SPAN, SPAN, SPAN)
                out[part, :] = acc[rows, :].astype(BF16)


def kv_grad_kernel(nz, key_ref, *refs):
    terms, dkv_ref = refs[:nz], refs[nz]
    total = terms[0][...].astype(F32)
    for term in terms[1:]:
        total = total + term[...].astype(F32)
    key = key_ref[...].astype(F32)
    dkv_ref[0, :, :] = norm_backward(key, inverse_rms(key), total[:, :HD]).astype(BF16)
    dkv_ref[1, :, :] = total[:, HD:].astype(BF16)


def terms_kernel(z_first, z_count, shard, piece, ids, xt, xt_other, *refs):
    tok = xt.shape[1]
    grads, work = refs[-2:]
    columns = grads.shape[0]
    first = z_first * 2 * shard // (NBR * BLK)
    ndp = shard // piece
    sources, outs = refs[: -2 - ndp], refs[-2 - ndp : -2]
    for n, ref in enumerate(sources):
        other = n % 2
        for i in range(ref.shape[0]):
            c = i - first if n < 2 else NQ + i - first
            if 0 <= c < columns:
                grads[c, other * tok : (other + 1) * tok, :] = ref[i]
    core, dp = lax.axis_index("ctx") % 2, lax.axis_index("dp")
    count = shard // BLK
    for z in range(z_count):
        for i in range(count):
            b = (2 * (z_first + z) + core) * count + i
            c = b // NBR
            rows = rows_at(ids[c, b % NBR] * BLK, BLK, BLK)
            picked = jnp.concatenate([xt[rows, :], xt_other[rows, :]], axis=1)
            at = (z * count + i) * BLK
            work[at : at + BLK, :] = dot(picked, grads[c - first]).astype(BF16)
    for k in range(ndp):
        for z in range(z_count):
            at = z * shard + lax.bitwise_xor(dp, k) * piece
            outs[k][z * piece : (z + 1) * piece, :] = work[rows_at(at, piece, 16), :]


def all_terms_kernel(ids, xt, dq_ref, dkv_ref, out_ref):
    for c in range(NCB):
        picked = jnp.concatenate(
            [xt[rows_at(ids[c, r] * BLK, BLK, BLK), :] for r in range(NBR)], axis=0
        )
        grad = dq_ref[c] if c < NQ else dkv_ref[c - NQ]
        out_ref[c * NBR * BLK : (c + 1) * NBR * BLK, :] = dot(picked, grad).astype(BF16)


def sum_kernel(ndp, nz, piece, *refs):
    head, tail = refs[:ndp], refs[ndp : 2 * ndp]
    outs, work = refs[2 * ndp : 2 * ndp + nz], refs[2 * ndp + nz]
    for group, first, count in ((head, 0, nz - 1), (tail, nz - 1, 1)):
        total = group[0][...].astype(F32)
        for term in group[1:]:
            total = total + term[...].astype(F32)
        work[first * piece : (first + count) * piece, :] = total.astype(BF16)
    for k in range(nz):
        at = lax.rem(lax.axis_index("ctx") // 2 + k, nz) * piece
        outs[k][...] = work[rows_at(at, piece, 16), :]


def place_kernel(piece, *refs):
    for k, ref in enumerate(refs[:-1]):
        at = lax.bitwise_xor(lax.axis_index("dp"), k) * piece
        refs[-1][rows_at(at, piece, 16), :] = ref[...].astype(F32)


def token_grad_kernel(ids, dq_ref, dkv_ref, w_ref, out_ref, work):
    wide = NBR * BLK
    cover = out_ref.shape[1] // wide
    for c in range(NCB):
        grad = dq_ref[c] if c < NQ else dkv_ref[c - NQ]
        spread = dot(grad, w_ref[c * wide : (c + 1) * wide, :], ((1,), (1,)))
        for r in range(NBR):
            columns = rows_at(ids[c, r] * BLK, BLK, BLK)
            term = spread[:, r * BLK : (r + 1) * BLK]
            if c < cover:
                work[:, columns] = term
            else:
                work[:, columns] += term
    out_ref[...] = work[...].astype(BF16)


def per_device(ndp, tokens, grad_attn, w_packed, ids, spans):
    nctx = lax.axis_size("ctx")
    nz = nctx // 2
    dp = lax.axis_index("dp")
    x = tokens[0]
    tok, width = x.shape
    length = spans.shape[0] * 2 * SPAN
    shard = w_packed.shape[0]
    piece = shard // ndp
    cut = (nz - 1) * 2 * shard
    half = NQ * SPAN
    fast = 2 < nz and cut <= NQ * NBR * BLK and shard % BLK == 0
    fast = fast and shard % (16 * ndp) == 0 and 1 < ndp and ndp & (ndp - 1) == 0

    def swap_core(v):
        return lax.ppermute(v, "ctx", [(i, i ^ 1) for i in range(nctx)])

    def shift_z(v, k):
        return lax.ppermute(
            v, "ctx", [(i, ((i // 2 + k) % nz) * 2 + i % 2) for i in range(nctx)]
        )

    def swap_dp(v, k):
        return lax.ppermute(v, "dp", [(i, i ^ k) for i in range(ndp)])

    def add(a, b):
        return (a.astype(F32) + b.astype(F32)).astype(BF16)

    xt, up, ids, spans = call(
        prepare_kernel,
        (ids, spans),
        (x, grad_attn[0]),
        [
            ((width, tok), BF16),
            ((tok * NQ, HD), BF16),
            (ids.shape, jnp.int32),
            (spans.shape, jnp.int32),
        ],
        moved=4 * x.size,
    )

    if fast:
        mine = lax.dynamic_slice_in_dim(w_packed, dp * piece, piece, 0)
        from_z = [shift_z(mine, k) for k in range(1, nz)]

        def both_cores(parts):
            return [v for part in parts for v in (part, swap_core(part))]

        shards = both_cores([w_packed])
        (stacked,) = call(
            stack_kernel,
            (),
            from_z,
            [(((nz - 1) * piece, BLK), BF16)],
            wait=(ids, shards[1]),
            moved=4 * nz * piece * BLK,
        )
        xt_other = swap_core(after(xt, stacked))
        pieces = [stacked] + [swap_dp(stacked, k) for k in range(1, ndp)]
        weights, kv, key = call(
            functools.partial(keys_kernel, nz),
            (ids,),
            (x, *shards, *both_cores(pieces)),
            [((NNZ * BLK, BLK), BF16), ((tok, 2 * HD), BF16), ((tok, HD), BF16)],
            wait=(xt_other,),
            flops=2 * tok * (NCB - NQ) * NBR * BLK * BLK,
            moved=6 * 2**20,
        )
        query, qhat = call(
            queries_kernel,
            (ids,),
            (x, weights),
            [((tok * NQ, HD), BF16)] * 2,
            flops=16 * tok * NQ * NBR * BLK * BLK,
            moved=3 * 2**20,
        )
    else:
        weights = lax.all_gather(w_packed, "ctx", axis=0, tiled=True)
        query, qhat, kv, key = call(
            project_kernel,
            (ids,),
            (x, weights),
            [((tok * NQ, HD), BF16)] * 2 + [((tok, 2 * HD), BF16), ((tok, HD), BF16)],
            flops=2 * tok * NNZ * BLK * BLK,
            moved=4 * 2**20,
        )

    kv_pieces = []
    for k in range(nz):
        part = kv if k == 0 else shift_z(kv, k)
        kv_pieces += [part, swap_core(after(part, query) if k == nz - 1 else part)]
    outs = call(
        functools.partial(attend_kernel, nz, math.gcd(512, length)),
        (spans,),
        (query, qhat, up, *kv_pieces),
        [((NQ, tok, HD), BF16)] + [((tok, 2 * HD), BF16)] * (2 * nz),
        scratch=[
            pltpu.VMEM((length, 2 * HD), BF16),
            pltpu.VMEM((length, half), F32),
            pltpu.VMEM((length, half), F32),
            pltpu.VMEM((length, 2 * HD), F32),
            pltpu.VMEM((HD, half), F32),
        ],
        flops=10 * tok * NQ * length * HD // 2,
        moved=4 * 2**20,
        exps=tok * NQ * length // 2,
    )
    dq, keep, send = outs[0], outs[1 : nz + 1], outs[nz + 1 :]
    sums = [add(keep[k], swap_core(send[k])) for k in range(nz)]
    kv_terms = [sums[0]] + [shift_z(sums[k], k) for k in range(1, nz)]

    def weight_terms(z_lo, z_count, grads):
        first = z_lo * 2 * shard // (NBR * BLK)
        last = ((z_lo + z_count) * 2 * shard - 1) // (NBR * BLK)
        return call(
            functools.partial(terms_kernel, z_lo, z_count, shard, piece),
            (ids,),
            (xt, xt_other, *grads),
            [((z_count * piece, BLK), BF16)] * ndp,
            scratch=[
                pltpu.VMEM((last - first + 1, 2 * tok, HD), BF16),
                pltpu.VMEM((z_count * shard, BLK), BF16),
            ],
            flops=4 * tok * z_count * shard * BLK,
            moved=4 * 2**20,
        )

    if fast:
        dq_pair = (dq, swap_core(dq))
        head = weight_terms(0, nz - 1, dq_pair)
        head = [head[0]] + [swap_dp(head[k], k) for k in range(1, ndp)]
    (dkv,) = call(
        functools.partial(kv_grad_kernel, nz),
        (),
        (key, *kv_terms),
        [((2, tok, HD), BF16)],
        moved=2**19,
    )
    if fast:
        tail = weight_terms(nz - 1, 1, (*dq_pair, dkv, swap_core(dkv)))
        tail = [tail[0]] + [
            swap_dp(after(tail[k], head[1]) if k == ndp - 1 else tail[k], k) for k in range(1, ndp)
        ]
        by_z = call(
            functools.partial(sum_kernel, ndp, nz, piece),
            (),
            (*head, *tail),
            [((piece, BLK), BF16)] * nz,
            scratch=[pltpu.VMEM((nz * piece, BLK), BF16)],
            moved=2 * 2**20,
        )
        owned = by_z[0].astype(F32)
        for k in range(1, nz):
            owned = owned + shift_z(by_z[k], k).astype(F32)
        owned = owned.astype(BF16)
        (grad_weights,) = call(
            functools.partial(place_kernel, piece),
            (),
            [owned] + [swap_dp(owned, k) for k in range(1, ndp)],
            [((shard, BLK), F32)],
            moved=2**20,
        )
    else:
        (partial_w,) = call(
            all_terms_kernel,
            (ids,),
            (xt, dq, dkv),
            [((NNZ * BLK, BLK), BF16)],
            flops=2 * tok * NNZ * BLK * BLK,
            moved=4 * 2**20,
        )
        received = lax.all_to_all(
            partial_w.reshape(nctx, shard, BLK), "ctx", split_axis=0, concat_axis=0, tiled=True
        )
        grad_weights = lax.psum(jnp.sum(received.astype(F32), axis=0), "dp")

    (grad_tokens,) = call(
        token_grad_kernel,
        (ids,),
        (dq, dkv, weights),
        [((tok, width), BF16)],
        scratch=[pltpu.VMEM((tok, width), F32)],
        flops=2 * tok * NNZ * BLK * BLK,
        moved=4 * 2**20,
    )
    return (grad_tokens[None], grad_weights)


def solution(mesh):
    in_specs = (P("dp", "ctx", None), P("dp", "ctx", None), P("ctx", None), P(), P())
    out_specs = (P("dp", "ctx", None), P("ctx", None))
    return jax.shard_map(
        functools.partial(per_device, mesh.shape["dp"]),
        mesh=mesh,
        in_specs=in_specs,
        out_specs=out_specs,
        check_vma=False,
    )
```

```python
import functools
import math

import jax
import jax.numpy as jnp
from jax import lax
from jax.experimental import pallas as pl
from jax.experimental.pallas import tpu as pltpu
from jax.sharding import PartitionSpec as P

HD = 128
BLK = 128
QPG = 8
GROUPS = 1
SPAN = 64
NBR = 8
NCB = 10
NNZ = 80
NQ = GROUPS * QPG
EPSILON = 1e-06
SCALE = 1.0 / math.sqrt(HD)
LOG2E = math.log2(math.e)

F32 = jnp.float32
BF16 = jnp.bfloat16
VMEM = pl.BlockSpec(memory_space=pltpu.VMEM)
SMEM = pl.BlockSpec(memory_space=pltpu.SMEM)
ANY = pl.BlockSpec(memory_space=pl.ANY)


def nbytes(shape, dtype):
    return math.prod(shape) * jnp.dtype(dtype).itemsize


def call(kernel, scalars, arrays, outs, scratch=(), wait=(), flops=0, moved=0, exps=0):
    def body(*refs):
        at = len(scalars) + len(arrays)
        kernel(*refs[:at], *refs[at + len(wait) :])

    held = [(v.shape, v.dtype) for v in arrays] + [(s, t) for s, t in outs]
    held += [(v.shape, v.dtype) for v in scratch]
    need = sum(nbytes(s, t) for s, t in held)
    return pl.pallas_call(
        body,
        in_specs=[SMEM] * len(scalars) + [VMEM] * len(arrays) + [ANY] * len(wait),
        out_specs=[SMEM if t == jnp.int32 else VMEM for _, t in outs],
        out_shape=[jax.ShapeDtypeStruct(s, t) for s, t in outs],
        scratch_shapes=list(scratch),
        compiler_params=pltpu.CompilerParams(vmem_limit_bytes=need + need // 4 + 4 * 2**20),
        cost_estimate=pl.CostEstimate(flops=flops, bytes_accessed=moved, transcendentals=exps),
    )(*scalars, *arrays, *wait)


def after(value, *wait):
    return pl.pallas_call(
        lambda *refs: None,
        in_specs=[ANY] * (1 + len(wait)),
        out_specs=ANY,
        out_shape=jax.ShapeDtypeStruct(value.shape, value.dtype),
        input_output_aliases={0: 0},
        compiler_params=pltpu.CompilerParams(vmem_limit_bytes=2**20),
    )(value, *wait)


def dot(a, b, contract=((1,), (0,))):
    return lax.dot_general(a, b, (contract, ((), ())), preferred_element_type=F32)


def rows_at(start, size, step):
    return pl.ds(pl.multiple_of(start, step), size)


def inverse_rms(values):
    return lax.rsqrt(jnp.mean(values * values, axis=-1, keepdims=True) + EPSILON)


def norm_backward(values, factor, upstream):
    return factor * upstream - values * (factor * factor * factor) * jnp.mean(
        upstream * values, axis=-1, keepdims=True
    )


def head_rows(p, c):
    return slice((p * NQ + c) * SPAN, (p * NQ + c + 1) * SPAN)


def prepare_kernel(ids, spans, x_ref, up_ref, xt_ref, up_out, ids_out, spans_out):
    for p in range(2):
        for h in range(NQ):
            up_out[head_rows(p, h), :] = up_ref[p * SPAN : (p + 1) * SPAN, h * HD : (h + 1) * HD]
    for b in range(x_ref.shape[1] // BLK):
        xt_ref[b * BLK : (b + 1) * BLK, :] = x_ref[:, b * BLK : (b + 1) * BLK].T
    for source, out in ((ids, ids_out), (spans, spans_out)):

        @pl.loop(0, source.shape[0])
        def _(i):
            for j in range(source.shape[1]):
                out[i, j] = source[i, j]


def part_kernel(w_ref, out):
    rows = out.shape[0]
    out[...] = w_ref[rows_at(lax.axis_index("dp") * rows, rows, 16), :]


def stack_kernel(*refs):
    rows = refs[0].shape[0]
    for k, ref in enumerate(refs[:-1]):
        refs[-1][k * rows : (k + 1) * rows, :] = ref[...]


def join_shards(shards, base, w_ref):
    core = lax.axis_index("ctx") % 2
    shard = shards[0].shape[0]
    for n, ref in enumerate(shards):
        at = base + (core if n == 0 else 1 - core) * shard
        w_ref[rows_at(at, shard, 128), :] = ref[...]


def join_pieces(pieces, slot, shard, piece, base, w_ref):
    core, dp = lax.axis_index("ctx") % 2, lax.axis_index("dp")
    for n, ref in enumerate(pieces):
        at = base + (core if n % 2 == 0 else 1 - core) * shard + (dp ^ (n // 2)) * piece
        w_ref[rows_at(at, piece, 16), :] = ref[slot * piece : (slot + 1) * piece, :]


def column_of(c, ids, x_ref):
    return jnp.concatenate(
        [x_ref[:, rows_at(ids[c, r] * BLK, BLK, BLK)] for r in range(NBR)], axis=1
    )


def project_keys(ids, x_ref, w_ref, first, kv_ref, key_ref):
    wide = NBR * BLK
    for c in range(NQ, NCB):
        at = c * wide - first
        out = dot(column_of(c, ids, x_ref), w_ref[at : at + wide, :]).astype(BF16)
        if c == NQ:
            key = out.astype(F32)
            key_ref[...] = out
            kv_ref[:, :HD] = (key * inverse_rms(key)).astype(BF16)
        else:
            kv_ref[:, HD:] = out


def project_queries(ids, x_ref, w_ref, q_ref, qhat_ref):
    wide = NBR * BLK
    for c in range(NQ):
        out = dot(column_of(c, ids, x_ref), w_ref[c * wide : (c + 1) * wide, :]).astype(BF16)
        query = out.astype(F32)
        normed = (query * inverse_rms(query)).astype(BF16)
        for p in range(2):
            q_ref[head_rows(p, c), :] = out[p * SPAN : (p + 1) * SPAN, :]
            qhat_ref[head_rows(p, c), :] = normed[p * SPAN : (p + 1) * SPAN, :]


def join_planes(nz, shards, pieces, w_ref, last_ref):
    shard, piece = shards[0].shape[0], pieces[0].shape[0] // (nz - 1)
    zi = lax.axis_index("ctx") // 2
    for k in range(nz):
        plane = lax.rem(zi + nz - k, nz)

        def place(base, out):
            if k == 0:
                join_shards(shards, base, out)
            else:
                join_pieces(pieces, k - 1, shard, piece, base, out)

        if w_ref is None:
            pl.when(plane == nz - 1)(lambda: place(0, last_ref))
        else:
            pl.when(plane < nz - 1)(lambda: place(plane * 2 * shard, w_ref))


def keys_kernel(nz, ids, x_ref, *refs):
    shards, pieces, (w_ref, kv_ref, key_ref) = refs[:2], refs[2:-3], refs[-3:]
    join_planes(nz, shards, pieces, None, w_ref)
    project_keys(ids, x_ref, w_ref, NNZ * BLK - w_ref.shape[0], kv_ref, key_ref)


def queries_kernel(nz, ids, x_ref, last_ref, *refs):
    shards, pieces, (w_ref, q_ref, qhat_ref) = refs[:2], refs[2:-3], refs[-3:]
    join_planes(nz, shards, pieces, w_ref, None)
    w_ref[NNZ * BLK - last_ref.shape[0] :, :] = last_ref[...]
    project_queries(ids, x_ref, w_ref, q_ref, qhat_ref)


def project_kernel(ids, x_ref, w_ref, q_ref, qhat_ref, kv_ref, key_ref):
    project_keys(ids, x_ref, w_ref, 0, kv_ref, key_ref)
    project_queries(ids, x_ref, w_ref, q_ref, qhat_ref)


def attend_kernel(nz, keys, spans, q_ref, qhat, up, *refs):
    pieces = refs[: 2 * nz]
    dq_ref = refs[2 * nz]
    keep = refs[2 * nz + 1 : 3 * nz + 1]
    send = refs[3 * nz + 1 : 4 * nz + 1]
    kv, expo, dprob, acc, dq_t = refs[4 * nz + 1 :]
    half = NQ * SPAN
    me = lax.axis_index("ctx")
    zi, core = me // 2, me % 2
    for k in range(nz):
        z_from = lax.rem(zi + nz - k, nz)
        for other in range(2):
            source = z_from * 2 + (core if other == 0 else 1 - core)
            for p in range(2):
                kv[rows_at(spans[source, p] * SPAN, SPAN, SPAN), :] = pieces[2 * k + other][
                    p * SPAN : (p + 1) * SPAN, :
                ]
    length = kv.shape[0]
    key_row = lax.broadcasted_iota(jnp.int32, (keys, half), 0)
    query_at = lax.broadcasted_iota(jnp.int32, (keys, half), 1) % SPAN
    for p in (1, 0):
        reach = length if p == 1 else length // 2
        sure = length // 2 if p == 1 else 0
        q_part = qhat[p * half : (p + 1) * half, :]
        up_part = up[p * half : (p + 1) * half, :]
        limit = query_at + spans[me, p] * SPAN
        total = jnp.zeros((8, half), F32)
        weighted = jnp.zeros((8, half), F32)
        for at in range(0, reach, keys):
            rows = slice(at, at + keys)
            e = jnp.exp2(dot(kv[rows, :HD], q_part, ((1,), (1,))) * (SCALE * LOG2E))
            if at + keys > sure:
                e = jnp.where(key_row + at <= limit, e, 0.0)
            dp = dot(kv[rows, HD:], up_part, ((1,), (1,)))
            expo[rows, :] = e
            dprob[rows, :] = dp
            term = e.astype(BF16).astype(F32) * dp
            total = total + jnp.sum(e.reshape(keys // 8, 8, half), axis=0)
            weighted = weighted + jnp.sum(term.reshape(keys // 8, 8, half), axis=0)
        inverse = 1.0 / jnp.sum(total, axis=0, keepdims=True)
        delta = jnp.sum(weighted, axis=0, keepdims=True) * inverse
        for at in range(0, reach, keys):
            rows = slice(at, at + keys)
            prob = expo[rows, :] * inverse
            dscore = (prob * (dprob[rows, :] - delta) * SCALE).astype(BF16)
            dkey, dvalue = dot(dscore, q_part), dot(prob.astype(BF16), up_part)
            dq_term = dot(kv[rows, :HD].T, dscore)
            if p == 1:
                acc[rows, :HD] = dkey
                acc[rows, HD:] = dvalue
            else:
                acc[rows, :HD] += dkey
                acc[rows, HD:] += dvalue
            if at == 0:
                dq_t[...] = dq_term
            else:
                dq_t[...] += dq_term
        q_rows = q_ref[p * half : (p + 1) * half, :].astype(F32)
        dq = norm_backward(q_rows, inverse_rms(q_rows), dq_t[...].T).astype(BF16)
        for h in range(NQ):
            dq_ref[h, p * SPAN : (p + 1) * SPAN, :] = dq[h * SPAN : (h + 1) * SPAN, :]
    for k in range(nz):
        z_to = lax.rem(zi + k, nz)
        for p in range(2):
            part = slice(p * SPAN, (p + 1) * SPAN)
            for out, owner in ((keep[k], z_to * 2 + core), (send[k], z_to * 2 + 1 - core)):
                rows = rows_at(spans[owner, p] * SPAN, SPAN, SPAN)
                out[part, :] = acc[rows, :].astype(BF16)


def kv_grad_kernel(nz, key_ref, *refs):
    terms, dkv_ref = refs[:nz], refs[nz]
    total = terms[0][...].astype(F32)
    for term in terms[1:]:
        total = total + term[...].astype(F32)
    key = key_ref[...].astype(F32)
    dkv_ref[0, :, :] = norm_backward(key, inverse_rms(key), total[:, :HD]).astype(BF16)
    dkv_ref[1, :, :] = total[:, HD:].astype(BF16)


def terms_kernel(z_first, z_count, shard, piece, ids, xt, xt_other, *refs):
    tok = xt.shape[1]
    grads, work = refs[-2:]
    columns = grads.shape[0]
    first = z_first * 2 * shard // (NBR * BLK)
    ndp = shard // piece
    sources, outs = refs[: -2 - ndp], refs[-2 - ndp : -2]
    for n, ref in enumerate(sources):
        other = n % 2
        for i in range(ref.shape[0]):
            c = i - first if n < 2 else NQ + i - first
            if 0 <= c < columns:
                grads[c, other * tok : (other + 1) * tok, :] = ref[i]
    core, dp = lax.axis_index("ctx") % 2, lax.axis_index("dp")
    count = shard // BLK
    for z in range(z_count):
        for i in range(count):
            b = (2 * (z_first + z) + core) * count + i
            c = b // NBR
            rows = rows_at(ids[c, b % NBR] * BLK, BLK, BLK)
            picked = jnp.concatenate([xt[rows, :], xt_other[rows, :]], axis=1)
            at = (z * count + i) * BLK
            work[at : at + BLK, :] = dot(picked, grads[c - first]).astype(BF16)
    for k in range(ndp):
        for z in range(z_count):
            at = z * shard + lax.bitwise_xor(dp, k) * piece
            outs[k][z * piece : (z + 1) * piece, :] = work[rows_at(at, piece, 16), :]


def all_terms_kernel(ids, xt, dq_ref, dkv_ref, out_ref):
    for c in range(NCB):
        picked = jnp.concatenate(
            [xt[rows_at(ids[c, r] * BLK, BLK, BLK), :] for r in range(NBR)], axis=0
        )
        grad = dq_ref[c] if c < NQ else dkv_ref[c - NQ]
        out_ref[c * NBR * BLK : (c + 1) * NBR * BLK, :] = dot(picked, grad).astype(BF16)


def sum_kernel(ndp, nz, piece, *refs):
    head, tail = refs[:ndp], refs[ndp : 2 * ndp]
    outs, work = refs[2 * ndp : 2 * ndp + nz], refs[2 * ndp + nz]
    for group, first, count in ((head, 0, nz - 1), (tail, nz - 1, 1)):
        total = group[0][...].astype(F32)
        for term in group[1:]:
            total = total + term[...].astype(F32)
        work[first * piece : (first + count) * piece, :] = total.astype(BF16)
    for k in range(nz):
        at = lax.rem(lax.axis_index("ctx") // 2 + k, nz) * piece
        outs[k][...] = work[rows_at(at, piece, 16), :]


def place_kernel(piece, *refs):
    for k, ref in enumerate(refs[:-1]):
        at = lax.bitwise_xor(lax.axis_index("dp"), k) * piece
        refs[-1][rows_at(at, piece, 16), :] = ref[...].astype(F32)


def token_grad_kernel(ids, dq_ref, dkv_ref, w_ref, out_ref, done_ref, work):
    done_ref[...] = jnp.zeros_like(done_ref)
    wide = NBR * BLK
    cover = out_ref.shape[1] // wide
    for c in range(NCB):
        grad = dq_ref[c] if c < NQ else dkv_ref[c - NQ]
        spread = dot(grad, w_ref[c * wide : (c + 1) * wide, :], ((1,), (1,)))
        for r in range(NBR):
            columns = rows_at(ids[c, r] * BLK, BLK, BLK)
            term = spread[:, r * BLK : (r + 1) * BLK]
            if c < cover:
                work[:, columns] = term
            else:
                work[:, columns] += term
    out_ref[...] = work[...].astype(BF16)


def per_device(ndp, tokens, grad_attn, w_packed, ids, spans):
    nctx = lax.axis_size("ctx")
    nz = nctx // 2
    x = tokens[0]
    tok, width = x.shape
    length = spans.shape[0] * 2 * SPAN
    shard = w_packed.shape[0]
    piece = shard // ndp
    cut = (nz - 1) * 2 * shard
    half = NQ * SPAN
    fast = 2 < nz and cut <= NQ * NBR * BLK and shard % BLK == 0
    fast = fast and shard % (16 * ndp) == 0 and 1 < ndp and ndp & (ndp - 1) == 0

    def swap_core(v):
        return lax.ppermute(v, "ctx", [(i, i ^ 1) for i in range(nctx)])

    def shift_z(v, k):
        return lax.ppermute(
            v, "ctx", [(i, ((i // 2 + k) % nz) * 2 + i % 2) for i in range(nctx)]
        )

    def swap_dp(v, k):
        return lax.ppermute(v, "dp", [(i, i ^ k) for i in range(ndp)])

    def add(a, b):
        return (a.astype(F32) + b.astype(F32)).astype(BF16)

    xt, up, ids, spans = call(
        prepare_kernel,
        (ids, spans),
        (x, grad_attn[0]),
        [
            ((width, tok), BF16),
            ((tok * NQ, HD), BF16),
            (ids.shape, jnp.int32),
            (spans.shape, jnp.int32),
        ],
        moved=4 * x.size,
    )

    if fast:
        (mine,) = call(part_kernel, (), (w_packed,), [((piece, BLK), BF16)], moved=4 * piece * BLK)
        from_z = [shift_z(mine, k) for k in range(1, nz)]

        def both_cores(parts):
            return [v for part in parts for v in (part, swap_core(part))]

        shards = both_cores([w_packed])
        (stacked,) = call(
            stack_kernel,
            (),
            from_z,
            [(((nz - 1) * piece, BLK), BF16)],
            wait=(ids, shards[1]),
            moved=4 * nz * piece * BLK,
        )
        xt_other = swap_core(after(xt, stacked))
        pieces = [stacked] + [swap_dp(stacked, k) for k in range(1, ndp)]
        pieces = both_cores(pieces)
        w_last, kv, key = call(
            functools.partial(keys_kernel, nz),
            (ids,),
            (x, *shards, *pieces),
            [((2 * shard, BLK), BF16), ((tok, 2 * HD), BF16), ((tok, HD), BF16)],
            wait=(xt_other,),
            flops=2 * tok * (NCB - NQ) * NBR * BLK * BLK,
            moved=4 * 2**20,
        )
        weights, query, qhat = call(
            functools.partial(queries_kernel, nz),
            (ids,),
            (x, w_last, *shards, *pieces),
            [((NNZ * BLK, BLK), BF16)] + [((tok * NQ, HD), BF16)] * 2,
            flops=2 * tok * NQ * NBR * BLK * BLK,
            moved=8 * 2**20,
        )
    else:
        weights = lax.all_gather(w_packed, "ctx", axis=0, tiled=True)
        query, qhat, kv, key = call(
            project_kernel,
            (ids,),
            (x, weights),
            [((tok * NQ, HD), BF16)] * 2 + [((tok, 2 * HD), BF16), ((tok, HD), BF16)],
            flops=2 * tok * NNZ * BLK * BLK,
            moved=4 * 2**20,
        )

    kv_pieces = []
    for k in range(nz):
        part = kv if k == 0 else shift_z(kv, k)
        kv_pieces += [part, swap_core(after(part, query) if k == nz - 1 else part)]
    outs = call(
        functools.partial(attend_kernel, nz, math.gcd(512, length // 2)),
        (spans,),
        (query, qhat, up, *kv_pieces),
        [((NQ, tok, HD), BF16)] + [((tok, 2 * HD), BF16)] * (2 * nz),
        scratch=[
            pltpu.VMEM((length, 2 * HD), BF16),
            pltpu.VMEM((length, half), F32),
            pltpu.VMEM((length, half), F32),
            pltpu.VMEM((length, 2 * HD), F32),
            pltpu.VMEM((HD, half), F32),
        ],
        flops=10 * tok * NQ * length * HD // 2,
        moved=4 * 2**20,
        exps=tok * NQ * length // 2,
    )
    dq, keep, send = outs[0], outs[1 : nz + 1], outs[nz + 1 :]
    sums = [add(keep[k], swap_core(send[k])) for k in range(nz)]
    kv_terms = [sums[0]] + [shift_z(sums[k], k) for k in range(1, nz)]

    def weight_terms(z_lo, z_count, grads):
        first = z_lo * 2 * shard // (NBR * BLK)
        last = ((z_lo + z_count) * 2 * shard - 1) // (NBR * BLK)
        return call(
            functools.partial(terms_kernel, z_lo, z_count, shard, piece),
            (ids,),
            (xt, xt_other, *grads),
            [((z_count * piece, BLK), BF16)] * ndp,
            scratch=[
                pltpu.VMEM((last - first + 1, 2 * tok, HD), BF16),
                pltpu.VMEM((z_count * shard, BLK), BF16),
            ],
            flops=4 * tok * z_count * shard * BLK,
            moved=4 * 2**20,
        )

    if fast:
        dq_pair = (dq, swap_core(dq))
        head = weight_terms(0, nz - 1, dq_pair)
        head = [head[0]] + [swap_dp(head[k], k) for k in range(1, ndp)]
    (dkv,) = call(
        functools.partial(kv_grad_kernel, nz),
        (),
        (key, *kv_terms),
        [((2, tok, HD), BF16)],
        moved=2**19,
    )
    grad_tokens, done = call(
        token_grad_kernel,
        (ids,),
        (dq, dkv, weights),
        [((tok, width), BF16), ((8, BLK), F32)],
        scratch=[pltpu.VMEM((tok, width), F32)],
        flops=2 * tok * NNZ * BLK * BLK,
        moved=4 * 2**20,
    )
    if fast:
        tail = weight_terms(nz - 1, 1, (*dq_pair, dkv, swap_core(dkv)))
        tail = [tail[0]] + [
            swap_dp(after(tail[k], head[1]) if k == ndp - 1 else tail[k], k) for k in range(1, ndp)
        ]
        by_z = call(
            functools.partial(sum_kernel, ndp, nz, piece),
            (),
            (*head, *tail),
            [((piece, BLK), BF16)] * nz,
            scratch=[pltpu.VMEM((nz * piece, BLK), BF16)],
            wait=(done,),
            moved=2 * 2**20,
        )
        owned = by_z[0].astype(F32)
        for k in range(1, nz):
            owned = owned + shift_z(by_z[k], k).astype(F32)
        owned = owned.astype(BF16)
        (grad_weights,) = call(
            functools.partial(place_kernel, piece),
            (),
            [owned] + [swap_dp(owned, k) for k in range(1, ndp)],
            [((shard, BLK), F32)],
            moved=2**20,
        )
    else:
        (partial_w,) = call(
            all_terms_kernel,
            (ids,),
            (xt, dq, dkv),
            [((NNZ * BLK, BLK), BF16)],
            flops=2 * tok * NNZ * BLK * BLK,
            moved=4 * 2**20,
        )
        received = lax.all_to_all(
            partial_w.reshape(nctx, shard, BLK), "ctx", split_axis=0, concat_axis=0, tiled=True
        )
        grad_weights = lax.psum(jnp.sum(received.astype(F32), axis=0), "dp")

    return (grad_tokens[None], grad_weights)


def solution(mesh):
    in_specs = (P("dp", "ctx", None), P("dp", "ctx", None), P("ctx", None), P(), P())
    out_specs = (P("dp", "ctx", None), P("ctx", None))
    return jax.shard_map(
        functools.partial(per_device, mesh.shape["dp"]),
        mesh=mesh,
        in_specs=in_specs,
        out_specs=out_specs,
        check_vma=False,
    )
```

```python
import functools
import math

import jax
import jax.numpy as jnp
from jax import lax
from jax.experimental import pallas as pl
from jax.experimental.pallas import tpu as pltpu
from jax.sharding import PartitionSpec as P

HD = 128
BLK = 128
QPG = 8
GROUPS = 1
SPAN = 64
NBR = 8
NCB = 10
NNZ = 80
NQ = GROUPS * QPG
EPSILON = 1e-06
SCALE = 1.0 / math.sqrt(HD)
LOG2E = math.log2(math.e)

F32 = jnp.float32
BF16 = jnp.bfloat16
VMEM = pl.BlockSpec(memory_space=pltpu.VMEM)
SMEM = pl.BlockSpec(memory_space=pltpu.SMEM)
ANY = pl.BlockSpec(memory_space=pl.ANY)


def nbytes(shape, dtype):
    return math.prod(shape) * jnp.dtype(dtype).itemsize


def call(kernel, scalars, arrays, outs, scratch=(), wait=(), flops=0, moved=0, exps=0):
    def body(*refs):
        at = len(scalars) + len(arrays)
        kernel(*refs[:at], *refs[at + len(wait) :])

    held = [(v.shape, v.dtype) for v in arrays] + [(s, t) for s, t in outs]
    held += [(v.shape, v.dtype) for v in scratch]
    need = sum(nbytes(s, t) for s, t in held)
    return pl.pallas_call(
        body,
        in_specs=[SMEM] * len(scalars) + [VMEM] * len(arrays) + [ANY] * len(wait),
        out_specs=[SMEM if t == jnp.int32 else VMEM for _, t in outs],
        out_shape=[jax.ShapeDtypeStruct(s, t) for s, t in outs],
        scratch_shapes=list(scratch),
        compiler_params=pltpu.CompilerParams(vmem_limit_bytes=need + need // 4 + 4 * 2**20),
        cost_estimate=pl.CostEstimate(flops=flops, bytes_accessed=moved, transcendentals=exps),
    )(*scalars, *arrays, *wait)


def after(value, *wait):
    return pl.pallas_call(
        lambda *refs: None,
        in_specs=[ANY] * (1 + len(wait)),
        out_specs=ANY,
        out_shape=jax.ShapeDtypeStruct(value.shape, value.dtype),
        input_output_aliases={0: 0},
        compiler_params=pltpu.CompilerParams(vmem_limit_bytes=2**20),
    )(value, *wait)


def dot(a, b, contract=((1,), (0,))):
    return lax.dot_general(a, b, (contract, ((), ())), preferred_element_type=F32)


def rows_at(start, size, step):
    return pl.ds(pl.multiple_of(start, step), size)


def plane_at(k):
    return lax.bitwise_xor(lax.axis_index("ctx") // 2, k)


def inverse_rms(values):
    return lax.rsqrt(jnp.mean(values * values, axis=-1, keepdims=True) + EPSILON)


def norm_backward(values, factor, upstream):
    return factor * upstream - values * (factor * factor * factor) * jnp.mean(
        upstream * values, axis=-1, keepdims=True
    )


def head_rows(p, c):
    return slice((p * NQ + c) * SPAN, (p * NQ + c + 1) * SPAN)


def prepare_kernel(ids, spans, x_ref, up_ref, xt_ref, up_out, ids_out, spans_out):
    for p in range(2):
        for h in range(NQ):
            up_out[head_rows(p, h), :] = up_ref[p * SPAN : (p + 1) * SPAN, h * HD : (h + 1) * HD]
    for b in range(x_ref.shape[1] // BLK):
        xt_ref[b * BLK : (b + 1) * BLK, :] = x_ref[:, b * BLK : (b + 1) * BLK].T
    for source, out in ((ids, ids_out), (spans, spans_out)):

        @pl.loop(0, source.shape[1])
        def _(j):
            for i in range(source.shape[0]):
                out[i, j] = source[i, j]


def part_kernel(w_ref, out):
    rows = out.shape[0]
    out[...] = w_ref[rows_at(lax.axis_index("dp") * rows, rows, 16), :]


def first_step(nz):
    step = plane_at(nz - 1)
    return jnp.where(step == 0, nz - 1, step)


def first_kernel(*refs):
    pieces, out = refs[:-1], refs[-1]
    for k, ref in enumerate(pieces):

        @pl.when(first_step(len(pieces) + 1) == k + 1)
        def _():
            out[...] = ref[...]


def others_kernel(*refs):
    pieces, out = refs[:-1], refs[-1]
    rows = pieces[0].shape[0]
    first = first_step(len(pieces) + 1)
    for k, ref in enumerate(pieces):
        for slot in (k - 1, k):
            if 0 <= slot < len(pieces) - 1:

                @pl.when(first < k + 1 if slot < k else first > k + 1)
                def _():
                    out[slot * rows : (slot + 1) * rows, :] = ref[...]


def stack_kernel(*refs):
    rows = refs[0].shape[0]
    for k, ref in enumerate(refs[:-1]):
        refs[-1][k * rows : (k + 1) * rows, :] = ref[...]


def join_shards(shards, base, w_ref):
    core = lax.axis_index("ctx") % 2
    shard = shards[0].shape[0]
    for n, ref in enumerate(shards):
        at = base + (core if n == 0 else 1 - core) * shard
        w_ref[rows_at(at, shard, 128), :] = ref[...]


def join_pieces(pieces, slot, shard, piece, base, w_ref):
    core, dp = lax.axis_index("ctx") % 2, lax.axis_index("dp")
    for n, ref in enumerate(pieces):
        at = base + (core if n % 2 == 0 else 1 - core) * shard + (dp ^ (n // 2)) * piece
        w_ref[rows_at(at, piece, 16), :] = ref[slot * piece : (slot + 1) * piece, :]


def column_of(c, ids, x_ref):
    return jnp.concatenate(
        [x_ref[:, rows_at(ids[r, c] * BLK, BLK, BLK)] for r in range(NBR)], axis=1
    )


def project_keys(ids, x_ref, w_ref, first, kv_ref, key_ref):
    wide = NBR * BLK
    for c in range(NQ, NCB):
        at = c * wide - first
        out = dot(column_of(c, ids, x_ref), w_ref[at : at + wide, :]).astype(BF16)
        if c == NQ:
            key = out.astype(F32)
            key_ref[...] = out
            kv_ref[:, :HD] = (key * inverse_rms(key)).astype(BF16)
        else:
            kv_ref[:, HD:] = out


def project_queries(ids, x_ref, w_ref, q_ref, qhat_ref):
    wide = NBR * BLK
    for c in range(NQ):
        out = dot(column_of(c, ids, x_ref), w_ref[c * wide : (c + 1) * wide, :]).astype(BF16)
        query = out.astype(F32)
        normed = (query * inverse_rms(query)).astype(BF16)
        for p in range(2):
            q_ref[head_rows(p, c), :] = out[p * SPAN : (p + 1) * SPAN, :]
            qhat_ref[head_rows(p, c), :] = normed[p * SPAN : (p + 1) * SPAN, :]


def keys_kernel(nz, ids, x_ref, *refs):
    shards, pieces, (w_ref, kv_ref, key_ref) = refs[:2], refs[2:-3], refs[-3:]
    shard, piece = shards[0].shape[0], pieces[0].shape[0]
    last = lax.axis_index("ctx") // 2 == nz - 1
    pl.when(last)(lambda: join_shards(shards, 0, w_ref))
    pl.when(jnp.logical_not(last))(lambda: join_pieces(pieces, 0, shard, piece, 0, w_ref))
    project_keys(ids, x_ref, w_ref, NNZ * BLK - w_ref.shape[0], kv_ref, key_ref)


def queries_kernel(nz, ids, x_ref, last_ref, *refs):
    shards, firsts, others, (w_ref, q_ref, qhat_ref) = refs[:2], refs[2:-5], refs[-5:-3], refs[-3:]
    shard, piece = shards[0].shape[0], firsts[0].shape[0]
    zi, core = lax.axis_index("ctx") // 2, lax.axis_index("ctx") % 2
    last = zi == nz - 1
    pl.when(last)(lambda: join_pieces(firsts, 0, shard, piece, 0, w_ref))
    pl.when(jnp.logical_not(last))(lambda: join_shards(shards, zi * 2 * shard, w_ref))
    for slot in range(nz - 2):
        step = slot + 1 + (slot + 1 >= first_step(nz)).astype(jnp.int32)
        base = plane_at(step) * 2 * shard
        for k in range(len(firsts) // 2):
            for n, ref in enumerate(others):
                at = base + (core if n == 0 else 1 - core) * shard
                at += lax.bitwise_xor(lax.axis_index("dp"), k) * piece
                row = (k * (nz - 2) + slot) * piece
                w_ref[rows_at(at, piece, 16), :] = ref[row : row + piece, :]
    w_ref[NNZ * BLK - last_ref.shape[0] :, :] = last_ref[...]
    project_queries(ids, x_ref, w_ref, q_ref, qhat_ref)


def project_kernel(ids, x_ref, w_ref, q_ref, qhat_ref, kv_ref, key_ref):
    project_keys(ids, x_ref, w_ref, 0, kv_ref, key_ref)
    project_queries(ids, x_ref, w_ref, q_ref, qhat_ref)


def attend_kernel(nz, keys, spans, q_ref, qhat, up, *refs):
    pieces = refs[: 2 * nz]
    dq_ref = refs[2 * nz]
    keep = refs[2 * nz + 1 : 3 * nz + 1]
    send = refs[3 * nz + 1 : 4 * nz + 1]
    kv, expo, dprob, acc, dq_t = refs[4 * nz + 1 :]
    half = NQ * SPAN
    me = lax.axis_index("ctx")
    zi, core = me // 2, me % 2
    for k in range(nz):
        z_from = plane_at(k)
        for other in range(2):
            source = z_from * 2 + (core if other == 0 else 1 - core)
            for p in range(2):
                kv[rows_at(spans[p, source] * SPAN, SPAN, SPAN), :] = pieces[2 * k + other][
                    p * SPAN : (p + 1) * SPAN, :
                ]
    length = kv.shape[0]
    key_row = lax.broadcasted_iota(jnp.int32, (keys, half), 0)
    query_at = lax.broadcasted_iota(jnp.int32, (keys, half), 1) % SPAN
    for p in (1, 0):
        reach = length if p == 1 else length // 2
        sure = length // 2 if p == 1 else 0
        q_part = qhat[p * half : (p + 1) * half, :]
        up_part = up[p * half : (p + 1) * half, :]
        limit = query_at + spans[p, me] * SPAN
        total = jnp.zeros((8, half), F32)
        weighted = jnp.zeros((8, half), F32)
        for at in range(0, reach, keys):
            rows = slice(at, at + keys)
            e = jnp.exp2(dot(kv[rows, :HD], q_part, ((1,), (1,))) * (SCALE * LOG2E))
            if at + keys > sure:
                e = jnp.where(key_row + at <= limit, e, 0.0)
            dp = dot(kv[rows, HD:], up_part, ((1,), (1,)))
            expo[rows, :] = e
            dprob[rows, :] = dp
            term = e.astype(BF16).astype(F32) * dp
            total = total + jnp.sum(e.reshape(keys // 8, 8, half), axis=0)
            weighted = weighted + jnp.sum(term.reshape(keys // 8, 8, half), axis=0)
        inverse = 1.0 / jnp.sum(total, axis=0, keepdims=True)
        delta = jnp.sum(weighted, axis=0, keepdims=True) * inverse
        for at in range(0, reach, keys):
            rows = slice(at, at + keys)
            prob = expo[rows, :] * inverse
            dscore = (prob * (dprob[rows, :] - delta) * SCALE).astype(BF16)
            dkey, dvalue = dot(dscore, q_part), dot(prob.astype(BF16), up_part)
            dq_term = dot(kv[rows, :HD].T, dscore)
            if p == 1:
                acc[rows, :HD] = dkey
                acc[rows, HD:] = dvalue
            else:
                acc[rows, :HD] += dkey
                acc[rows, HD:] += dvalue
            if at == 0:
                dq_t[...] = dq_term
            else:
                dq_t[...] += dq_term
        q_rows = q_ref[p * half : (p + 1) * half, :].astype(F32)
        dq = norm_backward(q_rows, inverse_rms(q_rows), dq_t[...].T).astype(BF16)
        for h in range(NQ):
            dq_ref[h, p * SPAN : (p + 1) * SPAN, :] = dq[h * SPAN : (h + 1) * SPAN, :]
    for k in range(nz):
        z_to = plane_at(k)
        for p in range(2):
            part = slice(p * SPAN, (p + 1) * SPAN)
            for out, owner in ((keep[k], z_to * 2 + core), (send[k], z_to * 2 + 1 - core)):
                rows = rows_at(spans[p, owner] * SPAN, SPAN, SPAN)
                out[part, :] = acc[rows, :].astype(BF16)


def kv_grad_kernel(nz, key_ref, *refs):
    terms, dkv_ref = refs[:nz], refs[nz]
    total = terms[0][...].astype(F32)
    for term in terms[1:]:
        total = total + term[...].astype(F32)
    key = key_ref[...].astype(F32)
    dkv_ref[0, :, :] = norm_backward(key, inverse_rms(key), total[:, :HD]).astype(BF16)
    dkv_ref[1, :, :] = total[:, HD:].astype(BF16)


def terms_kernel(z_first, z_count, shard, piece, ids, xt, xt_other, *refs):
    tok = xt.shape[1]
    grads, work = refs[-2:]
    columns = grads.shape[0]
    first = z_first * 2 * shard // (NBR * BLK)
    ndp = shard // piece
    sources, outs = refs[: -2 - ndp], refs[-2 - ndp : -2]
    for n, ref in enumerate(sources):
        other = n % 2
        for i in range(ref.shape[0]):
            c = i - first if n < 2 else NQ + i - first
            if 0 <= c < columns:
                grads[c, other * tok : (other + 1) * tok, :] = ref[i]
    core, dp = lax.axis_index("ctx") % 2, lax.axis_index("dp")
    count = shard // BLK
    for z in range(z_count):
        for i in range(count):
            b = (2 * (z_first + z) + core) * count + i
            c = b // NBR
            rows = rows_at(ids[b % NBR, c] * BLK, BLK, BLK)
            picked = jnp.concatenate([xt[rows, :], xt_other[rows, :]], axis=1)
            at = (z * count + i) * BLK
            work[at : at + BLK, :] = dot(picked, grads[c - first]).astype(BF16)
    for k in range(ndp):
        for z in range(z_count):
            at = z * shard + lax.bitwise_xor(dp, k) * piece
            outs[k][z * piece : (z + 1) * piece, :] = work[rows_at(at, piece, 16), :]


def all_terms_kernel(ids, xt, dq_ref, dkv_ref, out_ref):
    for c in range(NCB):
        picked = jnp.concatenate(
            [xt[rows_at(ids[r, c] * BLK, BLK, BLK), :] for r in range(NBR)], axis=0
        )
        grad = dq_ref[c] if c < NQ else dkv_ref[c - NQ]
        out_ref[c * NBR * BLK : (c + 1) * NBR * BLK, :] = dot(picked, grad).astype(BF16)


def sum_kernel(ndp, nz, piece, *refs):
    head, tail = refs[:ndp], refs[ndp : 2 * ndp]
    outs, work = refs[2 * ndp : 2 * ndp + nz], refs[2 * ndp + nz]
    for group, first, count in ((head, 0, nz - 1), (tail, nz - 1, 1)):
        total = group[0][...].astype(F32)
        for term in group[1:]:
            total = total + term[...].astype(F32)
        work[first * piece : (first + count) * piece, :] = total.astype(BF16)
    for k in range(nz):
        at = plane_at(k) * piece
        outs[k][...] = work[rows_at(at, piece, 16), :]


def place_kernel(piece, *refs):
    for k, ref in enumerate(refs[:-1]):
        at = lax.bitwise_xor(lax.axis_index("dp"), k) * piece
        refs[-1][rows_at(at, piece, 16), :] = ref[...].astype(F32)


def token_grad_kernel(ids, dq_ref, dkv_ref, w_ref, out_ref, done_ref, work):
    done_ref[...] = jnp.zeros_like(done_ref)
    wide = NBR * BLK
    cover = out_ref.shape[1] // wide
    for c in range(NCB):
        grad = dq_ref[c] if c < NQ else dkv_ref[c - NQ]
        spread = dot(grad, w_ref[c * wide : (c + 1) * wide, :], ((1,), (1,)))
        for r in range(NBR):
            columns = rows_at(ids[r, c] * BLK, BLK, BLK)
            term = spread[:, r * BLK : (r + 1) * BLK]
            if c < cover:
                work[:, columns] = term
            else:
                work[:, columns] += term
    out_ref[...] = work[...].astype(BF16)


def per_device(ndp, tokens, grad_attn, w_packed, block_rows, span_pairs):
    ids, spans = block_rows.T, span_pairs.T
    nctx = lax.axis_size("ctx")
    nz = nctx // 2
    x = tokens[0]
    tok, width = x.shape
    length = spans.shape[1] * 2 * SPAN
    shard = w_packed.shape[0]
    piece = shard // ndp
    cut = (nz - 1) * 2 * shard
    half = NQ * SPAN
    fast = 2 < nz and cut <= NQ * NBR * BLK and shard % BLK == 0
    fast = fast and shard % (16 * ndp) == 0 and 1 < ndp and ndp & (ndp - 1) == 0

    def swap_core(v):
        return lax.ppermute(v, "ctx", [(i, i ^ 1) for i in range(nctx)])

    def both_cores(parts):
        return [v for part in parts for v in (part, swap_core(part))]

    def swap_z(v, k):
        return lax.ppermute(v, "ctx", [(i, i ^ (2 * k)) for i in range(nctx)])

    def swap_dp(v, k):
        return lax.ppermute(v, "dp", [(i, i ^ k) for i in range(ndp)])

    def add(a, b):
        return (a.astype(F32) + b.astype(F32)).astype(BF16)

    xt, up, ids, spans = call(
        prepare_kernel,
        (ids, spans),
        (x, grad_attn[0]),
        [
            ((width, tok), BF16),
            ((tok * NQ, HD), BF16),
            (ids.shape, jnp.int32),
            (spans.shape, jnp.int32),
        ],
        moved=4 * x.size,
    )

    if fast:
        (mine,) = call(part_kernel, (), (w_packed,), [((piece, BLK), BF16)], moved=4 * piece * BLK)
        from_z = [swap_z(mine, k) for k in range(1, nz)]

        def pick(kernel, count, wait):
            return call(
                kernel,
                (),
                from_z,
                [((count * piece, BLK), BF16)],
                wait=wait,
                moved=4 * nz * piece * BLK,
            )[0]

        def to_all_dp(held):
            return [held] + [swap_dp(held, k) for k in range(1, ndp)]

        shards = both_cores([w_packed])
        first = pick(first_kernel, 1, (ids, shards[1]))
        firsts = to_all_dp(first)
        others = to_all_dp(pick(others_kernel, nz - 2, (first,)))
        firsts = both_cores(firsts)
        w_last, kv, key = call(
            functools.partial(keys_kernel, nz),
            (ids,),
            (x, *shards, *firsts),
            [((2 * shard, BLK), BF16), ((tok, 2 * HD), BF16), ((tok, HD), BF16)],
            flops=2 * tok * (NCB - NQ) * NBR * BLK * BLK,
            moved=3 * 2**20,
        )
        kv_from_z = [swap_z(kv, k) for k in range(1, nz)]
        kv_pieces = both_cores([kv] + kv_from_z)
        (stacked,) = call(
            stack_kernel,
            (),
            others,
            [((ndp * (nz - 2) * piece, BLK), BF16)],
            wait=kv_from_z,
            moved=4 * nz * shard * BLK,
        )
        weights, query, qhat = call(
            functools.partial(queries_kernel, nz),
            (ids,),
            (x, w_last, *shards, *firsts, stacked, swap_core(stacked)),
            [((NNZ * BLK, BLK), BF16)] + [((tok * NQ, HD), BF16)] * 2,
            wait=kv_pieces,
            flops=2 * tok * NQ * NBR * BLK * BLK,
            moved=8 * 2**20,
        )
        xt_other = swap_core(after(xt, qhat))
    else:
        weights = lax.all_gather(w_packed, "ctx", axis=0, tiled=True)
        query, qhat, kv, key = call(
            project_kernel,
            (ids,),
            (x, weights),
            [((tok * NQ, HD), BF16)] * 2 + [((tok, 2 * HD), BF16), ((tok, HD), BF16)],
            flops=2 * tok * NNZ * BLK * BLK,
            moved=4 * 2**20,
        )

        kv_pieces = both_cores([kv] + [swap_z(kv, k) for k in range(1, nz)])

    outs = call(
        functools.partial(attend_kernel, nz, math.gcd(512, length // 2)),
        (spans,),
        (query, qhat, up, *kv_pieces),
        [((NQ, tok, HD), BF16)] + [((tok, 2 * HD), BF16)] * (2 * nz),
        scratch=[
            pltpu.VMEM((length, 2 * HD), BF16),
            pltpu.VMEM((length, half), F32),
            pltpu.VMEM((length, half), F32),
            pltpu.VMEM((length, 2 * HD), F32),
            pltpu.VMEM((HD, half), F32),
        ],
        flops=10 * tok * NQ * length * HD // 2,
        moved=4 * 2**20,
        exps=tok * NQ * length // 2,
    )
    dq, keep, send = outs[0], outs[1 : nz + 1], outs[nz + 1 :]
    sums = [add(keep[k], swap_core(send[k])) for k in range(nz)]
    kv_terms = [sums[0]] + [swap_z(sums[k], k) for k in range(1, nz)]

    def weight_terms(z_lo, z_count, grads):
        first = z_lo * 2 * shard // (NBR * BLK)
        last = ((z_lo + z_count) * 2 * shard - 1) // (NBR * BLK)
        return call(
            functools.partial(terms_kernel, z_lo, z_count, shard, piece),
            (ids,),
            (xt, xt_other, *grads),
            [((z_count * piece, BLK), BF16)] * ndp,
            scratch=[
                pltpu.VMEM((last - first + 1, 2 * tok, HD), BF16),
                pltpu.VMEM((z_count * shard, BLK), BF16),
            ],
            flops=4 * tok * z_count * shard * BLK,
            moved=4 * 2**20,
        )

    if fast:
        dq_pair = (dq, swap_core(dq))
        head = weight_terms(0, nz - 1, dq_pair)
        head = [head[0]] + [swap_dp(head[k], k) for k in range(1, ndp)]
    (dkv,) = call(
        functools.partial(kv_grad_kernel, nz),
        (),
        (key, *kv_terms),
        [((2, tok, HD), BF16)],
        moved=2**19,
    )
    grad_tokens, done = call(
        token_grad_kernel,
        (ids,),
        (dq, dkv, weights),
        [((tok, width), BF16), ((8, BLK), F32)],
        scratch=[pltpu.VMEM((tok, width), F32)],
        flops=2 * tok * NNZ * BLK * BLK,
        moved=4 * 2**20,
    )
    if fast:
        tail = weight_terms(nz - 1, 1, (*dq_pair, dkv, swap_core(dkv)))
        tail = [tail[0]] + [
            swap_dp(after(tail[k], head[1]) if k == ndp - 1 else tail[k], k) for k in range(1, ndp)
        ]
        by_z = call(
            functools.partial(sum_kernel, ndp, nz, piece),
            (),
            (*head, *tail),
            [((piece, BLK), BF16)] * nz,
            scratch=[pltpu.VMEM((nz * piece, BLK), BF16)],
            wait=(done,),
            moved=2 * 2**20,
        )
        owned = by_z[0].astype(F32)
        for k in range(1, nz):
            owned = owned + swap_z(by_z[k], k).astype(F32)
        owned = owned.astype(BF16)
        (grad_weights,) = call(
            functools.partial(place_kernel, piece),
            (),
            [owned] + [swap_dp(owned, k) for k in range(1, ndp)],
            [((shard, BLK), F32)],
            moved=2**20,
        )
    else:
        (partial_w,) = call(
            all_terms_kernel,
            (ids,),
            (xt, dq, dkv),
            [((NNZ * BLK, BLK), BF16)],
            flops=2 * tok * NNZ * BLK * BLK,
            moved=4 * 2**20,
        )
        received = lax.all_to_all(
            partial_w.reshape(nctx, shard, BLK), "ctx", split_axis=0, concat_axis=0, tiled=True
        )
        grad_weights = lax.psum(jnp.sum(received.astype(F32), axis=0), "dp")

    return (grad_tokens[None], grad_weights)


def solution(mesh):
    in_specs = (P("dp", "ctx", None), P("dp", "ctx", None), P("ctx", None), P(), P())
    out_specs = (P("dp", "ctx", None), P("ctx", None))
    return jax.shard_map(
        functools.partial(per_device, mesh.shape["dp"]),
        mesh=mesh,
        in_specs=in_specs,
        out_specs=out_specs,
        check_vma=False,
    )
```

```python
import functools
import math

import jax
import jax.numpy as jnp
from jax import lax
from jax.experimental import pallas as pl
from jax.experimental.pallas import tpu as pltpu
from jax.sharding import PartitionSpec as P

HD = 128
BLK = 128
QPG = 8
GROUPS = 1
SPAN = 64
NBR = 8
NCB = 10
NNZ = 80
NQ = GROUPS * QPG
EPSILON = 1e-06
SCALE = 1.0 / math.sqrt(HD)
LOG2E = math.log2(math.e)

F32 = jnp.float32
BF16 = jnp.bfloat16
VMEM = pl.BlockSpec(memory_space=pltpu.VMEM)
SMEM = pl.BlockSpec(memory_space=pltpu.SMEM)
ANY = pl.BlockSpec(memory_space=pl.ANY)


def nbytes(shape, dtype):
    return math.prod(shape) * jnp.dtype(dtype).itemsize


def call(kernel, scalars, arrays, outs, scratch=(), wait=(), flops=0, moved=0, exps=0):
    def body(*refs):
        at = len(scalars) + len(arrays)
        kernel(*refs[:at], *refs[at + len(wait) :])

    held = [(v.shape, v.dtype) for v in arrays] + [(s, t) for s, t in outs]
    held += [(v.shape, v.dtype) for v in scratch]
    need = sum(nbytes(s, t) for s, t in held)
    return pl.pallas_call(
        body,
        in_specs=[SMEM] * len(scalars) + [VMEM] * len(arrays) + [ANY] * len(wait),
        out_specs=[SMEM if t == jnp.int32 else VMEM for _, t in outs],
        out_shape=[jax.ShapeDtypeStruct(s, t) for s, t in outs],
        scratch_shapes=list(scratch),
        compiler_params=pltpu.CompilerParams(vmem_limit_bytes=need + need // 4 + 4 * 2**20),
        cost_estimate=pl.CostEstimate(flops=flops, bytes_accessed=moved, transcendentals=exps),
    )(*scalars, *arrays, *wait)


def after(value, *wait):
    return pl.pallas_call(
        lambda *refs: None,
        in_specs=[ANY] * (1 + len(wait)),
        out_specs=ANY,
        out_shape=jax.ShapeDtypeStruct(value.shape, value.dtype),
        input_output_aliases={0: 0},
        compiler_params=pltpu.CompilerParams(vmem_limit_bytes=2**20),
    )(value, *wait)


def dot(a, b, contract=((1,), (0,))):
    return lax.dot_general(a, b, (contract, ((), ())), preferred_element_type=F32)


def rows_at(start, size, step):
    return pl.ds(pl.multiple_of(start, step), size)


def plane_at(k):
    return lax.bitwise_xor(lax.axis_index("ctx") // 2, k)


def inverse_rms(values):
    return lax.rsqrt(jnp.mean(values * values, axis=-1, keepdims=True) + EPSILON)


def norm_backward(values, factor, upstream):
    return factor * upstream - values * (factor * factor * factor) * jnp.mean(
        upstream * values, axis=-1, keepdims=True
    )


def head_rows(p, c):
    return slice((p * NQ + c) * SPAN, (p * NQ + c + 1) * SPAN)


def prepare_kernel(ids, spans, x_ref, up_ref, xt_ref, up_out, ids_out, spans_out):
    for p in range(2):
        for h in range(NQ):
            up_out[head_rows(p, h), :] = up_ref[p * SPAN : (p + 1) * SPAN, h * HD : (h + 1) * HD]
    for b in range(x_ref.shape[1] // BLK):
        xt_ref[b * BLK : (b + 1) * BLK, :] = x_ref[:, b * BLK : (b + 1) * BLK].T
    for source, out in ((ids, ids_out), (spans, spans_out)):

        @pl.loop(0, source.shape[1])
        def _(j):
            for i in range(source.shape[0]):
                out[i, j] = source[i, j]


def part_kernel(w_ref, out):
    rows = out.shape[0]
    out[...] = w_ref[rows_at(lax.axis_index("dp") * rows, rows, 16), :]


def first_step(nz):
    step = plane_at(nz - 1)
    return jnp.where(step == 0, nz - 1, step)


def first_kernel(*refs):
    pieces, out = refs[:-1], refs[-1]
    for k, ref in enumerate(pieces):

        @pl.when(first_step(len(pieces) + 1) == k + 1)
        def _():
            out[...] = ref[...]


def others_kernel(*refs):
    pieces, out = refs[:-1], refs[-1]
    rows = pieces[0].shape[0]
    first = first_step(len(pieces) + 1)
    for k, ref in enumerate(pieces):
        for slot in (k - 1, k):
            if 0 <= slot < len(pieces) - 1:

                @pl.when(first < k + 1 if slot < k else first > k + 1)
                def _():
                    out[slot * rows : (slot + 1) * rows, :] = ref[...]


def stack_kernel(*refs):
    rows = refs[0].shape[0]
    for k, ref in enumerate(refs[:-1]):
        refs[-1][k * rows : (k + 1) * rows, :] = ref[...]


def join_shards(shards, base, w_ref):
    core = lax.axis_index("ctx") % 2
    shard = shards[0].shape[0]
    for n, ref in enumerate(shards):
        at = base + (core if n == 0 else 1 - core) * shard
        w_ref[rows_at(at, shard, 128), :] = ref[...]


def join_pieces(pieces, slot, shard, piece, base, w_ref):
    core, dp = lax.axis_index("ctx") % 2, lax.axis_index("dp")
    for n, ref in enumerate(pieces):
        at = base + (core if n % 2 == 0 else 1 - core) * shard + (dp ^ (n // 2)) * piece
        w_ref[rows_at(at, piece, 16), :] = ref[slot * piece : (slot + 1) * piece, :]


def column_of(c, ids, x_ref):
    return jnp.concatenate(
        [x_ref[:, rows_at(ids[r, c] * BLK, BLK, BLK)] for r in range(NBR)], axis=1
    )


def project_keys(ids, x_ref, w_ref, first, kv_ref, key_ref):
    wide = NBR * BLK
    for c in range(NQ, NCB):
        at = c * wide - first
        out = dot(column_of(c, ids, x_ref), w_ref[at : at + wide, :]).astype(BF16)
        if c == NQ:
            key = out.astype(F32)
            key_ref[...] = out
            kv_ref[:, :HD] = (key * inverse_rms(key)).astype(BF16)
        else:
            kv_ref[:, HD:] = out


def project_queries(ids, x_ref, w_ref, q_ref, qhat_ref):
    wide = NBR * BLK
    for c in range(NQ):
        out = dot(column_of(c, ids, x_ref), w_ref[c * wide : (c + 1) * wide, :]).astype(BF16)
        query = out.astype(F32)
        normed = (query * inverse_rms(query)).astype(BF16)
        for p in range(2):
            q_ref[head_rows(p, c), :] = out[p * SPAN : (p + 1) * SPAN, :]
            qhat_ref[head_rows(p, c), :] = normed[p * SPAN : (p + 1) * SPAN, :]


def keys_kernel(nz, ids, x_ref, *refs):
    shards, pieces, (w_ref, kv_ref, key_ref) = refs[:2], refs[2:-3], refs[-3:]
    shard, piece = shards[0].shape[0], pieces[0].shape[0]
    last = lax.axis_index("ctx") // 2 == nz - 1
    pl.when(last)(lambda: join_shards(shards, 0, w_ref))
    pl.when(jnp.logical_not(last))(lambda: join_pieces(pieces, 0, shard, piece, 0, w_ref))
    project_keys(ids, x_ref, w_ref, NNZ * BLK - w_ref.shape[0], kv_ref, key_ref)


def queries_kernel(nz, ids, x_ref, last_ref, *refs):
    shards, firsts, others, (w_ref, q_ref, qhat_ref) = refs[:2], refs[2:-5], refs[-5:-3], refs[-3:]
    shard, piece = shards[0].shape[0], firsts[0].shape[0]
    zi, core = lax.axis_index("ctx") // 2, lax.axis_index("ctx") % 2
    last = zi == nz - 1
    pl.when(last)(lambda: join_pieces(firsts, 0, shard, piece, 0, w_ref))
    pl.when(jnp.logical_not(last))(lambda: join_shards(shards, zi * 2 * shard, w_ref))
    for slot in range(nz - 2):
        step = slot + 1 + (slot + 1 >= first_step(nz)).astype(jnp.int32)
        base = plane_at(step) * 2 * shard
        for k in range(len(firsts) // 2):
            for n, ref in enumerate(others):
                at = base + (core if n == 0 else 1 - core) * shard
                at += lax.bitwise_xor(lax.axis_index("dp"), k) * piece
                row = (k * (nz - 2) + slot) * piece
                w_ref[rows_at(at, piece, 16), :] = ref[row : row + piece, :]
    w_ref[NNZ * BLK - last_ref.shape[0] :, :] = last_ref[...]
    project_queries(ids, x_ref, w_ref, q_ref, qhat_ref)


def project_kernel(ids, x_ref, w_ref, q_ref, qhat_ref, kv_ref, key_ref):
    project_keys(ids, x_ref, w_ref, 0, kv_ref, key_ref)
    project_queries(ids, x_ref, w_ref, q_ref, qhat_ref)


def attend_kernel(nz, keys, spans, q_ref, qhat, up, *refs):
    pieces = refs[: 2 * nz]
    dq_ref = refs[2 * nz]
    keep = refs[2 * nz + 1 : 3 * nz + 1]
    send = refs[3 * nz + 1 : 4 * nz + 1]
    kv, expo, dprob, acc, dq_t = refs[4 * nz + 1 :]
    half = NQ * SPAN
    me = lax.axis_index("ctx")
    zi, core = me // 2, me % 2
    for k in range(nz):
        z_from = plane_at(k)
        for other in range(2):
            source = z_from * 2 + (core if other == 0 else 1 - core)
            for p in range(2):
                kv[rows_at(spans[p, source] * SPAN, SPAN, SPAN), :] = pieces[2 * k + other][
                    p * SPAN : (p + 1) * SPAN, :
                ]
    length = kv.shape[0]
    key_row = lax.broadcasted_iota(jnp.int32, (keys, half), 0)
    query_at = lax.broadcasted_iota(jnp.int32, (keys, half), 1) % SPAN
    for p in (1, 0):
        reach = length if p == 1 else length // 2
        sure = length // 2 if p == 1 else 0
        q_part = qhat[p * half : (p + 1) * half, :]
        up_part = up[p * half : (p + 1) * half, :]
        limit = query_at + spans[p, me] * SPAN
        total = jnp.zeros((8, half), F32)
        weighted = jnp.zeros((8, half), F32)
        for at in range(0, reach, keys):
            rows = slice(at, at + keys)
            e = jnp.exp2(dot(kv[rows, :HD], q_part, ((1,), (1,))) * (SCALE * LOG2E))
            if at + keys > sure:
                e = jnp.where(key_row + at <= limit, e, 0.0)
            dp = dot(kv[rows, HD:], up_part, ((1,), (1,)))
            expo[rows, :] = e
            dprob[rows, :] = dp
            term = e.astype(BF16).astype(F32) * dp
            total = total + jnp.sum(e.reshape(keys // 8, 8, half), axis=0)
            weighted = weighted + jnp.sum(term.reshape(keys // 8, 8, half), axis=0)
        inverse = 1.0 / jnp.sum(total, axis=0, keepdims=True)
        delta = jnp.sum(weighted, axis=0, keepdims=True) * inverse
        for at in range(0, reach, keys):
            rows = slice(at, at + keys)
            prob = expo[rows, :] * inverse
            dscore = (prob * (dprob[rows, :] - delta) * SCALE).astype(BF16)
            dkey, dvalue = dot(dscore, q_part), dot(prob.astype(BF16), up_part)
            dq_term = dot(kv[rows, :HD].T, dscore)
            if p == 1:
                acc[rows, :HD] = dkey
                acc[rows, HD:] = dvalue
            else:
                acc[rows, :HD] += dkey
                acc[rows, HD:] += dvalue
            if at == 0:
                dq_t[...] = dq_term
            else:
                dq_t[...] += dq_term
        q_rows = q_ref[p * half : (p + 1) * half, :].astype(F32)
        dq = norm_backward(q_rows, inverse_rms(q_rows), dq_t[...].T).astype(BF16)
        for h in range(NQ):
            dq_ref[h, p * SPAN : (p + 1) * SPAN, :] = dq[h * SPAN : (h + 1) * SPAN, :]
    for k in range(nz):
        z_to = plane_at(k)
        for p in range(2):
            part = slice(p * SPAN, (p + 1) * SPAN)
            for out, owner in ((keep[k], z_to * 2 + core), (send[k], z_to * 2 + 1 - core)):
                rows = rows_at(spans[p, owner] * SPAN, SPAN, SPAN)
                out[part, :] = acc[rows, :].astype(BF16)


def kv_grad_kernel(nz, key_ref, *refs):
    terms, dkv_ref = refs[:nz], refs[nz]
    total = terms[0][...].astype(F32)
    for term in terms[1:]:
        total = total + term[...].astype(F32)
    key = key_ref[...].astype(F32)
    dkv_ref[0, :, :] = norm_backward(key, inverse_rms(key), total[:, :HD]).astype(BF16)
    dkv_ref[1, :, :] = total[:, HD:].astype(BF16)


def terms_kernel(z_first, z_count, shard, piece, ids, xt, xt_other, *refs):
    tok = xt.shape[1]
    grads, work = refs[-2:]
    columns = grads.shape[0]
    first = z_first * 2 * shard // (NBR * BLK)
    ndp = shard // piece
    sources, outs = refs[: -2 - ndp], refs[-2 - ndp : -2]
    for n, ref in enumerate(sources):
        other = n % 2
        for i in range(ref.shape[0]):
            c = i - first if n < 2 else NQ + i - first
            if 0 <= c < columns:
                grads[c, other * tok : (other + 1) * tok, :] = ref[i]
    core, dp = lax.axis_index("ctx") % 2, lax.axis_index("dp")
    count = shard // BLK
    for z in range(z_count):
        for i in range(count):
            b = (2 * (z_first + z) + core) * count + i
            c = b // NBR
            rows = rows_at(ids[b % NBR, c] * BLK, BLK, BLK)
            picked = jnp.concatenate([xt[rows, :], xt_other[rows, :]], axis=1)
            at = (z * count + i) * BLK
            work[at : at + BLK, :] = dot(picked, grads[c - first]).astype(BF16)
    for k in range(ndp):
        for z in range(z_count):
            at = z * shard + lax.bitwise_xor(dp, k) * piece
            outs[k][z * piece : (z + 1) * piece, :] = work[rows_at(at, piece, 16), :]


def all_terms_kernel(ids, xt, dq_ref, dkv_ref, out_ref):
    for c in range(NCB):
        picked = jnp.concatenate(
            [xt[rows_at(ids[r, c] * BLK, BLK, BLK), :] for r in range(NBR)], axis=0
        )
        grad = dq_ref[c] if c < NQ else dkv_ref[c - NQ]
        out_ref[c * NBR * BLK : (c + 1) * NBR * BLK, :] = dot(picked, grad).astype(BF16)


def sum_kernel(ndp, nz, piece, *refs):
    head, tail = refs[:ndp], refs[ndp : 2 * ndp]
    outs, work = refs[2 * ndp : 2 * ndp + nz], refs[2 * ndp + nz]
    for group, first, count in ((head, 0, nz - 1), (tail, nz - 1, 1)):
        total = group[0][...].astype(F32)
        for term in group[1:]:
            total = total + term[...].astype(F32)
        work[first * piece : (first + count) * piece, :] = total.astype(BF16)
    for k in range(nz):
        at = plane_at(k) * piece
        outs[k][...] = work[rows_at(at, piece, 16), :]


def place_kernel(piece, *refs):
    for k, ref in enumerate(refs[:-1]):
        at = lax.bitwise_xor(lax.axis_index("dp"), k) * piece
        refs[-1][rows_at(at, piece, 16), :] = ref[...].astype(F32)


def token_grad_kernel(ids, dq_ref, dkv_ref, w_ref, out_ref, done_ref, work):
    done_ref[...] = jnp.zeros_like(done_ref)
    wide = NBR * BLK
    cover = out_ref.shape[1] // wide
    for c in range(NCB):
        grad = dq_ref[c] if c < NQ else dkv_ref[c - NQ]
        spread = dot(grad, w_ref[c * wide : (c + 1) * wide, :], ((1,), (1,)))
        for r in range(NBR):
            columns = rows_at(ids[r, c] * BLK, BLK, BLK)
            term = spread[:, r * BLK : (r + 1) * BLK]
            if c < cover:
                work[:, columns] = term
            else:
                work[:, columns] += term
    out_ref[...] = work[...].astype(BF16)


def per_device(ndp, tokens, grad_attn, w_packed, block_rows, span_pairs):
    ids, spans = block_rows.T, span_pairs.T
    nctx = lax.axis_size("ctx")
    nz = nctx // 2
    x = tokens[0]
    tok, width = x.shape
    length = spans.shape[1] * 2 * SPAN
    shard = w_packed.shape[0]
    piece = shard // ndp
    cut = (nz - 1) * 2 * shard
    half = NQ * SPAN
    fast = 2 < nz and cut <= NQ * NBR * BLK and shard % BLK == 0
    fast = fast and shard % (16 * ndp) == 0 and 1 < ndp and ndp & (ndp - 1) == 0

    def swap_core(v):
        return lax.ppermute(v, "ctx", [(i, i ^ 1) for i in range(nctx)])

    def both_cores(parts):
        return [v for part in parts for v in (part, swap_core(part))]

    def swap_z(v, k):
        return lax.ppermute(v, "ctx", [(i, i ^ (2 * k)) for i in range(nctx)])

    def swap_dp(v, k):
        return lax.ppermute(v, "dp", [(i, i ^ k) for i in range(ndp)])

    def add(a, b):
        return (a.astype(F32) + b.astype(F32)).astype(BF16)

    xt, up, ids, spans = call(
        prepare_kernel,
        (ids, spans),
        (x, grad_attn[0]),
        [
            ((width, tok), BF16),
            ((tok * NQ, HD), BF16),
            (ids.shape, jnp.int32),
            (spans.shape, jnp.int32),
        ],
        moved=4 * x.size,
    )

    if fast:
        (mine,) = call(part_kernel, (), (w_packed,), [((piece, BLK), BF16)], moved=4 * piece * BLK)
        from_z = [swap_z(mine, k) for k in range(1, nz)]

        def pick(kernel, count, wait):
            return call(
                kernel,
                (),
                from_z,
                [((count * piece, BLK), BF16)],
                wait=wait,
                moved=4 * nz * piece * BLK,
            )[0]

        def to_all_dp(held):
            return [held] + [swap_dp(held, k) for k in range(1, ndp)]

        shards = both_cores([w_packed])
        first = pick(first_kernel, 1, (ids, shards[1]))
        firsts = to_all_dp(first)
        others = to_all_dp(pick(others_kernel, nz - 2, (first,)))
        firsts = both_cores(firsts)
        w_last, kv, key = call(
            functools.partial(keys_kernel, nz),
            (ids,),
            (x, *shards, *firsts),
            [((2 * shard, BLK), BF16), ((tok, 2 * HD), BF16), ((tok, HD), BF16)],
            flops=2 * tok * (NCB - NQ) * NBR * BLK * BLK,
            moved=3 * 2**20,
        )
        kv_from_z = [swap_z(kv, k) for k in range(1, nz)]
        kv_pieces = both_cores([kv] + kv_from_z)
        (stacked,) = call(
            stack_kernel,
            (),
            others,
            [((ndp * (nz - 2) * piece, BLK), BF16)],
            wait=kv_from_z,
            moved=4 * nz * shard * BLK,
        )
        weights, query, qhat = call(
            functools.partial(queries_kernel, nz),
            (ids,),
            (x, w_last, *shards, *firsts, stacked, swap_core(stacked)),
            [((NNZ * BLK, BLK), BF16)] + [((tok * NQ, HD), BF16)] * 2,
            wait=kv_pieces,
            flops=2 * tok * NQ * NBR * BLK * BLK,
            moved=8 * 2**20,
        )
        xt_other = swap_core(after(xt, qhat))
    else:
        weights = lax.all_gather(w_packed, "ctx", axis=0, tiled=True)
        query, qhat, kv, key = call(
            project_kernel,
            (ids,),
            (x, weights),
            [((tok * NQ, HD), BF16)] * 2 + [((tok, 2 * HD), BF16), ((tok, HD), BF16)],
            flops=2 * tok * NNZ * BLK * BLK,
            moved=4 * 2**20,
        )

        kv_pieces = both_cores([kv] + [swap_z(kv, k) for k in range(1, nz)])

    outs = call(
        functools.partial(attend_kernel, nz, math.gcd(512, length // 2)),
        (spans,),
        (query, qhat, up, *kv_pieces),
        [((NQ, tok, HD), BF16)] + [((tok, 2 * HD), BF16)] * (2 * nz),
        scratch=[
            pltpu.VMEM((length, 2 * HD), BF16),
            pltpu.VMEM((length, half), F32),
            pltpu.VMEM((length, half), F32),
            pltpu.VMEM((length, 2 * HD), F32),
            pltpu.VMEM((HD, half), F32),
        ],
        flops=10 * tok * NQ * length * HD // 2,
        moved=4 * 2**20,
        exps=tok * NQ * length // 2,
    )
    dq, keep, send = outs[0], outs[1 : nz + 1], outs[nz + 1 :]
    sums = [add(keep[k], swap_core(send[k])) for k in range(nz)]

    def weight_terms(z_lo, z_count, grads):
        first = z_lo * 2 * shard // (NBR * BLK)
        last = ((z_lo + z_count) * 2 * shard - 1) // (NBR * BLK)
        return call(
            functools.partial(terms_kernel, z_lo, z_count, shard, piece),
            (ids,),
            (xt, xt_other, *grads),
            [((z_count * piece, BLK), BF16)] * ndp,
            scratch=[
                pltpu.VMEM((last - first + 1, 2 * tok, HD), BF16),
                pltpu.VMEM((z_count * shard, BLK), BF16),
            ],
            flops=4 * tok * z_count * shard * BLK,
            moved=4 * 2**20,
        )

    if fast:
        dq_pair = (dq, swap_core(dq))
        head_raw = weight_terms(0, nz - 1, dq_pair)
        head = [head_raw[0]] + [swap_dp(head_raw[k], k) for k in range(1, ndp)]
    gate = head_raw[:1] if fast else []
    kv_terms = [sums[0], swap_z(after(sums[1], *gate), 1)]
    kv_terms += [swap_z(sums[k], k) for k in range(2, nz)]
    (dkv,) = call(
        functools.partial(kv_grad_kernel, nz),
        (),
        (key, *kv_terms),
        [((2, tok, HD), BF16)],
        moved=2**19,
    )
    grad_tokens, done = call(
        token_grad_kernel,
        (ids,),
        (dq, dkv, weights),
        [((tok, width), BF16), ((8, BLK), F32)],
        scratch=[pltpu.VMEM((tok, width), F32)],
        flops=2 * tok * NNZ * BLK * BLK,
        moved=4 * 2**20,
    )
    if fast:
        tail = weight_terms(nz - 1, 1, (*dq_pair, dkv, swap_core(dkv)))
        tail = [tail[0]] + [
            swap_dp(after(tail[k], head[1]) if k == ndp - 1 else tail[k], k) for k in range(1, ndp)
        ]
        by_z = call(
            functools.partial(sum_kernel, ndp, nz, piece),
            (),
            (*head, *tail),
            [((piece, BLK), BF16)] * nz,
            scratch=[pltpu.VMEM((nz * piece, BLK), BF16)],
            wait=(done,),
            moved=2 * 2**20,
        )
        owned = by_z[0].astype(F32)
        for k in range(1, nz):
            owned = owned + swap_z(by_z[k], k).astype(F32)
        owned = owned.astype(BF16)
        (grad_weights,) = call(
            functools.partial(place_kernel, piece),
            (),
            [owned] + [swap_dp(owned, k) for k in range(1, ndp)],
            [((shard, BLK), F32)],
            moved=2**20,
        )
    else:
        (partial_w,) = call(
            all_terms_kernel,
            (ids,),
            (xt, dq, dkv),
            [((NNZ * BLK, BLK), BF16)],
            flops=2 * tok * NNZ * BLK * BLK,
            moved=4 * 2**20,
        )
        received = lax.all_to_all(
            partial_w.reshape(nctx, shard, BLK), "ctx", split_axis=0, concat_axis=0, tiled=True
        )
        grad_weights = lax.psum(jnp.sum(received.astype(F32), axis=0), "dp")

    return (grad_tokens[None], grad_weights)


def solution(mesh):
    in_specs = (P("dp", "ctx", None), P("dp", "ctx", None), P("ctx", None), P(), P())
    out_specs = (P("dp", "ctx", None), P("ctx", None))
    return jax.shard_map(
        functools.partial(per_device, mesh.shape["dp"]),
        mesh=mesh,
        in_specs=in_specs,
        out_specs=out_specs,
        check_vma=False,
    )
```

```python
import functools
import math

import jax
import jax.numpy as jnp
from jax import lax
from jax.experimental import pallas as pl
from jax.experimental.pallas import tpu as pltpu
from jax.sharding import PartitionSpec as P

HD = 128
BLK = 128
QPG = 8
GROUPS = 1
SPAN = 64
NBR = 8
NCB = 10
NNZ = 80
NQ = GROUPS * QPG
EPSILON = 1e-06
SCALE = 1.0 / math.sqrt(HD)
LOG2E = math.log2(math.e)

F32 = jnp.float32
BF16 = jnp.bfloat16
VMEM = pl.BlockSpec(memory_space=pltpu.VMEM)
SMEM = pl.BlockSpec(memory_space=pltpu.SMEM)
ANY = pl.BlockSpec(memory_space=pl.ANY)


def nbytes(shape, dtype):
    return math.prod(shape) * jnp.dtype(dtype).itemsize


def call(kernel, scalars, arrays, outs, scratch=(), wait=(), flops=0, moved=0, exps=0):
    def body(*refs):
        at = len(scalars) + len(arrays)
        kernel(*refs[:at], *refs[at + len(wait) :])

    held = [(v.shape, v.dtype) for v in arrays] + [(s, t) for s, t in outs]
    held += [(v.shape, v.dtype) for v in scratch]
    need = sum(nbytes(s, t) for s, t in held)
    return pl.pallas_call(
        body,
        in_specs=[SMEM] * len(scalars) + [VMEM] * len(arrays) + [ANY] * len(wait),
        out_specs=[SMEM if t == jnp.int32 else VMEM for _, t in outs],
        out_shape=[jax.ShapeDtypeStruct(s, t) for s, t in outs],
        scratch_shapes=list(scratch),
        compiler_params=pltpu.CompilerParams(vmem_limit_bytes=need + need // 4 + 4 * 2**20),
        cost_estimate=pl.CostEstimate(flops=flops, bytes_accessed=moved, transcendentals=exps),
    )(*scalars, *arrays, *wait)


def after(value, *wait):
    return pl.pallas_call(
        lambda *refs: None,
        in_specs=[ANY] * (1 + len(wait)),
        out_specs=ANY,
        out_shape=jax.ShapeDtypeStruct(value.shape, value.dtype),
        input_output_aliases={0: 0},
        compiler_params=pltpu.CompilerParams(vmem_limit_bytes=2**20),
    )(value, *wait)


def dot(a, b, contract=((1,), (0,))):
    return lax.dot_general(a, b, (contract, ((), ())), preferred_element_type=F32)


def rows_at(start, size, step):
    return pl.ds(pl.multiple_of(start, step), size)


def plane_at(k):
    return lax.bitwise_xor(lax.axis_index("ctx") // 2, k)


def inverse_rms(values):
    return lax.rsqrt(jnp.mean(values * values, axis=-1, keepdims=True) + EPSILON)


def norm_backward(values, factor, upstream):
    return factor * upstream - values * (factor * factor * factor) * jnp.mean(
        upstream * values, axis=-1, keepdims=True
    )


def head_rows(p, c):
    return slice((p * NQ + c) * SPAN, (p * NQ + c + 1) * SPAN)


def prepare_kernel(ids, spans, x_ref, up_ref, xt_ref, up_out, ids_out, spans_out):
    for p in range(2):
        for h in range(NQ):
            up_out[head_rows(p, h), :] = up_ref[p * SPAN : (p + 1) * SPAN, h * HD : (h + 1) * HD]
    for b in range(x_ref.shape[1] // BLK):
        xt_ref[b * BLK : (b + 1) * BLK, :] = x_ref[:, b * BLK : (b + 1) * BLK].T
    for source, out in ((ids, ids_out), (spans, spans_out)):

        @pl.loop(0, source.shape[1])
        def _(j):
            for i in range(source.shape[0]):
                out[i, j] = source[i, j]


def part_kernel(w_ref, out):
    rows = out.shape[0]
    out[...] = w_ref[rows_at(lax.axis_index("dp") * rows, rows, 16), :]


def first_step(nz):
    step = plane_at(nz - 1)
    return jnp.where(step == 0, nz - 1, step)


def first_kernel(*refs):
    pieces, out = refs[:-1], refs[-1]
    for k, ref in enumerate(pieces):

        @pl.when(first_step(len(pieces) + 1) == k + 1)
        def _():
            out[...] = ref[...]


def others_kernel(*refs):
    pieces, out = refs[:-1], refs[-1]
    rows = pieces[0].shape[0]
    first = first_step(len(pieces) + 1)
    for k, ref in enumerate(pieces):
        for slot in (k - 1, k):
            if 0 <= slot < len(pieces) - 1:

                @pl.when(first < k + 1 if slot < k else first > k + 1)
                def _():
                    out[slot * rows : (slot + 1) * rows, :] = ref[...]


def stack_kernel(*refs):
    rows = refs[0].shape[0]
    for k, ref in enumerate(refs[:-1]):
        refs[-1][k * rows : (k + 1) * rows, :] = ref[...]


def join_shards(shards, base, w_ref):
    core = lax.axis_index("ctx") % 2
    shard = shards[0].shape[0]
    for n, ref in enumerate(shards):
        at = base + (core if n == 0 else 1 - core) * shard
        w_ref[rows_at(at, shard, 128), :] = ref[...]


def join_pieces(pieces, slot, shard, piece, base, w_ref):
    core, dp = lax.axis_index("ctx") % 2, lax.axis_index("dp")
    for n, ref in enumerate(pieces):
        at = base + (core if n % 2 == 0 else 1 - core) * shard + (dp ^ (n // 2)) * piece
        w_ref[rows_at(at, piece, 16), :] = ref[slot * piece : (slot + 1) * piece, :]


def column_of(c, ids, x_ref):
    return jnp.concatenate(
        [x_ref[:, rows_at(ids[r, c] * BLK, BLK, BLK)] for r in range(NBR)], axis=1
    )


def project_keys(ids, x_ref, w_ref, first, kv_ref, key_ref):
    wide = NBR * BLK
    for c in range(NQ, NCB):
        at = c * wide - first
        out = dot(column_of(c, ids, x_ref), w_ref[at : at + wide, :]).astype(BF16)
        if c == NQ:
            key = out.astype(F32)
            key_ref[...] = out
            kv_ref[:, :HD] = (key * inverse_rms(key)).astype(BF16)
        else:
            kv_ref[:, HD:] = out


def project_queries(ids, x_ref, w_ref, q_ref, qhat_ref):
    wide = NBR * BLK
    for c in range(NQ):
        out = dot(column_of(c, ids, x_ref), w_ref[c * wide : (c + 1) * wide, :]).astype(BF16)
        query = out.astype(F32)
        normed = (query * inverse_rms(query)).astype(BF16)
        for p in range(2):
            q_ref[head_rows(p, c), :] = out[p * SPAN : (p + 1) * SPAN, :]
            qhat_ref[head_rows(p, c), :] = normed[p * SPAN : (p + 1) * SPAN, :]


def keys_kernel(nz, ids, x_ref, *refs):
    shards, pieces, (w_ref, kv_ref, key_ref) = refs[:2], refs[2:-3], refs[-3:]
    shard, piece = shards[0].shape[0], pieces[0].shape[0]
    last = lax.axis_index("ctx") // 2 == nz - 1
    pl.when(last)(lambda: join_shards(shards, 0, w_ref))
    pl.when(jnp.logical_not(last))(lambda: join_pieces(pieces, 0, shard, piece, 0, w_ref))
    project_keys(ids, x_ref, w_ref, NNZ * BLK - w_ref.shape[0], kv_ref, key_ref)


def queries_kernel(nz, ids, x_ref, last_ref, *refs):
    shards, firsts, others, (w_ref, q_ref, qhat_ref) = refs[:2], refs[2:-5], refs[-5:-3], refs[-3:]
    shard, piece = shards[0].shape[0], firsts[0].shape[0]
    zi, core = lax.axis_index("ctx") // 2, lax.axis_index("ctx") % 2
    last = zi == nz - 1
    pl.when(last)(lambda: join_pieces(firsts, 0, shard, piece, 0, w_ref))
    pl.when(jnp.logical_not(last))(lambda: join_shards(shards, zi * 2 * shard, w_ref))
    for slot in range(nz - 2):
        step = slot + 1 + (slot + 1 >= first_step(nz)).astype(jnp.int32)
        base = plane_at(step) * 2 * shard
        for k in range(len(firsts) // 2):
            for n, ref in enumerate(others):
                at = base + (core if n == 0 else 1 - core) * shard
                at += lax.bitwise_xor(lax.axis_index("dp"), k) * piece
                row = (k * (nz - 2) + slot) * piece
                w_ref[rows_at(at, piece, 16), :] = ref[row : row + piece, :]
    w_ref[NNZ * BLK - last_ref.shape[0] :, :] = last_ref[...]
    project_queries(ids, x_ref, w_ref, q_ref, qhat_ref)


def project_kernel(ids, x_ref, w_ref, q_ref, qhat_ref, kv_ref, key_ref):
    project_keys(ids, x_ref, w_ref, 0, kv_ref, key_ref)
    project_queries(ids, x_ref, w_ref, q_ref, qhat_ref)


def attend_kernel(nz, keys, spans, q_ref, qhat, up, *refs):
    pieces = refs[: 2 * nz]
    dq_ref = refs[2 * nz]
    keep = refs[2 * nz + 1 : 3 * nz + 1]
    send = refs[3 * nz + 1 : 4 * nz + 1]
    kv, expo, dprob, acc, dq_t, sums = refs[4 * nz + 1 :]
    half = NQ * SPAN
    me = lax.axis_index("ctx")
    zi, core = me // 2, me % 2
    for k in range(nz):
        z_from = plane_at(k)
        for other in range(2):
            source = z_from * 2 + (core if other == 0 else 1 - core)
            for p in range(2):
                kv[rows_at(spans[p, source] * SPAN, SPAN, SPAN), :] = pieces[2 * k + other][
                    p * SPAN : (p + 1) * SPAN, :
                ]
    length = kv.shape[0]
    key_row = lax.broadcasted_iota(jnp.int32, (keys, half), 0)
    query_at = lax.broadcasted_iota(jnp.int32, (keys, half), 1) % SPAN
    def when_seen(p, at, body):
        if at <= p * (length // 2):
            body()
        else:
            pl.when(at < (spans[p, me] + 1) * SPAN)(body)

    sums[...] = jnp.zeros_like(sums)
    acc[length // 2 + keys :, :] = jnp.zeros((length // 2 - keys, 2 * HD), F32)
    for p in (1, 0):
        base = 0 if p == 1 else length
        limit = query_at + spans[p, me] * SPAN
        for at in range(0, length // 2 * (p + 1), keys):

            def forward():
                q_part = qhat[p * half : (p + 1) * half, :]
                up_part = up[p * half : (p + 1) * half, :]
                rows, held = slice(at, at + keys), slice(base + at, base + at + keys)
                e = jnp.exp2(dot(kv[rows, :HD], q_part, ((1,), (1,))) * (SCALE * LOG2E))
                if at + keys > p * (length // 2):
                    e = jnp.where(key_row + at <= limit, e, 0.0)
                dp = dot(kv[rows, HD:], up_part, ((1,), (1,)))
                expo[held, :] = e
                dprob[held, :] = dp
                term = e.astype(BF16).astype(F32) * dp
                sums[2 * p] += jnp.sum(e.reshape(keys // 8, 8, half), axis=0)
                sums[2 * p + 1] += jnp.sum(term.reshape(keys // 8, 8, half), axis=0)

            when_seen(p, at, forward)
    for p in (1, 0):
        base = 0 if p == 1 else length
        inverse = 1.0 / jnp.sum(sums[2 * p], axis=0, keepdims=True)
        delta = jnp.sum(sums[2 * p + 1], axis=0, keepdims=True) * inverse
        for at in range(0, length // 2 * (p + 1), keys):

            def backward():
                q_part = qhat[p * half : (p + 1) * half, :]
                up_part = up[p * half : (p + 1) * half, :]
                rows, held = slice(at, at + keys), slice(base + at, base + at + keys)
                prob = expo[held, :] * inverse
                dscore = (prob * (dprob[held, :] - delta) * SCALE).astype(BF16)
                dkey, dvalue = dot(dscore, q_part), dot(prob.astype(BF16), up_part)
                dq_term = dot(kv[rows, :HD].T, dscore)
                if p == 1 and at <= length // 2:
                    acc[rows, :HD] = dkey
                    acc[rows, HD:] = dvalue
                else:
                    acc[rows, :HD] += dkey
                    acc[rows, HD:] += dvalue
                if at == 0:
                    dq_t[...] = dq_term
                else:
                    dq_t[...] += dq_term

            when_seen(p, at, backward)
        q_rows = q_ref[p * half : (p + 1) * half, :].astype(F32)
        dq = norm_backward(q_rows, inverse_rms(q_rows), dq_t[...].T).astype(BF16)
        for h in range(NQ):
            dq_ref[h, p * SPAN : (p + 1) * SPAN, :] = dq[h * SPAN : (h + 1) * SPAN, :]
    for k in range(nz):
        z_to = plane_at(k)
        for p in range(2):
            part = slice(p * SPAN, (p + 1) * SPAN)
            for out, owner in ((keep[k], z_to * 2 + core), (send[k], z_to * 2 + 1 - core)):
                rows = rows_at(spans[p, owner] * SPAN, SPAN, SPAN)
                out[part, :] = acc[rows, :].astype(BF16)


def kv_grad_kernel(nz, key_ref, *refs):
    terms, dkv_ref = refs[:nz], refs[nz]
    total = terms[0][...].astype(F32)
    for term in terms[1:]:
        total = total + term[...].astype(F32)
    key = key_ref[...].astype(F32)
    dkv_ref[0, :, :] = norm_backward(key, inverse_rms(key), total[:, :HD]).astype(BF16)
    dkv_ref[1, :, :] = total[:, HD:].astype(BF16)


def terms_kernel(z_first, z_count, shard, piece, ids, xt, xt_other, *refs):
    tok = xt.shape[1]
    grads, work = refs[-2:]
    columns = grads.shape[0]
    first = z_first * 2 * shard // (NBR * BLK)
    ndp = shard // piece
    sources, outs = refs[: -2 - ndp], refs[-2 - ndp : -2]
    for n, ref in enumerate(sources):
        other = n % 2
        for i in range(ref.shape[0]):
            c = i - first if n < 2 else NQ + i - first
            if 0 <= c < columns:
                grads[c, other * tok : (other + 1) * tok, :] = ref[i]
    core, dp = lax.axis_index("ctx") % 2, lax.axis_index("dp")
    count = shard // BLK
    for z in range(z_count):
        for i in range(count):
            b = (2 * (z_first + z) + core) * count + i
            c = b // NBR
            rows = rows_at(ids[b % NBR, c] * BLK, BLK, BLK)
            picked = jnp.concatenate([xt[rows, :], xt_other[rows, :]], axis=1)
            at = (z * count + i) * BLK
            work[at : at + BLK, :] = dot(picked, grads[c - first]).astype(BF16)
    for k in range(ndp):
        for z in range(z_count):
            at = z * shard + lax.bitwise_xor(dp, k) * piece
            outs[k][z * piece : (z + 1) * piece, :] = work[rows_at(at, piece, 16), :]


def all_terms_kernel(ids, xt, dq_ref, dkv_ref, out_ref):
    for c in range(NCB):
        picked = jnp.concatenate(
            [xt[rows_at(ids[r, c] * BLK, BLK, BLK), :] for r in range(NBR)], axis=0
        )
        grad = dq_ref[c] if c < NQ else dkv_ref[c - NQ]
        out_ref[c * NBR * BLK : (c + 1) * NBR * BLK, :] = dot(picked, grad).astype(BF16)


def sum_kernel(ndp, nz, piece, *refs):
    head, tail = refs[:ndp], refs[ndp : 2 * ndp]
    outs, work = refs[2 * ndp : 2 * ndp + nz], refs[2 * ndp + nz]
    for group, first, count in ((head, 0, nz - 1), (tail, nz - 1, 1)):
        total = group[0][...].astype(F32)
        for term in group[1:]:
            total = total + term[...].astype(F32)
        work[first * piece : (first + count) * piece, :] = total.astype(BF16)
    for k in range(nz):
        at = plane_at(k) * piece
        outs[k][...] = work[rows_at(at, piece, 16), :]


def place_kernel(piece, *refs):
    for k, ref in enumerate(refs[:-1]):
        at = lax.bitwise_xor(lax.axis_index("dp"), k) * piece
        refs[-1][rows_at(at, piece, 16), :] = ref[...].astype(F32)


def token_grad_kernel(ids, dq_ref, dkv_ref, w_ref, out_ref, done_ref, work):
    done_ref[...] = jnp.zeros_like(done_ref)
    wide = NBR * BLK
    cover = out_ref.shape[1] // wide
    for c in range(NCB):
        grad = dq_ref[c] if c < NQ else dkv_ref[c - NQ]
        spread = dot(grad, w_ref[c * wide : (c + 1) * wide, :], ((1,), (1,)))
        for r in range(NBR):
            columns = rows_at(ids[r, c] * BLK, BLK, BLK)
            term = spread[:, r * BLK : (r + 1) * BLK]
            if c < cover:
                work[:, columns] = term
            else:
                work[:, columns] += term
    out_ref[...] = work[...].astype(BF16)


def per_device(ndp, tokens, grad_attn, w_packed, block_rows, span_pairs):
    ids, spans = block_rows.T, span_pairs.T
    nctx = lax.axis_size("ctx")
    nz = nctx // 2
    x = tokens[0]
    tok, width = x.shape
    length = spans.shape[1] * 2 * SPAN
    shard = w_packed.shape[0]
    piece = shard // ndp
    cut = (nz - 1) * 2 * shard
    half = NQ * SPAN
    fast = 2 < nz and cut <= NQ * NBR * BLK and shard % BLK == 0
    fast = fast and shard % (16 * ndp) == 0 and 1 < ndp and ndp & (ndp - 1) == 0

    def swap_core(v):
        return lax.ppermute(v, "ctx", [(i, i ^ 1) for i in range(nctx)])

    def both_cores(parts):
        return [v for part in parts for v in (part, swap_core(part))]

    def swap_z(v, k):
        return lax.ppermute(v, "ctx", [(i, i ^ (2 * k)) for i in range(nctx)])

    def swap_dp(v, k):
        return lax.ppermute(v, "dp", [(i, i ^ k) for i in range(ndp)])

    def add(a, b):
        return (a.astype(F32) + b.astype(F32)).astype(BF16)

    xt, up, ids, spans = call(
        prepare_kernel,
        (ids, spans),
        (x, grad_attn[0]),
        [
            ((width, tok), BF16),
            ((tok * NQ, HD), BF16),
            (ids.shape, jnp.int32),
            (spans.shape, jnp.int32),
        ],
        moved=4 * x.size,
    )

    if fast:
        (mine,) = call(part_kernel, (), (w_packed,), [((piece, BLK), BF16)], moved=4 * piece * BLK)
        from_z = [swap_z(mine, k) for k in range(1, nz)]

        def pick(kernel, count, wait):
            return call(
                kernel,
                (),
                from_z,
                [((count * piece, BLK), BF16)],
                wait=wait,
                moved=4 * nz * piece * BLK,
            )[0]

        def to_all_dp(held):
            return [held] + [swap_dp(held, k) for k in range(1, ndp)]

        shards = both_cores([w_packed])
        first = pick(first_kernel, 1, (ids, shards[1]))
        firsts = to_all_dp(first)
        others = to_all_dp(pick(others_kernel, nz - 2, (first,)))
        firsts = both_cores(firsts)
        w_last, kv, key = call(
            functools.partial(keys_kernel, nz),
            (ids,),
            (x, *shards, *firsts),
            [((2 * shard, BLK), BF16), ((tok, 2 * HD), BF16), ((tok, HD), BF16)],
            flops=2 * tok * (NCB - NQ) * NBR * BLK * BLK,
            moved=3 * 2**20,
        )
        kv_from_z = [swap_z(kv, k) for k in range(1, nz)]
        kv_pieces = both_cores([kv] + kv_from_z)
        (stacked,) = call(
            stack_kernel,
            (),
            others,
            [((ndp * (nz - 2) * piece, BLK), BF16)],
            wait=kv_from_z,
            moved=4 * nz * shard * BLK,
        )
        weights, query, qhat = call(
            functools.partial(queries_kernel, nz),
            (ids,),
            (x, w_last, *shards, *firsts, stacked, swap_core(stacked)),
            [((NNZ * BLK, BLK), BF16)] + [((tok * NQ, HD), BF16)] * 2,
            wait=kv_pieces,
            flops=2 * tok * NQ * NBR * BLK * BLK,
            moved=8 * 2**20,
        )
        xt_other = swap_core(after(xt, qhat))
    else:
        weights = lax.all_gather(w_packed, "ctx", axis=0, tiled=True)
        query, qhat, kv, key = call(
            project_kernel,
            (ids,),
            (x, weights),
            [((tok * NQ, HD), BF16)] * 2 + [((tok, 2 * HD), BF16), ((tok, HD), BF16)],
            flops=2 * tok * NNZ * BLK * BLK,
            moved=4 * 2**20,
        )

        kv_pieces = both_cores([kv] + [swap_z(kv, k) for k in range(1, nz)])

    outs = call(
        functools.partial(attend_kernel, nz, math.gcd(256, length // 2)),
        (spans,),
        (query, qhat, up, *kv_pieces),
        [((NQ, tok, HD), BF16)] + [((tok, 2 * HD), BF16)] * (2 * nz),
        scratch=[
            pltpu.VMEM((length, 2 * HD), BF16),
            pltpu.VMEM((length + length // 2, half), F32),
            pltpu.VMEM((length + length // 2, half), F32),
            pltpu.VMEM((length, 2 * HD), F32),
            pltpu.VMEM((HD, half), F32),
            pltpu.VMEM((4, 8, half), F32),
        ],
        flops=10 * tok * NQ * length * HD // 2,
        moved=4 * 2**20,
        exps=tok * NQ * length // 2,
    )
    dq, keep, send = outs[0], outs[1 : nz + 1], outs[nz + 1 :]
    sums = [add(keep[k], swap_core(send[k])) for k in range(nz)]

    def weight_terms(z_lo, z_count, grads):
        first = z_lo * 2 * shard // (NBR * BLK)
        last = ((z_lo + z_count) * 2 * shard - 1) // (NBR * BLK)
        return call(
            functools.partial(terms_kernel, z_lo, z_count, shard, piece),
            (ids,),
            (xt, xt_other, *grads),
            [((z_count * piece, BLK), BF16)] * ndp,
            scratch=[
                pltpu.VMEM((last - first + 1, 2 * tok, HD), BF16),
                pltpu.VMEM((z_count * shard, BLK), BF16),
            ],
            flops=4 * tok * z_count * shard * BLK,
            moved=4 * 2**20,
        )

    if fast:
        dq_pair = (dq, swap_core(dq))
        head_raw = weight_terms(0, nz - 1, dq_pair)
        head = [head_raw[0]] + [swap_dp(head_raw[k], k) for k in range(1, ndp)]
    gate = head_raw[:1] if fast else []
    kv_terms = [sums[0], swap_z(after(sums[1], *gate), 1)]
    kv_terms += [swap_z(sums[k], k) for k in range(2, nz)]
    (dkv,) = call(
        functools.partial(kv_grad_kernel, nz),
        (),
        (key, *kv_terms),
        [((2, tok, HD), BF16)],
        moved=2**19,
    )
    grad_tokens, done = call(
        token_grad_kernel,
        (ids,),
        (dq, dkv, weights),
        [((tok, width), BF16), ((8, BLK), F32)],
        scratch=[pltpu.VMEM((tok, width), F32)],
        flops=2 * tok * NNZ * BLK * BLK,
        moved=4 * 2**20,
    )
    if fast:
        tail = weight_terms(nz - 1, 1, (*dq_pair, dkv, swap_core(dkv)))
        tail = [tail[0]] + [
            swap_dp(after(tail[k], head[1]) if k == ndp - 1 else tail[k], k) for k in range(1, ndp)
        ]
        by_z = call(
            functools.partial(sum_kernel, ndp, nz, piece),
            (),
            (*head, *tail),
            [((piece, BLK), BF16)] * nz,
            scratch=[pltpu.VMEM((nz * piece, BLK), BF16)],
            wait=(done,),
            moved=2 * 2**20,
        )
        owned = by_z[0].astype(F32)
        for k in range(1, nz):
            owned = owned + swap_z(by_z[k], k).astype(F32)
        owned = owned.astype(BF16)
        (grad_weights,) = call(
            functools.partial(place_kernel, piece),
            (),
            [owned] + [swap_dp(owned, k) for k in range(1, ndp)],
            [((shard, BLK), F32)],
            moved=2**20,
        )
    else:
        (partial_w,) = call(
            all_terms_kernel,
            (ids,),
            (xt, dq, dkv),
            [((NNZ * BLK, BLK), BF16)],
            flops=2 * tok * NNZ * BLK * BLK,
            moved=4 * 2**20,
        )
        received = lax.all_to_all(
            partial_w.reshape(nctx, shard, BLK), "ctx", split_axis=0, concat_axis=0, tiled=True
        )
        grad_weights = lax.psum(jnp.sum(received.astype(F32), axis=0), "dp")

    return (grad_tokens[None], grad_weights)


def solution(mesh):
    in_specs = (P("dp", "ctx", None), P("dp", "ctx", None), P("ctx", None), P(), P())
    out_specs = (P("dp", "ctx", None), P("ctx", None))
    return jax.shard_map(
        functools.partial(per_device, mesh.shape["dp"]),
        mesh=mesh,
        in_specs=in_specs,
        out_specs=out_specs,
        check_vma=False,
    )
```

```python
import functools
import math

import jax
import jax.numpy as jnp
from jax import lax
from jax.experimental import pallas as pl
from jax.experimental.pallas import tpu as pltpu
from jax.sharding import PartitionSpec as P

HD = 128
BLK = 128
QPG = 8
GROUPS = 1
SPAN = 64
NBR = 8
NCB = 10
NNZ = 80
NQ = GROUPS * QPG
EPSILON = 1e-06
SCALE = 1.0 / math.sqrt(HD)
LOG2E = math.log2(math.e)

F32 = jnp.float32
BF16 = jnp.bfloat16
VMEM = pl.BlockSpec(memory_space=pltpu.VMEM)
SMEM = pl.BlockSpec(memory_space=pltpu.SMEM)
ANY = pl.BlockSpec(memory_space=pl.ANY)


def nbytes(shape, dtype):
    return math.prod(shape) * jnp.dtype(dtype).itemsize


def call(kernel, scalars, arrays, outs, scratch=(), wait=(), flops=0, moved=0, exps=0):
    def body(*refs):
        at = len(scalars) + len(arrays)
        kernel(*refs[:at], *refs[at + len(wait) :])

    held = [(v.shape, v.dtype) for v in arrays] + [(s, t) for s, t in outs]
    held += [(v.shape, v.dtype) for v in scratch]
    need = sum(nbytes(s, t) for s, t in held)
    return pl.pallas_call(
        body,
        in_specs=[SMEM] * len(scalars) + [VMEM] * len(arrays) + [ANY] * len(wait),
        out_specs=[SMEM if t == jnp.int32 else VMEM for _, t in outs],
        out_shape=[jax.ShapeDtypeStruct(s, t) for s, t in outs],
        scratch_shapes=list(scratch),
        compiler_params=pltpu.CompilerParams(vmem_limit_bytes=need + need // 4 + 4 * 2**20),
        cost_estimate=pl.CostEstimate(flops=flops, bytes_accessed=moved, transcendentals=exps),
    )(*scalars, *arrays, *wait)


def after(value, *wait):
    return pl.pallas_call(
        lambda *refs: None,
        in_specs=[ANY] * (1 + len(wait)),
        out_specs=ANY,
        out_shape=jax.ShapeDtypeStruct(value.shape, value.dtype),
        input_output_aliases={0: 0},
        compiler_params=pltpu.CompilerParams(vmem_limit_bytes=2**20),
    )(value, *wait)


def dot(a, b, contract=((1,), (0,))):
    return lax.dot_general(a, b, (contract, ((), ())), preferred_element_type=F32)


def rows_at(start, size, step):
    return pl.ds(pl.multiple_of(start, step), size)


def plane_at(k):
    return lax.bitwise_xor(lax.axis_index("ctx") // 2, k)


def inverse_rms(values):
    return lax.rsqrt(jnp.mean(values * values, axis=-1, keepdims=True) + EPSILON)


def norm_backward(values, factor, upstream):
    return factor * upstream - values * (factor * factor * factor) * jnp.mean(
        upstream * values, axis=-1, keepdims=True
    )


def head_rows(p, c):
    return slice((p * NQ + c) * SPAN, (p * NQ + c + 1) * SPAN)


def prepare_kernel(ids, spans, x_ref, up_ref, xt_ref, up_out, ids_out, spans_out):
    for p in range(2):
        for h in range(NQ):
            up_out[head_rows(p, h), :] = up_ref[p * SPAN : (p + 1) * SPAN, h * HD : (h + 1) * HD]
    for b in range(x_ref.shape[1] // BLK):
        xt_ref[b * BLK : (b + 1) * BLK, :] = x_ref[:, b * BLK : (b + 1) * BLK].T
    for source, out in ((ids, ids_out), (spans, spans_out)):

        @pl.loop(0, source.shape[1])
        def _(j):
            for i in range(source.shape[0]):
                out[i, j] = source[i, j]


def part_kernel(w_ref, out):
    rows = out.shape[0]
    out[...] = w_ref[rows_at(lax.axis_index("dp") * rows, rows, 16), :]


def first_step(nz):
    step = plane_at(nz - 1)
    return jnp.where(step == 0, nz - 1, step)


def first_kernel(*refs):
    pieces, out = refs[:-1], refs[-1]
    for k, ref in enumerate(pieces):

        @pl.when(first_step(len(pieces) + 1) == k + 1)
        def _():
            out[...] = ref[...]


def others_kernel(*refs):
    pieces, out = refs[:-1], refs[-1]
    rows = pieces[0].shape[0]
    first = first_step(len(pieces) + 1)
    for k, ref in enumerate(pieces):
        for slot in (k - 1, k):
            if 0 <= slot < len(pieces) - 1:

                @pl.when(first < k + 1 if slot < k else first > k + 1)
                def _():
                    out[slot * rows : (slot + 1) * rows, :] = ref[...]


def stack_kernel(*refs):
    rows = refs[0].shape[0]
    for k, ref in enumerate(refs[:-1]):
        refs[-1][k * rows : (k + 1) * rows, :] = ref[...]


def join_shards(shards, base, w_ref):
    core = lax.axis_index("ctx") % 2
    shard = shards[0].shape[0]
    for n, ref in enumerate(shards):
        at = base + (core if n == 0 else 1 - core) * shard
        w_ref[rows_at(at, shard, 128), :] = ref[...]


def join_pieces(pieces, slot, shard, piece, base, w_ref):
    core, dp = lax.axis_index("ctx") % 2, lax.axis_index("dp")
    for n, ref in enumerate(pieces):
        at = base + (core if n % 2 == 0 else 1 - core) * shard + (dp ^ (n // 2)) * piece
        w_ref[rows_at(at, piece, 16), :] = ref[slot * piece : (slot + 1) * piece, :]


def column_of(c, ids, x_ref):
    return jnp.concatenate(
        [x_ref[:, rows_at(ids[r, c] * BLK, BLK, BLK)] for r in range(NBR)], axis=1
    )


def project_keys(ids, x_ref, w_ref, first, kv_ref, key_ref):
    wide = NBR * BLK
    for c in range(NQ, NCB):
        at = c * wide - first
        out = dot(column_of(c, ids, x_ref), w_ref[at : at + wide, :]).astype(BF16)
        if c == NQ:
            key = out.astype(F32)
            key_ref[...] = out
            kv_ref[:, :HD] = (key * inverse_rms(key)).astype(BF16)
        else:
            kv_ref[:, HD:] = out


def project_queries(ids, x_ref, w_ref, q_ref, qhat_ref):
    wide = NBR * BLK
    for c in range(NQ):
        out = dot(column_of(c, ids, x_ref), w_ref[c * wide : (c + 1) * wide, :]).astype(BF16)
        query = out.astype(F32)
        normed = (query * inverse_rms(query)).astype(BF16)
        for p in range(2):
            q_ref[head_rows(p, c), :] = out[p * SPAN : (p + 1) * SPAN, :]
            qhat_ref[head_rows(p, c), :] = normed[p * SPAN : (p + 1) * SPAN, :]


def keys_kernel(nz, ids, x_ref, *refs):
    shards, pieces, (w_ref, kv_ref, key_ref) = refs[:2], refs[2:-3], refs[-3:]
    shard, piece = shards[0].shape[0], pieces[0].shape[0]
    last = lax.axis_index("ctx") // 2 == nz - 1
    pl.when(last)(lambda: join_shards(shards, 0, w_ref))
    pl.when(jnp.logical_not(last))(lambda: join_pieces(pieces, 0, shard, piece, 0, w_ref))
    project_keys(ids, x_ref, w_ref, NNZ * BLK - w_ref.shape[0], kv_ref, key_ref)


def queries_kernel(nz, ids, x_ref, last_ref, *refs):
    shards, firsts, others, (w_ref, q_ref, qhat_ref) = refs[:2], refs[2:-5], refs[-5:-3], refs[-3:]
    shard, piece = shards[0].shape[0], firsts[0].shape[0]
    zi, core = lax.axis_index("ctx") // 2, lax.axis_index("ctx") % 2
    last = zi == nz - 1
    pl.when(last)(lambda: join_pieces(firsts, 0, shard, piece, 0, w_ref))
    pl.when(jnp.logical_not(last))(lambda: join_shards(shards, zi * 2 * shard, w_ref))
    for slot in range(nz - 2):
        step = slot + 1 + (slot + 1 >= first_step(nz)).astype(jnp.int32)
        base = plane_at(step) * 2 * shard
        for k in range(len(firsts) // 2):
            for n, ref in enumerate(others):
                at = base + (core if n == 0 else 1 - core) * shard
                at += lax.bitwise_xor(lax.axis_index("dp"), k) * piece
                row = (k * (nz - 2) + slot) * piece
                w_ref[rows_at(at, piece, 16), :] = ref[row : row + piece, :]
    w_ref[NNZ * BLK - last_ref.shape[0] :, :] = last_ref[...]
    project_queries(ids, x_ref, w_ref, q_ref, qhat_ref)


def project_kernel(ids, x_ref, w_ref, q_ref, qhat_ref, kv_ref, key_ref):
    project_keys(ids, x_ref, w_ref, 0, kv_ref, key_ref)
    project_queries(ids, x_ref, w_ref, q_ref, qhat_ref)


def attend_kernel(nz, keys, spans, q_ref, qhat, up, *refs):
    pieces = refs[: 2 * nz]
    dq_ref = refs[2 * nz]
    keep = refs[2 * nz + 1 : 3 * nz + 1]
    send = refs[3 * nz + 1 : 4 * nz + 1]
    kv, expo, dprob, acc, dq_t = refs[4 * nz + 1 :]
    half = NQ * SPAN
    me = lax.axis_index("ctx")
    zi, core = me // 2, me % 2
    for k in range(nz):
        z_from = plane_at(k)
        for other in range(2):
            source = z_from * 2 + (core if other == 0 else 1 - core)
            for p in range(2):
                kv[rows_at(spans[p, source] * SPAN, SPAN, SPAN), :] = pieces[2 * k + other][
                    p * SPAN : (p + 1) * SPAN, :
                ]
    length = kv.shape[0]
    key_row = lax.broadcasted_iota(jnp.int32, (keys, half), 0)
    query_at = lax.broadcasted_iota(jnp.int32, (keys, half), 1) % SPAN
    found = {}
    for p in (1, 0):
        reach = length if p == 1 else length // 2
        base = 0 if p == 1 else length
        sure = length // 2 if p == 1 else 0
        q_part = qhat[p * half : (p + 1) * half, :]
        up_part = up[p * half : (p + 1) * half, :]
        limit = query_at + spans[p, me] * SPAN
        total = jnp.zeros((8, half), F32)
        weighted = jnp.zeros((8, half), F32)
        for at in range(0, reach, keys):
            rows = slice(at, at + keys)
            e = jnp.exp2(dot(kv[rows, :HD], q_part, ((1,), (1,))) * (SCALE * LOG2E))
            if at + keys > sure:
                e = jnp.where(key_row + at <= limit, e, 0.0)
            dp = dot(kv[rows, HD:], up_part, ((1,), (1,)))
            expo[base + at : base + at + keys, :] = e
            dprob[base + at : base + at + keys, :] = dp
            term = e.astype(BF16).astype(F32) * dp
            total = total + jnp.sum(e.reshape(keys // 8, 8, half), axis=0)
            weighted = weighted + jnp.sum(term.reshape(keys // 8, 8, half), axis=0)
        inverse = 1.0 / jnp.sum(total, axis=0, keepdims=True)
        found[p] = (inverse, jnp.sum(weighted, axis=0, keepdims=True) * inverse)
    for p in (1, 0):
        reach = length if p == 1 else length // 2
        base = 0 if p == 1 else length
        q_part = qhat[p * half : (p + 1) * half, :]
        up_part = up[p * half : (p + 1) * half, :]
        inverse, delta = found[p]
        for at in range(0, reach, keys):
            rows = slice(at, at + keys)
            held = slice(base + at, base + at + keys)
            prob = expo[held, :] * inverse
            dscore = (prob * (dprob[held, :] - delta) * SCALE).astype(BF16)
            dkey, dvalue = dot(dscore, q_part), dot(prob.astype(BF16), up_part)
            dq_term = dot(kv[rows, :HD].T, dscore)
            if p == 1:
                acc[rows, :HD] = dkey
                acc[rows, HD:] = dvalue
            else:
                acc[rows, :HD] += dkey
                acc[rows, HD:] += dvalue
            if at == 0:
                dq_t[...] = dq_term
            else:
                dq_t[...] += dq_term
        q_rows = q_ref[p * half : (p + 1) * half, :].astype(F32)
        dq = norm_backward(q_rows, inverse_rms(q_rows), dq_t[...].T).astype(BF16)
        for h in range(NQ):
            dq_ref[h, p * SPAN : (p + 1) * SPAN, :] = dq[h * SPAN : (h + 1) * SPAN, :]
    for k in range(nz):
        z_to = plane_at(k)
        for p in range(2):
            part = slice(p * SPAN, (p + 1) * SPAN)
            for out, owner in ((keep[k], z_to * 2 + core), (send[k], z_to * 2 + 1 - core)):
                rows = rows_at(spans[p, owner] * SPAN, SPAN, SPAN)
                out[part, :] = acc[rows, :].astype(BF16)


def kv_grad_kernel(nz, key_ref, *refs):
    terms, dkv_ref = refs[:nz], refs[nz]
    total = terms[0][...].astype(F32)
    for term in terms[1:]:
        total = total + term[...].astype(F32)
    key = key_ref[...].astype(F32)
    dkv_ref[0, :, :] = norm_backward(key, inverse_rms(key), total[:, :HD]).astype(BF16)
    dkv_ref[1, :, :] = total[:, HD:].astype(BF16)


def terms_kernel(z_first, z_count, shard, piece, ids, xt, xt_other, *refs):
    tok = xt.shape[1]
    grads, work = refs[-2:]
    columns = grads.shape[0]
    first = z_first * 2 * shard // (NBR * BLK)
    ndp = shard // piece
    sources, outs = refs[: -2 - ndp], refs[-2 - ndp : -2]
    for n, ref in enumerate(sources):
        other = n % 2
        for i in range(ref.shape[0]):
            c = i - first if n < 2 else NQ + i - first
            if 0 <= c < columns:
                grads[c, other * tok : (other + 1) * tok, :] = ref[i]
    core, dp = lax.axis_index("ctx") % 2, lax.axis_index("dp")
    count = shard // BLK
    for z in range(z_count):
        for i in range(count):
            b = (2 * (z_first + z) + core) * count + i
            c = b // NBR
            rows = rows_at(ids[b % NBR, c] * BLK, BLK, BLK)
            picked = jnp.concatenate([xt[rows, :], xt_other[rows, :]], axis=1)
            at = (z * count + i) * BLK
            work[at : at + BLK, :] = dot(picked, grads[c - first]).astype(BF16)
    for k in range(ndp):
        for z in range(z_count):
            at = z * shard + lax.bitwise_xor(dp, k) * piece
            outs[k][z * piece : (z + 1) * piece, :] = work[rows_at(at, piece, 16), :]


def all_terms_kernel(ids, xt, dq_ref, dkv_ref, out_ref):
    for c in range(NCB):
        picked = jnp.concatenate(
            [xt[rows_at(ids[r, c] * BLK, BLK, BLK), :] for r in range(NBR)], axis=0
        )
        grad = dq_ref[c] if c < NQ else dkv_ref[c - NQ]
        out_ref[c * NBR * BLK : (c + 1) * NBR * BLK, :] = dot(picked, grad).astype(BF16)


def sum_kernel(ndp, nz, piece, *refs):
    head, tail = refs[:ndp], refs[ndp : 2 * ndp]
    outs, work = refs[2 * ndp : 2 * ndp + nz], refs[2 * ndp + nz]
    for group, first, count in ((head, 0, nz - 1), (tail, nz - 1, 1)):
        total = group[0][...].astype(F32)
        for term in group[1:]:
            total = total + term[...].astype(F32)
        work[first * piece : (first + count) * piece, :] = total.astype(BF16)
    for k in range(nz):
        at = plane_at(k) * piece
        outs[k][...] = work[rows_at(at, piece, 16), :]


def place_kernel(piece, *refs):
    for k, ref in enumerate(refs[:-1]):
        at = lax.bitwise_xor(lax.axis_index("dp"), k) * piece
        refs[-1][rows_at(at, piece, 16), :] = ref[...].astype(F32)


def token_grad_kernel(ids, dq_ref, dkv_ref, w_ref, out_ref, done_ref, work):
    done_ref[...] = jnp.zeros_like(done_ref)
    wide = NBR * BLK
    cover = out_ref.shape[1] // wide
    for c in range(NCB):
        grad = dq_ref[c] if c < NQ else dkv_ref[c - NQ]
        spread = dot(grad, w_ref[c * wide : (c + 1) * wide, :], ((1,), (1,)))
        for r in range(NBR):
            columns = rows_at(ids[r, c] * BLK, BLK, BLK)
            term = spread[:, r * BLK : (r + 1) * BLK]
            if c < cover:
                work[:, columns] = term
            else:
                work[:, columns] += term
    out_ref[...] = work[...].astype(BF16)


def per_device(ndp, tokens, grad_attn, w_packed, block_rows, span_pairs):
    ids, spans = block_rows.T, span_pairs.T
    nctx = lax.axis_size("ctx")
    nz = nctx // 2
    x = tokens[0]
    tok, width = x.shape
    length = spans.shape[1] * 2 * SPAN
    shard = w_packed.shape[0]
    piece = shard // ndp
    cut = (nz - 1) * 2 * shard
    half = NQ * SPAN
    fast = 2 < nz and cut <= NQ * NBR * BLK and shard % BLK == 0
    fast = fast and shard % (16 * ndp) == 0 and 1 < ndp and ndp & (ndp - 1) == 0

    def swap_core(v):
        return lax.ppermute(v, "ctx", [(i, i ^ 1) for i in range(nctx)])

    def both_cores(parts):
        return [v for part in parts for v in (part, swap_core(part))]

    def swap_z(v, k):
        return lax.ppermute(v, "ctx", [(i, i ^ (2 * k)) for i in range(nctx)])

    def swap_dp(v, k):
        return lax.ppermute(v, "dp", [(i, i ^ k) for i in range(ndp)])

    def add(a, b):
        return (a.astype(F32) + b.astype(F32)).astype(BF16)

    xt, up, ids, spans = call(
        prepare_kernel,
        (ids, spans),
        (x, grad_attn[0]),
        [
            ((width, tok), BF16),
            ((tok * NQ, HD), BF16),
            (ids.shape, jnp.int32),
            (spans.shape, jnp.int32),
        ],
        moved=4 * x.size,
    )

    if fast:
        (mine,) = call(part_kernel, (), (w_packed,), [((piece, BLK), BF16)], moved=4 * piece * BLK)
        from_z = [swap_z(mine, k) for k in range(1, nz)]

        def pick(kernel, count, wait):
            return call(
                kernel,
                (),
                from_z,
                [((count * piece, BLK), BF16)],
                wait=wait,
                moved=4 * nz * piece * BLK,
            )[0]

        def to_all_dp(held):
            return [held] + [swap_dp(held, k) for k in range(1, ndp)]

        shards = both_cores([w_packed])
        first = pick(first_kernel, 1, (ids, shards[1]))
        firsts = to_all_dp(first)
        others = to_all_dp(pick(others_kernel, nz - 2, (first,)))
        firsts = both_cores(firsts)
        w_last, kv, key = call(
            functools.partial(keys_kernel, nz),
            (ids,),
            (x, *shards, *firsts),
            [((2 * shard, BLK), BF16), ((tok, 2 * HD), BF16), ((tok, HD), BF16)],
            flops=2 * tok * (NCB - NQ) * NBR * BLK * BLK,
            moved=3 * 2**20,
        )
        kv_from_z = [swap_z(kv, k) for k in range(1, nz)]
        kv_pieces = both_cores([kv] + kv_from_z)
        (stacked,) = call(
            stack_kernel,
            (),
            others,
            [((ndp * (nz - 2) * piece, BLK), BF16)],
            wait=kv_from_z,
            moved=4 * nz * shard * BLK,
        )
        weights, query, qhat = call(
            functools.partial(queries_kernel, nz),
            (ids,),
            (x, w_last, *shards, *firsts, stacked, swap_core(stacked)),
            [((NNZ * BLK, BLK), BF16)] + [((tok * NQ, HD), BF16)] * 2,
            wait=kv_pieces,
            flops=2 * tok * NQ * NBR * BLK * BLK,
            moved=8 * 2**20,
        )
        xt_other = swap_core(after(xt, qhat))
    else:
        weights = lax.all_gather(w_packed, "ctx", axis=0, tiled=True)
        query, qhat, kv, key = call(
            project_kernel,
            (ids,),
            (x, weights),
            [((tok * NQ, HD), BF16)] * 2 + [((tok, 2 * HD), BF16), ((tok, HD), BF16)],
            flops=2 * tok * NNZ * BLK * BLK,
            moved=4 * 2**20,
        )

        kv_pieces = both_cores([kv] + [swap_z(kv, k) for k in range(1, nz)])

    outs = call(
        functools.partial(attend_kernel, nz, math.gcd(512, length // 2)),
        (spans,),
        (query, qhat, up, *kv_pieces),
        [((NQ, tok, HD), BF16)] + [((tok, 2 * HD), BF16)] * (2 * nz),
        scratch=[
            pltpu.VMEM((length, 2 * HD), BF16),
            pltpu.VMEM((length + length // 2, half), F32),
            pltpu.VMEM((length + length // 2, half), F32),
            pltpu.VMEM((length, 2 * HD), F32),
            pltpu.VMEM((HD, half), F32),
        ],
        flops=10 * tok * NQ * length * HD // 2,
        moved=4 * 2**20,
        exps=tok * NQ * length // 2,
    )
    dq, keep, send = outs[0], outs[1 : nz + 1], outs[nz + 1 :]
    sums = [add(keep[k], swap_core(send[k])) for k in range(nz)]

    def weight_terms(z_lo, z_count, grads):
        first = z_lo * 2 * shard // (NBR * BLK)
        last = ((z_lo + z_count) * 2 * shard - 1) // (NBR * BLK)
        return call(
            functools.partial(terms_kernel, z_lo, z_count, shard, piece),
            (ids,),
            (xt, xt_other, *grads),
            [((z_count * piece, BLK), BF16)] * ndp,
            scratch=[
                pltpu.VMEM((last - first + 1, 2 * tok, HD), BF16),
                pltpu.VMEM((z_count * shard, BLK), BF16),
            ],
            flops=4 * tok * z_count * shard * BLK,
            moved=4 * 2**20,
        )

    if fast:
        dq_pair = (dq, swap_core(dq))
        head_raw = weight_terms(0, nz - 1, dq_pair)
        head = [head_raw[0]] + [swap_dp(head_raw[k], k) for k in range(1, ndp)]
    gate = head_raw[:1] if fast else []
    kv_terms = [sums[0], swap_z(after(sums[1], *gate), 1)]
    kv_terms += [swap_z(sums[k], k) for k in range(2, nz)]
    (dkv,) = call(
        functools.partial(kv_grad_kernel, nz),
        (),
        (key, *kv_terms),
        [((2, tok, HD), BF16)],
        moved=2**19,
    )
    grad_tokens, done = call(
        token_grad_kernel,
        (ids,),
        (dq, dkv, weights),
        [((tok, width), BF16), ((8, BLK), F32)],
        scratch=[pltpu.VMEM((tok, width), F32)],
        flops=2 * tok * NNZ * BLK * BLK,
        moved=4 * 2**20,
    )
    if fast:
        tail = weight_terms(nz - 1, 1, (*dq_pair, dkv, swap_core(dkv)))
        tail = [tail[0]] + [
            swap_dp(after(tail[k], head[1]) if k == ndp - 1 else tail[k], k) for k in range(1, ndp)
        ]
        by_z = call(
            functools.partial(sum_kernel, ndp, nz, piece),
            (),
            (*head, *tail),
            [((piece, BLK), BF16)] * nz,
            scratch=[pltpu.VMEM((nz * piece, BLK), BF16)],
            wait=(done,),
            moved=2 * 2**20,
        )
        owned = by_z[0].astype(F32)
        for k in range(1, nz):
            owned = owned + swap_z(by_z[k], k).astype(F32)
        owned = owned.astype(BF16)
        (grad_weights,) = call(
            functools.partial(place_kernel, piece),
            (),
            [owned] + [swap_dp(owned, k) for k in range(1, ndp)],
            [((shard, BLK), F32)],
            moved=2**20,
        )
    else:
        (partial_w,) = call(
            all_terms_kernel,
            (ids,),
            (xt, dq, dkv),
            [((NNZ * BLK, BLK), BF16)],
            flops=2 * tok * NNZ * BLK * BLK,
            moved=4 * 2**20,
        )
        received = lax.all_to_all(
            partial_w.reshape(nctx, shard, BLK), "ctx", split_axis=0, concat_axis=0, tiled=True
        )
        grad_weights = lax.psum(jnp.sum(received.astype(F32), axis=0), "dp")

    return (grad_tokens[None], grad_weights)


def solution(mesh):
    in_specs = (P("dp", "ctx", None), P("dp", "ctx", None), P("ctx", None), P(), P())
    out_specs = (P("dp", "ctx", None), P("ctx", None))
    return jax.shard_map(
        functools.partial(per_device, mesh.shape["dp"]),
        mesh=mesh,
        in_specs=in_specs,
        out_specs=out_specs,
        check_vma=False,
    )
```
